32 devices in a mesh: batch: 2 (over x), blk: 16 (over z, y, core).
Axes of the slice: x: 2, y: 2, z: 4, core: 2. Of those that a mesh axis runs over, the one named last changes fastest.
Arguments:
- triplane: bfloat16 [4, 768, 1024], P('batch', 'blk'), may hold values from -6 to 6
- patches: bfloat16 [4, 256, 1024], P('batch', 'blk'), may hold values from -6 to 6
- cotangent: bfloat16 [4, 768, 1024], P('batch', 'blk'), may hold values from -6 to 6
- camera_index: int32 [4, 4], P('batch'), may hold values from 0 to 255
- triplane_count: int32 [4], P('batch'), may hold values from 744 to 768, as said below
- patch_count: int32 [4], P('batch'), may hold values from 128 to 256, as said below
- camera_table: bfloat16 [256, 1024], replicated, may hold values from -6 to 6
- mod_weight: bfloat16 [1024, 2048], replicated, may hold values from -0.1875 to 0.1875
- qkv_weight: bfloat16 [1024, 3072], replicated, may hold values from -0.1875 to 0.1875
- self_out: bfloat16 [1024, 1024], replicated, may hold values from -3 to 3
- gain_mid: float32 [1024], replicated, may hold values from 0.25 to 1.75
- bias_mid: float32 [1024], replicated, may hold values from -3 to 3
- cross_query: bfloat16 [1024, 1024], replicated, may hold values from -0.1875 to 0.1875
- cross_memory: bfloat16 [1024, 2048], replicated, may hold values from -0.1875 to 0.1875
- cross_out: bfloat16 [1024, 1024], replicated, may hold values from -3 to 3
- gain_last: float32 [1024], replicated, may hold values from 0.25 to 1.75
- bias_last: float32 [1024], replicated, may hold values from -3 to 3
- up_weight: bfloat16 [1024, 4096], replicated, may hold values from -0.1875 to 0.1875
- down_weight: bfloat16 [4096, 1024], replicated, may hold values from -0.09375 to 0.09375
Outputs:
- layer_out: float32 [4, 768, 1024], P('batch', 'blk')
- grad_triplane: float32 [4, 768, 1024], P('batch', 'blk')
- grad_patches: float32 [4, 256, 1024], P('batch', 'blk')
- grad_camera_table: float32 [256, 1024], P(('batch', 'blk'))
- grad_mod_weight: float32 [1024, 2048], P(('batch', 'blk'))
- grad_qkv_weight: float32 [1024, 3072], P(('batch', 'blk'))
- grad_self_out: float32 [1024, 1024], P(('batch', 'blk'))
- grad_gain_mid: float32 [1024], P(('batch', 'blk'))
- grad_bias_mid: float32 [1024], P(('batch', 'blk'))
- grad_cross_query: float32 [1024, 1024], P(('batch', 'blk'))
- grad_cross_memory: float32 [1024, 2048], P(('batch', 'blk'))
- grad_cross_out: float32 [1024, 1024], P(('batch', 'blk'))
- grad_gain_last: float32 [1024], P(('batch', 'blk'))
- grad_bias_last: float32 [1024], P(('batch', 'blk'))
- grad_up_weight: float32 [1024, 4096], P(('batch', 'blk'))
- grad_down_weight: float32 [4096, 1024], P(('batch', 'blk'))
The draws below stay inside these ranges and needn't reach their ends.
Inputs may be any that keep to these rules, and one draw needn't show every extreme that they name: Only the first triplane_count triplane tokens of an item are keys of its self-attention; in every draw one item of each 2 in a row has all 768, the others lose at most 48. Only the first patch_count patch tokens of an item are keys of its cross-attention; in every draw one item of each 2 in a row has all 256, the others lose at most 128.
All inputs are finite; a program needn't handle non-finite values.
Results may differ from the reference program's by a relative error of at most 0.035.
Values may be sent and summed in bfloat16 or wider, within the bound.
No kernel may reach another device: no remote copies, remote signals or barrier semaphores. Data moves between devices by JAX's collectives and lax.ppermute only.
A program may use at most 384 MiB of HBM per device.

```python
import math
import jax
import jax.numpy as jnp
from jax import lax

D = 1024
HEADS = 16
HEAD_DIM = 64
FF = 4096
VIEWS = 4
CAMS = 256
ITEMS_DEV = 2
TRI_DEV = 48
ITEMS = 4
TRI_TOT = 768
PATCH_TOT = 256


def draw_triplane_count(key, part):
    key = jax.random.fold_in(key, 11)
    first, second = jax.random.split(key)
    short = jax.random.randint(first, (ITEMS,), 0, TRI_DEV // 2 + 1)
    whole = jax.random.randint(second, (ITEMS // ITEMS_DEV,), 0, ITEMS_DEV)
    chosen = jnp.arange(ITEMS) % ITEMS_DEV == jnp.repeat(whole, ITEMS_DEV, total_repeat_length=ITEMS)
    short = jnp.where(chosen, 0, short)
    return (TRI_TOT - short).astype(jnp.int32)


def draw_patch_count(key, part):
    key = jax.random.fold_in(key, 23)
    first, second = jax.random.split(key)
    short = jax.random.randint(first, (ITEMS,), 0, PATCH_TOT // 2 + 1)
    whole = jax.random.randint(second, (ITEMS // ITEMS_DEV,), 0, ITEMS_DEV)
    chosen = jnp.arange(ITEMS) % ITEMS_DEV == jnp.repeat(whole, ITEMS_DEV, total_repeat_length=ITEMS)
    short = jnp.where(chosen, 0, short)
    return (PATCH_TOT - short).astype(jnp.int32)


def set_ends(entries, key, least, top_value):
    dims = entries.shape
    index_at = [jax.random.randint(jax.random.fold_in(key, axis), (), 0, dims[axis]) for axis in range(len(dims))]
    entries = entries.at[tuple(index_at)].set(least)
    longest = dims.index(max(dims))
    index_at[longest] = (index_at[longest] + 1) % dims[longest]
    return entries.at[tuple(index_at)].set(top_value)


def steps_of(key, extent, cuts, smallest, largest):
    gain = 1.0
    for position, blocks in cuts:
        draws = jax.random.uniform(jax.random.fold_in(jax.random.fold_in(key, 6), position), (blocks,), jnp.float32, smallest / len(cuts), largest / len(cuts))
        gain = gain * jnp.repeat(jnp.exp(draws), extent[position] // blocks).reshape((-1,) + (1,) * (len(extent) - 1 - position))
    return gain


def normal_values(own_key, extent, deviation, most, cuts=(), kind=jnp.bfloat16):
    loudness = steps_of(own_key, extent, cuts, -0.22, 0.18) if cuts else 1.0
    values = jax.random.normal(own_key, extent, jnp.float32) * deviation * loudness
    return jnp.minimum(jnp.maximum(values, -most), most).astype(kind)


def setup_inputs(seed: int = 0) -> dict:
    streams_of = jax.random.split(jax.random.key(seed), 20)
    return {
        "triplane": normal_values(streams_of[0], (ITEMS, TRI_TOT, D), 1.0, 6.0, ((0, 2), (1, 16))),
        "patches": normal_values(streams_of[1], (ITEMS, PATCH_TOT, D), 1.0, 6.0, ((0, 2), (1, 16))),
        "cotangent": normal_values(streams_of[2], (ITEMS, TRI_TOT, D), 1.0, 6.0, ((0, 2), (1, 16))),
        "camera_index": set_ends(jax.random.randint(streams_of[3], (ITEMS, VIEWS), 0, CAMS), jax.random.fold_in(streams_of[3], 1), 0, CAMS - 1).astype(jnp.int32),
        "triplane_count": draw_triplane_count(jax.random.fold_in(streams_of[19], 71), 0),
        "patch_count": draw_patch_count(jax.random.fold_in(streams_of[19], 71), 0),
        "camera_table": normal_values(streams_of[6], (CAMS, D), 1.0, 6.0),
        "mod_weight": normal_values(streams_of[7], (D, 2 * D), D ** -0.5, 0.1875),
        "qkv_weight": normal_values(streams_of[8], (D, 3 * D), D ** -0.5, 0.1875),
        "self_out": normal_values(streams_of[9], (D, D), 4 ** -0.5, 3.0),
        "gain_mid": jnp.clip(1.0 + 0.15 * jax.random.normal(streams_of[10], (D,), jnp.float32), 0.25, 1.75),
        "bias_mid": normal_values(streams_of[11], (D,), 0.5, 3.0, (), jnp.float32),
        "cross_query": normal_values(streams_of[12], (D, D), D ** -0.5, 0.1875),
        "cross_memory": normal_values(streams_of[13], (D, 2 * D), D ** -0.5, 0.1875),
        "cross_out": normal_values(streams_of[14], (D, D), 4 ** -0.5, 3.0),
        "gain_last": jnp.clip(1.0 + 0.15 * jax.random.normal(streams_of[15], (D,), jnp.float32), 0.25, 1.75),
        "bias_last": normal_values(streams_of[16], (D,), 0.5, 3.0, (), jnp.float32),
        "up_weight": normal_values(streams_of[17], (D, FF), D ** -0.5, 0.1875),
        "down_weight": normal_values(streams_of[18], (FF, D), FF ** -0.5, 0.09375),
    }


@jax.custom_vjp
def low(v):
    return lax.optimization_barrier(v.astype(jnp.bfloat16)).astype(jnp.float32)

@jax.custom_vjp
def low_back(v):
    return v

def low_keep(v):
    return (low(v), None)

def low_pass(kept, grad):
    return (grad,)

def back_keep(v):
    return (v, None)

def back_low(kept, grad):
    return (low(grad),)
low.defvjp(low_keep, low_pass)
low_back.defvjp(back_keep, back_low)

def normalize(values):
    center = values - lax.optimization_barrier(jnp.mean(values, axis=-1, keepdims=True))
    return center * lax.rsqrt(lax.optimization_barrier(jnp.mean(center * center, axis=-1, keepdims=True)) + 1e-05)

def attention(queries, memory, limit):
    rows, width = queries.shape
    keys = memory[:, :width].reshape(memory.shape[0], HEADS, HEAD_DIM)
    values = memory[:, width:].reshape(memory.shape[0], HEADS, HEAD_DIM)
    stride = math.gcd(rows, 256)
    valid = jnp.arange(memory.shape[0], dtype=jnp.int32) < limit

    def block(part):
        heads_q = part.reshape(stride, HEADS, HEAD_DIM)
        scores = low_back(jnp.einsum('rhd,nhd->hrn', heads_q, keys, precision=lax.Precision.HIGHEST) * HEAD_DIM ** (-0.5))
        scores = jnp.where(valid[None, None, :], scores, -1e+30)
        probs = jax.nn.softmax(scores, axis=-1)
        return jnp.einsum('hrn,nhd->rhd', low(probs), values, precision=lax.Precision.HIGHEST).reshape(stride, width)
    blocks = queries.reshape(rows // stride, stride, width)
    return lax.map(jax.checkpoint(block), blocks).reshape(rows, width)

def layer(params, triplane, patches, cams, self_limit, cross_limit):
    table, mod_weight, qkv_weight, self_out, gain_mid, bias_mid, cross_query, cross_memory, cross_out, gain_last, bias_last, up_weight, down_weight = params
    highest = lax.Precision.HIGHEST
    width = triplane.shape[1]
    pick = (cams[:, None] == jnp.arange(CAMS, dtype=jnp.int32)[None, :]).astype(jnp.float32)
    code = lax.optimization_barrier(jnp.mean(jnp.dot(pick, table, precision=highest), axis=0))
    modulation = jnp.dot(low(code), mod_weight, precision=highest)
    shift = modulation[:width]
    scale = modulation[width:]
    normed = low(normalize(triplane) * (1.0 + scale) + shift)
    packed = low_back(low(jnp.dot(normed, qkv_weight, precision=highest)))
    attended = low_back(low(attention(packed[:, :width], packed[:, width:], self_limit)))
    middle = triplane + low_back(jnp.dot(attended, self_out, precision=highest))
    normed_mid = low(normalize(middle) * gain_mid + bias_mid)
    cross_q = low_back(low(jnp.dot(normed_mid, cross_query, precision=highest)))
    memory = low_back(low(jnp.dot(patches, cross_memory, precision=highest)))
    crossed = low_back(low(attention(cross_q, memory, cross_limit)))
    later = middle + low_back(jnp.dot(crossed, cross_out, precision=highest))
    normed_last = low(normalize(later) * gain_last + bias_last)
    hidden = low(jax.nn.gelu(low_back(jnp.dot(normed_last, up_weight, precision=highest))))
    return later + jnp.dot(hidden, down_weight, precision=highest)

def reference(triplane, patches, cotangent, camera_index, triplane_count, patch_count, camera_table, mod_weight, qkv_weight, self_out, gain_mid, bias_mid, cross_query, cross_memory, cross_out, gain_last, bias_last, up_weight, down_weight):
    params = tuple((entry.astype(jnp.float32) for entry in (camera_table, mod_weight, qkv_weight, self_out, gain_mid, bias_mid, cross_query, cross_memory, cross_out, gain_last, bias_last, up_weight, down_weight)))

    def forward(weights, tri_values, patch_values):

        def one_item(pieces):
            tri_rows, patch_rows, cams, self_limit, cross_limit = pieces
            return layer(weights, tri_rows, patch_rows, cams, self_limit, cross_limit)
        return lax.map(one_item, (tri_values, patch_values, camera_index, triplane_count, patch_count))
    result, pull = jax.vjp(forward, params, triplane.astype(jnp.float32), patches.astype(jnp.float32))
    grads, grad_triplane, grad_patches = pull(cotangent.astype(jnp.float32))
    g_table, g_mod, g_qkv, g_self, g_gain_mid, g_bias_mid, g_cross_q, g_cross_mem, g_cross_out, g_gain_last, g_bias_last, g_up, g_down = grads
    return (result, grad_triplane, grad_patches, g_table, g_mod, g_qkv, g_self, g_gain_mid, g_bias_mid, g_cross_q, g_cross_mem, g_cross_out, g_gain_last, g_bias_last, g_up, g_down)
```

```python
import functools

import jax
import jax.numpy as jnp
from jax import lax
from jax.experimental import pallas as pl
from jax.experimental.pallas import tpu as pltpu
from jax.sharding import PartitionSpec as P

HEADS = 16
HEAD_DIM = 64
LANES = 128
PAIRS = HEADS * HEAD_DIM // LANES
BF = jnp.bfloat16
F32 = jnp.float32
BOTH = ("batch", "blk")
TINY = -1e30


def mm(a, b):
    return jnp.dot(a, b, preferred_element_type=F32)


def mm_nt(a, b):
    return lax.dot_general(a, b, (((1,), (1,)), ((), ())), preferred_element_type=F32)


def mm_tn(a, b):
    return lax.dot_general(a, b, (((0,), (0,)), ((), ())), preferred_element_type=F32)


def center_scale(values):
    center = values - jnp.mean(values, axis=-1, keepdims=True)
    rstd = lax.rsqrt(jnp.mean(center * center, axis=-1, keepdims=True) + 1e-05)
    return center * rstd, rstd


def norm_back(unit, rstd, grad):
    return rstd * (
        grad
        - jnp.mean(grad, axis=-1, keepdims=True)
        - unit * jnp.mean(grad * unit, axis=-1, keepdims=True)
    )


def self_forward_kernel(count_ref, q_ref, k_ref, v_ref, out_ref, lse_ref):
    queries = q_ref[...].reshape(-1, LANES) * BF(HEAD_DIM**-0.5)
    keys = k_ref[...].reshape(-1, LANES)
    values_t = v_ref[...].reshape(-1, LANES).T
    lane = lax.broadcasted_iota(jnp.int32, queries.shape, 1) // HEAD_DIM
    row = lax.broadcasted_iota(jnp.int32, (keys.shape[0], queries.shape[0]), 0)
    parts = []
    for item in range(2):
        mine = jnp.where(lane == item, queries, BF(0))
        scores = jnp.where(row < count_ref[item], mm_nt(keys, mine), TINY)
        top = jnp.max(scores, axis=0, keepdims=True)
        weights = jnp.exp(scores - top)
        total = jnp.sum(weights, axis=0, keepdims=True)
        span = slice(item * HEAD_DIM, (item + 1) * HEAD_DIM)
        parts.append(mm(values_t[span], weights.astype(BF)) / total)
        lse_ref[item : item + 1, :] = top + jnp.log(total)
    out = jnp.concatenate(parts, axis=0).T
    out_ref[...] = out.astype(BF).reshape(out_ref.shape)


def self_backward_kernel(
    steps, count_ref, q_ref, k_ref, v_ref, do_ref, lse_ref, dq_ref, dkv_ref, dk_acc, dv_acc
):
    step = pl.program_id(0)
    queries = q_ref[...].reshape(-1, LANES) * BF(HEAD_DIM**-0.5)
    keys = k_ref[...].reshape(-1, LANES)
    values = v_ref[...].reshape(-1, LANES)
    keys_t = keys.T
    grads = do_ref[...].reshape(-1, LANES)
    lane = lax.broadcasted_iota(jnp.int32, queries.shape, 1) // HEAD_DIM
    row = lax.broadcasted_iota(jnp.int32, (keys.shape[0], queries.shape[0]), 0)
    parts = []
    d_keys = None
    for item in range(2):
        mine = jnp.where(lane == item, queries, BF(0))
        d_mine = jnp.where(lane == item, grads, BF(0))
        scores = mm_nt(keys, mine)
        probs = jnp.where(
            row < count_ref[item], jnp.exp(scores - lse_ref[item : item + 1, :]), 0.0
        )
        d_probs = mm_nt(values, d_mine)
        delta = jnp.sum(probs * d_probs, axis=0, keepdims=True)
        d_scores = (probs * (d_probs - delta)).astype(BF)
        new_v = mm(probs.astype(BF), d_mine)
        new_k = mm(d_scores, mine)
        d_values = new_v if d_keys is None else d_values + new_v
        d_keys = new_k if d_keys is None else d_keys + new_k
        span = slice(item * HEAD_DIM, (item + 1) * HEAD_DIM)
        parts.append(mm(keys_t[span], d_scores) * HEAD_DIM**-0.5)
    d_q = jnp.concatenate(parts, axis=0).T
    dq_ref[...] = d_q.astype(BF).reshape(dq_ref.shape)

    @pl.when(step == 0)
    def _():
        dk_acc[...] = d_keys
        dv_acc[...] = d_values

    @pl.when(step > 0)
    def _():
        dk_acc[...] += d_keys
        dv_acc[...] += d_values

    @pl.when(step == steps - 1)
    def _():
        shape = (dkv_ref.shape[0], 1) + dkv_ref.shape[2:]
        dkv_ref[:, 0:1] = dk_acc[...].astype(dkv_ref.dtype).reshape(shape)
        dkv_ref[:, 1:2] = dv_acc[...].astype(dkv_ref.dtype).reshape(shape)


def q_steps(blocks):
    return 2 if blocks % 2 == 0 else 1


def self_specs(q_arr, kv_arr, first):
    blocks, _, rows, _ = q_arr.shape
    steps = q_steps(blocks)
    part = blocks // steps
    many = kv_arr.shape[0]
    return steps, part, rows, many, [
        pl.BlockSpec(memory_space=pltpu.SMEM),
        pl.BlockSpec((part, 1, rows, LANES), lambda i: (i, 0, 0, 0)),
        pl.BlockSpec((many, 1, rows, LANES), lambda i: (0, first, 0, 0)),
        pl.BlockSpec((many, 1, rows, LANES), lambda i: (0, first + 1, 0, 0)),
    ]


def self_forward(counts, q_arr, kv_arr, first):
    steps, part, rows, many, specs = self_specs(q_arr, kv_arr, first)
    blocks = q_arr.shape[0]
    pairs = blocks * rows * many * rows * 2
    return pl.pallas_call(
        self_forward_kernel,
        grid=(steps,),
        in_specs=specs,
        out_specs=[
            pl.BlockSpec((part, rows, LANES), lambda i: (i, 0, 0)),
            pl.BlockSpec((2, part * rows), lambda i: (0, i)),
        ],
        out_shape=[
            jax.ShapeDtypeStruct((blocks, rows, LANES), BF),
            jax.ShapeDtypeStruct((2, blocks * rows), F32),
        ],
        compiler_params=pltpu.CompilerParams(vmem_limit_bytes=56 << 20),
        cost_estimate=pl.CostEstimate(
            flops=pairs * 4 * LANES, bytes_accessed=1 << 20, transcendentals=pairs
        ),
        name="self_forward",
    )(counts, q_arr, kv_arr, kv_arr)


def self_backward(counts, q_arr, kv_arr, first, d_out, lse, low):
    steps, part, rows, many, specs = self_specs(q_arr, kv_arr, first)
    blocks = q_arr.shape[0]
    pairs = blocks * rows * many * rows * 2
    return pl.pallas_call(
        functools.partial(self_backward_kernel, steps),
        grid=(steps,),
        in_specs=specs
        + [
            pl.BlockSpec((part, rows, LANES), lambda i: (i, 0, 0)),
            pl.BlockSpec((2, part * rows), lambda i: (0, i)),
        ],
        out_specs=[
            pl.BlockSpec((part, 1, rows, LANES), lambda i: (i, 0, 0, 0)),
            pl.BlockSpec((many, 2, rows, LANES), lambda i: (0, 0, 0, 0)),
        ],
        out_shape=[
            jax.ShapeDtypeStruct((blocks, 1, rows, LANES), BF),
            jax.ShapeDtypeStruct((many, 2, rows, LANES), BF if low else F32),
        ],
        scratch_shapes=[
            pltpu.VMEM((many * rows, LANES), F32),
            pltpu.VMEM((many * rows, LANES), F32),
        ],
        compiler_params=pltpu.CompilerParams(vmem_limit_bytes=56 << 20),
        cost_estimate=pl.CostEstimate(
            flops=pairs * 10 * LANES, bytes_accessed=2 << 20, transcendentals=pairs
        ),
        name="self_backward",
    )(counts, q_arr, kv_arr, kv_arr, d_out, lse)


def stack_heads(block, lane):
    zero = jnp.zeros((), block.dtype)
    return jnp.concatenate(
        [jnp.where(lane < HEAD_DIM, block, zero), jnp.where(lane >= HEAD_DIM, block, zero)], axis=0
    )


def merge_heads(block, lane):
    rows = block.shape[0] // 2
    return jnp.where(lane < HEAD_DIM, block[:rows], block[rows:])


def cross_forward_kernel(count_ref, q_ref, mem_ref, out_ref, lse_ref):
    item = pl.program_id(0)
    limit = count_ref[item]
    rows = q_ref.shape[1]
    width = q_ref.shape[2]
    many = mem_ref.shape[1]
    lane = lax.broadcasted_iota(jnp.int32, (rows, LANES), 1)
    row = lax.broadcasted_iota(jnp.int32, (many, 2 * rows), 0)
    for pair in range(width // LANES):
        span = slice(pair * LANES, (pair + 1) * LANES)
        over = slice(width + pair * LANES, width + (pair + 1) * LANES)
        queries = stack_heads(q_ref[0, :, span] * BF(HEAD_DIM**-0.5), lane)
        scores = jnp.where(row < limit, mm_nt(mem_ref[0, :, span], queries), TINY)
        top = jnp.max(scores, axis=0, keepdims=True)
        weights = jnp.exp(scores - top)
        total = jnp.sum(weights, axis=0, keepdims=True)
        out = mm(mem_ref[0, :, over].T, weights.astype(BF)) / total
        out_ref[0, :, span] = merge_heads(out.T, lane).astype(BF)
        lse_ref[0, pair : pair + 1, : 2 * rows] = top + jnp.log(total)


def cross_backward_kernel(count_ref, q_ref, mem_ref, do_ref, lse_ref, dq_ref, dmem_ref):
    item = pl.program_id(0)
    limit = count_ref[item]
    rows = q_ref.shape[1]
    width = q_ref.shape[2]
    many = mem_ref.shape[1]
    pairs = width // LANES
    lane = lax.broadcasted_iota(jnp.int32, (rows, LANES), 1)
    row = lax.broadcasted_iota(jnp.int32, (many, 2 * rows), 0)
    for pair in range(pairs):
        span = slice(pair * LANES, (pair + 1) * LANES)
        over = slice(width + pair * LANES, width + (pair + 1) * LANES)
        queries = stack_heads(q_ref[0, :, span] * BF(HEAD_DIM**-0.5), lane)
        grads = stack_heads(do_ref[0, :, span], lane)
        keys = mem_ref[0, :, span]
        scores = mm_nt(keys, queries)
        probs = jnp.where(
            row < limit, jnp.exp(scores - lse_ref[0, pair : pair + 1, : 2 * rows]), 0.0
        )
        d_probs = mm_nt(mem_ref[0, :, over], grads)
        delta = jnp.sum(probs * d_probs, axis=0, keepdims=True)
        d_scores = (probs * (d_probs - delta)).astype(BF)
        dmem_ref[pair, 0] = mm(d_scores, queries).astype(dmem_ref.dtype)
        dmem_ref[pairs + pair, 0] = mm(probs.astype(BF), grads).astype(dmem_ref.dtype)
        d_q = mm(keys.T, d_scores) * HEAD_DIM**-0.5
        dq_ref[0, :, span] = merge_heads(d_q.T, lane).astype(BF)


def cross_forward(counts, cross_q, memory):
    items, rows, width = cross_q.shape
    many = memory.shape[1]
    pairs = items * rows * HEADS * many
    return pl.pallas_call(
        cross_forward_kernel,
        grid=(items,),
        in_specs=[
            pl.BlockSpec(memory_space=pltpu.SMEM),
            pl.BlockSpec((1, rows, width), lambda i: (i, 0, 0)),
            pl.BlockSpec((1, many, 2 * width), lambda i: (i, 0, 0)),
        ],
        out_specs=[
            pl.BlockSpec((1, rows, width), lambda i: (i, 0, 0)),
            pl.BlockSpec((1, PAIRS, LANES), lambda i: (i, 0, 0)),
        ],
        out_shape=[
            jax.ShapeDtypeStruct((items, rows, width), BF),
            jax.ShapeDtypeStruct((items, PAIRS, LANES), F32),
        ],
        compiler_params=pltpu.CompilerParams(vmem_limit_bytes=48 << 20),
        cost_estimate=pl.CostEstimate(
            flops=pairs * 4 * LANES, bytes_accessed=3 << 20, transcendentals=pairs
        ),
        name="cross_forward",
    )(counts, cross_q, memory)


def cross_backward(counts, cross_q, memory, d_out, lse):
    items, rows, width = cross_q.shape
    many = memory.shape[1]
    pairs = items * rows * HEADS * many
    return pl.pallas_call(
        cross_backward_kernel,
        grid=(items,),
        in_specs=[
            pl.BlockSpec(memory_space=pltpu.SMEM),
            pl.BlockSpec((1, rows, width), lambda i: (i, 0, 0)),
            pl.BlockSpec((1, many, 2 * width), lambda i: (i, 0, 0)),
            pl.BlockSpec((1, rows, width), lambda i: (i, 0, 0)),
            pl.BlockSpec((1, PAIRS, LANES), lambda i: (i, 0, 0)),
        ],
        out_specs=[
            pl.BlockSpec((1, rows, width), lambda i: (i, 0, 0)),
            pl.BlockSpec((2 * PAIRS, 1, many, LANES), lambda i: (0, i, 0, 0)),
        ],
        out_shape=[
            jax.ShapeDtypeStruct((items, rows, width), BF),
            jax.ShapeDtypeStruct((2 * PAIRS, items, many, LANES), BF),
        ],
        compiler_params=pltpu.CompilerParams(vmem_limit_bytes=48 << 20),
        cost_estimate=pl.CostEstimate(
            flops=pairs * 10 * LANES, bytes_accessed=6 << 20, transcendentals=pairs
        ),
        name="cross_backward",
    )(counts, cross_q, memory, d_out, lse)


def xor_blk(values, bit, count):
    return lax.ppermute(values, "blk", [(i, i ^ bit) for i in range(count)])


def swap_batch(values):
    return lax.ppermute(values, "batch", [(0, 1), (1, 0)])


def take(values, index, axis):
    return lax.dynamic_index_in_dim(values, index, axis, keepdims=False)


def local(
    count_blk,
    triplane,
    patches,
    cotangent,
    camera_index,
    triplane_count,
    patch_count,
    camera_table,
    mod_weight,
    qkv_weight,
    self_out,
    gain_mid,
    bias_mid,
    cross_query,
    cross_memory,
    cross_out,
    gain_last,
    bias_last,
    up_weight,
    down_weight,
):
    items, own, width = triplane.shape
    own_patches = patches.shape[1]
    rows = items * own
    spare = count_blk // HEADS
    devices = 2 * count_blk
    row_groups = (
        None
        if spare == 1
        else [[part * HEADS + head for head in range(HEADS)] for part in range(spare)]
    )
    head_groups = [[part * HEADS + head for part in range(spare)] for head in range(HEADS)]
    rest_groups = [[low + 4 * k for k in range(count_blk // 4)] for low in range(4)]
    batch_at = lax.axis_index("batch")
    blk_at = lax.axis_index("blk")
    head_at = lax.rem(blk_at, HEADS)

    def to_heads(values):
        return lax.all_to_all(values, "blk", 0, 0, axis_index_groups=row_groups, tiled=True)

    def quad_y(values):
        paired = jnp.stack([values, xor_blk(values, 2, count_blk)])
        other = xor_blk(paired, 1, count_blk)
        return jnp.concatenate([paired[0], other[0], paired[1], other[1]], axis=0)

    def quad_x(values):
        paired = jnp.stack([values, swap_batch(values)])
        other = xor_blk(paired, 1, count_blk)
        return jnp.concatenate([paired[0], other[0], paired[1], other[1]], axis=0)

    def pieces_y(values):
        span = values.shape[1] // devices
        cut = values.reshape(values.shape[0], 2, count_blk // 4, 4, span)
        cut = jnp.transpose(cut, (3, 0, 1, 2, 4)).reshape(4, values.shape[0], -1)
        low = jnp.bitwise_and(blk_at, 3)
        got = [take(cut, low, 0)]
        for bit in (1, 2, 3):
            got.append(xor_blk(take(cut, jnp.bitwise_xor(low, bit), 0), bit, count_blk))
        return jnp.concatenate(got, axis=0)

    def pieces_x(values):
        span = values.shape[1] // devices
        cut = values.reshape(values.shape[0], 2, count_blk // 2, 2, span)
        cut = jnp.transpose(cut, (1, 3, 0, 2, 4)).reshape(4, values.shape[0], -1)
        low = jnp.bitwise_and(blk_at, 1)
        got = [take(cut, 2 * batch_at + low, 0)]
        got.append(xor_blk(take(cut, 2 * batch_at + 1 - low, 0), 1, count_blk))
        far = take(cut, 2 * (1 - batch_at) + low, 0)
        got.append(swap_batch(far))
        far = take(cut, 2 * (1 - batch_at) + 1 - low, 0)
        got.append(
            lax.ppermute(
                far,
                BOTH,
                [
                    (b * count_blk + j, (1 - b) * count_blk + (j ^ 1))
                    for b in range(2)
                    for j in range(count_blk)
                ],
            )
        )
        return jnp.concatenate(got, axis=0)

    def rest_sum(values):
        got = lax.all_to_all(values, "blk", 0, 0, axis_index_groups=rest_groups, tiled=True)
        return jnp.sum(got.astype(F32), axis=0)

    def finish_y(product):
        given = swap_batch(take(product, 1 - batch_at, 0))
        kept = take(product, batch_at, 0).astype(F32) + given.astype(F32)
        return rest_sum(kept.astype(BF))

    def finish_x(product):
        bit = jnp.bitwise_and(lax.div(blk_at, 2), 1)
        given = xor_blk(take(product, 1 - bit, 1), 2, count_blk)
        kept = take(product, bit, 1).astype(F32) + given.astype(F32)
        return rest_sum(kept.astype(BF))

    def product_y(left, right):
        span = left.shape[1] // (count_blk // 2)
        return mm_tn(left, right).astype(BF).reshape(2, count_blk // 4, span, right.shape[1])

    def product_x(left, right):
        span = left.shape[1] // (count_blk // 2)
        return mm_tn(left, right).astype(BF).reshape(count_blk // 4, 2, span, right.shape[1])

    others = swap_batch(camera_index)
    cams = jnp.where(
        batch_at == 0,
        jnp.concatenate([camera_index, others], axis=0),
        jnp.concatenate([others, camera_index], axis=0),
    )
    views = cams.shape[1]
    table_rows = jnp.arange(camera_table.shape[0], dtype=jnp.int32)
    pick = jnp.sum((cams[:, :, None] == table_rows[None, None, :]).astype(F32), axis=1)
    code_low = (mm(pick.astype(BF), camera_table) / views).astype(BF)
    code_mine = lax.dynamic_slice_in_dim(code_low, batch_at * items, items, 0)
    modulation = mm(code_mine, mod_weight)
    shift = modulation[:, :width]
    scale = modulation[:, width:]
    inputs = triplane.astype(F32)
    unit_first, rstd_first = center_scale(inputs)
    normed = (unit_first * (1.0 + scale[:, None, :]) + shift[:, None, :]).astype(BF)
    packed = mm(normed.reshape(rows, width), qkv_weight).astype(BF)
    sent = jnp.transpose(
        packed.reshape(items, own, 3, HEADS, HEAD_DIM), (3, 2, 1, 0, 4)
    ).reshape(HEADS, 3, own, items * HEAD_DIM)
    qkv = to_heads(sent)

    patches_all = lax.all_gather(patches, "blk", axis=1, tiled=True)
    many_patches = patches_all.shape[1]
    memory = (
        mm(patches_all.reshape(items * many_patches, width), cross_memory)
        .astype(BF)
        .reshape(items, many_patches, 2 * width)
    )
    grad_out = cotangent.reshape(rows, width)
    d_hidden = mm_nt(grad_out, down_weight)
    grad_quad = quad_x(grad_out)

    if spare == 1:
        kv, kv_first = qkv, 1
    else:
        kv = lax.all_gather(qkv[:, 1:], "blk", axis=0, axis_index_groups=head_groups, tiled=True)
        kv_first = 0
    attended_heads, self_lse = self_forward(triplane_count, qkv, kv, kv_first)
    attended_got = to_heads(attended_heads)

    def to_rows(got):
        return jnp.transpose(
            got.reshape(HEADS, own, items, HEAD_DIM), (2, 1, 0, 3)
        ).reshape(rows, width)

    attended_low = to_rows(attended_got)
    middle = inputs.reshape(rows, width) + mm(attended_low, self_out)
    unit_mid, rstd_mid = center_scale(middle)
    normed_mid = (unit_mid * gain_mid + bias_mid).astype(BF)
    cross_q = mm(normed_mid, cross_query).astype(BF).reshape(items, own, width)
    crossed, cross_lse = cross_forward(patch_count, cross_q, memory)
    crossed_low = crossed.reshape(rows, width)
    later = middle + mm(crossed_low, cross_out)
    unit_last, rstd_last = center_scale(later)
    normed_last = (unit_last * gain_last + bias_last).astype(BF)
    hidden_pre = mm(normed_last, up_weight)
    hidden, gelu_back = jax.vjp(jax.nn.gelu, hidden_pre)
    hidden = hidden.astype(BF)
    result = later + mm(hidden, down_weight)
    d_pre = gelu_back(d_hidden)[0].astype(BF)

    down_product = product_x(pieces_x(hidden), grad_quad)
    up_product = product_y(pieces_y(normed_last), quad_y(d_pre))
    d_normed_last = mm_nt(d_pre, up_weight)
    d_gain_last = jnp.sum(d_normed_last * unit_last, axis=0)
    d_bias_last = jnp.sum(d_normed_last, axis=0)
    d_later = grad_out.astype(F32) + norm_back(unit_last, rstd_last, d_normed_last * gain_last)
    d_later_low = d_later.astype(BF)
    cross_out_product = product_x(pieces_x(crossed_low), quad_x(d_later_low))
    g_up = finish_y(up_product)
    down_both = finish_x(jnp.concatenate([down_product, cross_out_product], axis=2))
    down_rows = down_product.shape[2]
    g_down, g_cross_out = down_both[:down_rows], down_both[down_rows:]

    d_crossed = mm_nt(d_later_low, cross_out).astype(BF).reshape(items, own, width)
    d_cross_q, d_memory = cross_backward(patch_count, cross_q, memory, d_crossed, cross_lse)
    d_cross_low = d_cross_q.reshape(rows, width)
    d_normed_mid = mm_nt(d_cross_low, cross_query)
    d_gain_mid = jnp.sum(d_normed_mid * unit_mid, axis=0)
    d_bias_mid = jnp.sum(d_normed_mid, axis=0)
    d_middle = d_later + norm_back(unit_mid, rstd_mid, d_normed_mid * gain_mid)
    d_middle_low = d_middle.astype(BF)
    d_attended = mm_nt(d_middle_low, self_out).astype(BF)
    d_attended = jnp.transpose(
        d_attended.reshape(items, own, HEADS, HEAD_DIM), (2, 1, 0, 3)
    ).reshape(HEADS, own, items * HEAD_DIM)
    d_attended = to_heads(d_attended)
    query_product = product_y(pieces_y(normed_mid), quad_y(d_cross_low))
    self_product = product_y(pieces_y(attended_low), quad_y(d_middle_low))
    both = finish_y(jnp.concatenate([query_product, self_product], axis=2))
    half = query_product.shape[2]
    g_cross_q, g_self = both[:half], both[half:]

    if spare > 1:
        d_memory = lax.psum_scatter(
            d_memory.astype(F32),
            "blk",
            scatter_dimension=2,
            axis_index_groups=head_groups,
            tiled=True,
        ).astype(BF)
    bit = 1
    while bit < HEADS:
        low = jnp.bitwise_and(lax.div(blk_at, bit), 1)
        cut = d_memory.reshape((d_memory.shape[0] // 2, 2) + d_memory.shape[1:])
        given = xor_blk(take(cut, 1 - low, 1), bit, count_blk)
        d_memory = (take(cut, low, 1).astype(F32) + given.astype(F32)).astype(BF)
        bit *= 2
    d_memory = d_memory[0]
    part_patches = d_memory.shape[1]
    d_memory_rows = jnp.transpose(
        d_memory.reshape(items, HEADS, own_patches, LANES), (1, 0, 2, 3)
    )
    d_memory_rows = to_heads(d_memory_rows)
    d_memory_rows = jnp.transpose(d_memory_rows, (1, 2, 0, 3)).reshape(
        items * own_patches, 2 * width
    )
    d_patches = mm_nt(d_memory_rows, cross_memory)
    first_patch = lax.div(blk_at, HEADS) * part_patches
    patch_part = lax.dynamic_slice_in_dim(patches_all, first_patch, part_patches, 1)
    memory_product = mm_tn(
        patch_part.reshape(items * part_patches, width),
        d_memory.reshape(items * part_patches, LANES),
    )

    def spread(product):
        span = product.shape[0] // devices
        got = lax.all_to_all(
            product.astype(BF).reshape(devices, span, product.shape[1]), BOTH, 0, 0, tiled=True
        )
        got = got.reshape(2 * spare, HEADS, span, product.shape[1])
        return jnp.transpose(jnp.sum(got.astype(F32), axis=0), (1, 0, 2))

    g_cross_mem = spread(memory_product).reshape(-1, 2 * width)

    ends = jnp.stack([d_gain_mid, d_bias_mid, d_gain_last, d_bias_last])
    ends = jnp.transpose(ends.reshape(4, devices, -1), (1, 0, 2)).reshape(devices, -1)
    ends = lax.all_to_all(ends, BOTH, 0, 0, tiled=True)
    ends = jnp.sum(ends, axis=0).reshape(4, -1)

    d_q, d_kv = self_backward(
        triplane_count, qkv, kv, kv_first, d_attended, self_lse, spare == 1
    )
    if spare > 1:
        d_kv = lax.psum_scatter(
            d_kv, "blk", scatter_dimension=0, axis_index_groups=head_groups, tiled=True
        ).astype(BF)
    d_heads = jnp.concatenate([d_q, d_kv], axis=1)
    d_got = to_heads(d_heads)
    d_packed = jnp.transpose(
        d_got.reshape(HEADS, 3, own, items, HEAD_DIM), (3, 2, 1, 0, 4)
    ).reshape(rows, 3 * width)

    kept = lax.optimization_barrier((triplane, attended_heads))[0]
    rows_all = lax.all_gather(kept, "blk", axis=1, axis_index_groups=row_groups, tiled=True)
    unit_all = center_scale(rows_all.astype(F32))[0].astype(BF)
    d_items = jnp.transpose(
        d_heads.reshape(HEADS, 3, own, items, HEAD_DIM), (3, 0, 2, 1, 4)
    ).reshape(items, HEADS * own, 3 * HEAD_DIM)
    outer = jnp.einsum("ird,ire->ide", unit_all, d_items, preferred_element_type=F32)
    column = jnp.sum(d_items.astype(F32), axis=1)
    qkv_product = jnp.sum(
        outer * (1.0 + scale[:, :, None]) + shift[:, :, None] * column[:, None, :], axis=0
    )
    head_weight = take(qkv_weight.reshape(width, 3, HEADS, HEAD_DIM), head_at, 2)
    head_weight = head_weight.reshape(width, 3 * HEAD_DIM).astype(F32)
    d_scale = jnp.sum(outer * head_weight, axis=2)
    d_shift = jnp.sum(column[:, None, :] * head_weight, axis=2)
    d_modulation = jnp.concatenate([d_shift, d_scale], axis=1)
    cut = jnp.transpose(d_modulation.reshape(items, count_blk, -1), (1, 0, 2))
    cut = jnp.sum(lax.all_to_all(cut, "blk", 0, 0, tiled=True), axis=0)
    cut = jnp.broadcast_to(cut, (devices,) + cut.shape)
    cut = lax.all_to_all(cut, BOTH, 0, 0, tiled=True)
    d_modulation = jnp.transpose(
        cut.reshape(2, count_blk, items, -1), (0, 2, 1, 3)
    ).reshape(2 * items, 2 * width)
    g_qkv = spread(qkv_product).reshape(-1, HEADS, 3, HEAD_DIM)
    g_qkv = jnp.transpose(g_qkv, (0, 2, 1, 3)).reshape(-1, 3 * width)

    place = batch_at * count_blk + blk_at
    mod_rows = width // devices
    code_rows = lax.dynamic_slice_in_dim(code_low, place * mod_rows, mod_rows, 1).astype(F32)
    g_mod = jnp.sum(code_rows[:, :, None] * d_modulation[:, None, :], axis=0)
    d_code = mm_nt(d_modulation.astype(BF), mod_weight)
    cam_rows = camera_table.shape[0] // devices
    pick_rows = lax.dynamic_slice_in_dim(pick, place * cam_rows, cam_rows, 1)
    g_table = jnp.sum(pick_rows[:, :, None] * d_code[:, None, :], axis=0) / views

    d_normed = mm_nt(d_packed, qkv_weight).reshape(items, own, width)
    d_triplane = d_middle.reshape(items, own, width) + norm_back(
        unit_first, rstd_first, d_normed * (1.0 + scale[:, None, :])
    )
    return (
        result.reshape(items, own, width),
        d_triplane,
        d_patches.reshape(items, own_patches, width),
        g_table,
        g_mod,
        g_qkv,
        g_self,
        ends[0],
        ends[1],
        g_cross_q,
        g_cross_mem,
        g_cross_out,
        ends[2],
        ends[3],
        g_up,
        g_down,
    )


def solution(mesh):
    rows = P("batch", "blk", None)
    split = P(BOTH, None)
    line = P(BOTH)
    whole = P()
    return jax.shard_map(
        functools.partial(local, mesh.shape["blk"]),
        mesh=mesh,
        in_specs=(rows, rows, rows, P("batch", None), P("batch"), P("batch")) + (whole,) * 13,
        out_specs=(
            rows,
            rows,
            rows,
            split,
            split,
            split,
            split,
            line,
            line,
            split,
            split,
            split,
            line,
            line,
            split,
            split,
        ),
        check_vma=False,
    )
```

```python
import functools

import jax
import jax.numpy as jnp
from jax import lax
from jax.experimental import pallas as pl
from jax.experimental.pallas import tpu as pltpu
from jax.sharding import PartitionSpec as P

HEADS = 16
HEAD_DIM = 64
LANES = 128
PAIRS = HEADS * HEAD_DIM // LANES
BF = jnp.bfloat16
F32 = jnp.float32
BOTH = ("batch", "blk")
TINY = -1e30
GROUP = 4
WIDE = GROUP * HEAD_DIM
ANYWHERE = pl.BlockSpec(memory_space=pl.ANY)
ROOM = 60 << 20
IN_SMEM = pl.BlockSpec(memory_space=pltpu.SMEM)


def whole(shape):
    return pl.BlockSpec(shape, lambda *at: (0,) * len(shape))


def mm(a, b):
    return jnp.dot(a, b, preferred_element_type=F32)


def mm_nt(a, b):
    return lax.dot_general(a, b, (((1,), (1,)), ((), ())), preferred_element_type=F32)


def mm_tn(a, b):
    return lax.dot_general(a, b, (((0,), (0,)), ((), ())), preferred_element_type=F32)


def center_scale(values):
    center = values - jnp.mean(values, axis=-1, keepdims=True)
    rstd = lax.rsqrt(jnp.mean(center * center, axis=-1, keepdims=True) + 1e-05)
    return center * rstd, rstd


def norm_back(unit, rstd, grad):
    return rstd * (
        grad
        - jnp.mean(grad, axis=-1, keepdims=True)
        - unit * jnp.mean(grad * unit, axis=-1, keepdims=True)
    )


def self_forward_kernel(count_ref, q_ref, k_ref, v_ref, out_ref, lse_ref):
    queries = q_ref[...].reshape(-1, LANES) * BF(HEAD_DIM**-0.5)
    keys = k_ref[...].reshape(-1, LANES)
    values_t = v_ref[...].reshape(-1, LANES).T
    lane = lax.broadcasted_iota(jnp.int32, queries.shape, 1) // HEAD_DIM
    row = lax.broadcasted_iota(jnp.int32, (keys.shape[0], queries.shape[0]), 0)
    parts = []
    for item in range(2):
        mine = jnp.where(lane == item, queries, BF(0))
        scores = jnp.where(row < count_ref[item], mm_nt(keys, mine), TINY)
        top = jnp.max(scores, axis=0, keepdims=True)
        weights = jnp.exp(scores - top)
        total = jnp.sum(weights, axis=0, keepdims=True)
        span = slice(item * HEAD_DIM, (item + 1) * HEAD_DIM)
        parts.append(mm(values_t[span], weights.astype(BF)) / total)
        lse_ref[item : item + 1, :] = top + jnp.log(total)
    out = jnp.concatenate(parts, axis=0).T
    out_ref[...] = out.astype(BF).reshape(out_ref.shape)


def self_backward_kernel(
    steps, count_ref, q_ref, k_ref, v_ref, do_ref, lse_ref, *rest
):
    dq_ref, dkv_ref, dk_acc, dv_acc = rest[-4:]
    step = pl.program_id(0)
    queries = q_ref[...].reshape(-1, LANES) * BF(HEAD_DIM**-0.5)
    keys = k_ref[...].reshape(-1, LANES)
    values = v_ref[...].reshape(-1, LANES)
    keys_t = keys.T
    grads = do_ref[...].reshape(-1, LANES)
    lane = lax.broadcasted_iota(jnp.int32, queries.shape, 1) // HEAD_DIM
    row = lax.broadcasted_iota(jnp.int32, (keys.shape[0], queries.shape[0]), 0)
    parts = []
    d_keys = None
    for item in range(2):
        mine = jnp.where(lane == item, queries, BF(0))
        d_mine = jnp.where(lane == item, grads, BF(0))
        scores = mm_nt(keys, mine)
        probs = jnp.where(
            row < count_ref[item], jnp.exp(scores - lse_ref[item : item + 1, :]), 0.0
        )
        d_probs = mm_nt(values, d_mine)
        delta = jnp.sum(probs * d_probs, axis=0, keepdims=True)
        d_scores = (probs * (d_probs - delta)).astype(BF)
        new_v = mm(probs.astype(BF), d_mine)
        new_k = mm(d_scores, mine)
        d_values = new_v if d_keys is None else d_values + new_v
        d_keys = new_k if d_keys is None else d_keys + new_k
        span = slice(item * HEAD_DIM, (item + 1) * HEAD_DIM)
        parts.append(mm(keys_t[span], d_scores) * HEAD_DIM**-0.5)
    d_q = jnp.concatenate(parts, axis=0).T
    dq_ref[...] = d_q.astype(BF).reshape(dq_ref.shape)

    @pl.when(step == 0)
    def _():
        dk_acc[...] = d_keys
        dv_acc[...] = d_values

    @pl.when(step > 0)
    def _():
        dk_acc[...] += d_keys
        dv_acc[...] += d_values

    @pl.when(step == steps - 1)
    def _():
        shape = (dkv_ref.shape[0], 1) + dkv_ref.shape[2:]
        dkv_ref[:, 0:1] = dk_acc[...].astype(dkv_ref.dtype).reshape(shape)
        dkv_ref[:, 1:2] = dv_acc[...].astype(dkv_ref.dtype).reshape(shape)


def q_steps(blocks):
    return 2 if blocks % 2 == 0 else 1


def self_specs(q_arr, kv_arr, first):
    blocks, _, rows, _ = q_arr.shape
    steps = q_steps(blocks)
    part = blocks // steps
    many = kv_arr.shape[0]
    return steps, part, rows, many, [
        pl.BlockSpec(memory_space=pltpu.SMEM),
        pl.BlockSpec((part, 1, rows, LANES), lambda i: (i, 0, 0, 0)),
        pl.BlockSpec((many, 1, rows, LANES), lambda i: (0, first, 0, 0)),
        pl.BlockSpec((many, 1, rows, LANES), lambda i: (0, first + 1, 0, 0)),
    ]


def self_forward(counts, q_arr, kv_arr, first):
    steps, part, rows, many, specs = self_specs(q_arr, kv_arr, first)
    blocks = q_arr.shape[0]
    pairs = blocks * rows * many * rows * 2
    return pl.pallas_call(
        self_forward_kernel,
        grid=(steps,),
        in_specs=specs,
        out_specs=[
            pl.BlockSpec((part, rows, LANES), lambda i: (i, 0, 0)),
            pl.BlockSpec((2, part * rows), lambda i: (0, i)),
        ],
        out_shape=[
            jax.ShapeDtypeStruct((blocks, rows, LANES), BF),
            jax.ShapeDtypeStruct((2, blocks * rows), F32),
        ],
        compiler_params=pltpu.CompilerParams(vmem_limit_bytes=ROOM),
        cost_estimate=pl.CostEstimate(
            flops=pairs * 4 * LANES, bytes_accessed=1 << 20, transcendentals=pairs
        ),
        name="self_forward",
    )(counts, q_arr, kv_arr, kv_arr)


def self_backward(counts, q_arr, kv_arr, first, d_out, lse, low):
    steps, part, rows, many, specs = self_specs(q_arr, kv_arr, first)
    blocks = q_arr.shape[0]
    pairs = blocks * rows * many * rows * 2
    return pl.pallas_call(
        functools.partial(self_backward_kernel, steps),
        grid=(steps,),
        in_specs=specs
        + [
            pl.BlockSpec((part, 1, rows, LANES), lambda i: (i, 0, 0, 0)),
            pl.BlockSpec((2, part * rows), lambda i: (0, i)),
        ],
        out_specs=[
            pl.BlockSpec((part, 1, rows, LANES), lambda i: (i, 0, 0, 0)),
            pl.BlockSpec((many, 2, rows, LANES), lambda i: (0, 0, 0, 0)),
        ],
        out_shape=[
            jax.ShapeDtypeStruct((blocks, 1, rows, LANES), BF),
            jax.ShapeDtypeStruct((many, 2, rows, LANES), BF if low else F32),
        ],
        scratch_shapes=[
            pltpu.VMEM((many * rows, LANES), F32),
            pltpu.VMEM((many * rows, LANES), F32),
        ],
        compiler_params=pltpu.CompilerParams(vmem_limit_bytes=ROOM),
        cost_estimate=pl.CostEstimate(
            flops=pairs * 10 * LANES, bytes_accessed=2 << 20, transcendentals=pairs
        ),
        name="self_backward",
    )(counts, q_arr, kv_arr, kv_arr, d_out, lse)


def stack_heads(block, lane):
    zero = jnp.zeros((), block.dtype)
    return jnp.concatenate(
        [jnp.where(lane == head, block, zero) for head in range(GROUP)], axis=0
    )


def merge_heads(block, lane):
    rows = block.shape[0] // GROUP
    out = block[:rows]
    for head in range(1, GROUP):
        out = jnp.where(lane == head, block[head * rows : (head + 1) * rows], out)
    return out


def cross_forward_kernel(
    count_ref,
    q_ref,
    mem_ref,
    mid_ref,
    gain,
    bias,
    out_hbm,
    out_ref,
    lse_ref,
    later_ref,
    normed_ref,
    out_w,
    sem,
):
    fetch = pltpu.make_async_copy(out_hbm, out_w, sem)
    fetch.start()
    items, rows, width = q_ref.shape
    many = mem_ref.shape[1]
    lane = lax.broadcasted_iota(jnp.int32, (rows, WIDE), 1) // HEAD_DIM
    row = lax.broadcasted_iota(jnp.int32, (many, GROUP * rows), 0)

    def body(group, carry):
        span = pl.ds(pl.multiple_of(group * WIDE, WIDE), WIDE)
        over = pl.ds(pl.multiple_of(width + group * WIDE, WIDE), WIDE)
        for item in range(items):
            queries = stack_heads(q_ref[item, :, span] * BF(HEAD_DIM**-0.5), lane)
            scores = mm_nt(mem_ref[item, :, span], queries)
            scores = jnp.where(row < count_ref[item], scores, TINY)
            top = jnp.max(scores, axis=0, keepdims=True)
            weights = jnp.exp(scores - top)
            total = jnp.sum(weights, axis=0, keepdims=True)
            out = mm(mem_ref[item, :, over].T, weights.astype(BF)) / total
            out_ref[item, :, span] = merge_heads(out.T, lane).astype(BF)
            lse_ref[item, pl.ds(group, 1), : GROUP * rows] = top + jnp.log(total)
        return carry

    lax.fori_loop(0, width // WIDE, body, 0, unroll=2)
    fetch.wait()
    later = mid_ref[...] + mm(out_ref[...].reshape(items * rows, width), out_w[...])
    later_ref[...] = later
    unit, unused = center_scale(later)
    normed_ref[...] = (unit * gain[...] + bias[...]).astype(BF)


def cross_backward_kernel(count_ref, q_ref, mem_ref, do_ref, lse_ref, dq_ref):
    items, rows, width = q_ref.shape
    many = mem_ref.shape[1]
    lane = lax.broadcasted_iota(jnp.int32, (rows, WIDE), 1) // HEAD_DIM
    row = lax.broadcasted_iota(jnp.int32, (many, GROUP * rows), 0)

    def body(group, carry):
        span = pl.ds(pl.multiple_of(group * WIDE, WIDE), WIDE)
        over = pl.ds(pl.multiple_of(width + group * WIDE, WIDE), WIDE)
        for item in range(items):
            queries = stack_heads(q_ref[item, :, span] * BF(HEAD_DIM**-0.5), lane)
            grads = stack_heads(do_ref[item, :, span], lane)
            keys = mem_ref[item, :, span]
            scores = mm_nt(keys, queries)
            lse = lse_ref[item, pl.ds(group, 1), : GROUP * rows]
            probs = jnp.where(row < count_ref[item], jnp.exp(scores - lse), 0.0)
            d_probs = mm_nt(mem_ref[item, :, over], grads)
            delta = jnp.sum(probs * d_probs, axis=0, keepdims=True)
            d_scores = (probs * (d_probs - delta)).astype(BF)
            d_q = mm(keys.T, d_scores) * HEAD_DIM**-0.5
            dq_ref[item, :, span] = merge_heads(d_q.T, lane).astype(BF)
        return carry

    lax.fori_loop(0, width // WIDE, body, 0, unroll=2)


def cross_forward(counts, cross_q, memory, middle, cross_out, gain, bias):
    items, rows, width = cross_q.shape
    many = memory.shape[1]
    pairs = items * rows * HEADS * many
    return pl.pallas_call(
        cross_forward_kernel,
        grid=(1,),
        in_specs=[IN_SMEM]
        + [whole(x.shape) for x in (cross_q, memory, middle)]
        + [whole((1, width))] * 2
        + [ANYWHERE],
        out_specs=[
            whole((items, rows, width)),
            whole((items, width // WIDE, WIDE)),
            whole((items * rows, width)),
            whole((items * rows, width)),
        ],
        out_shape=[
            jax.ShapeDtypeStruct((items, rows, width), BF),
            jax.ShapeDtypeStruct((items, width // WIDE, WIDE), F32),
            jax.ShapeDtypeStruct((items * rows, width), F32),
            jax.ShapeDtypeStruct((items * rows, width), BF),
        ],
        scratch_shapes=[pltpu.VMEM(cross_out.shape, BF), pltpu.SemaphoreType.DMA],
        compiler_params=pltpu.CompilerParams(vmem_limit_bytes=ROOM),
        cost_estimate=pl.CostEstimate(
            flops=pairs * 4 * WIDE, bytes_accessed=3 << 20, transcendentals=pairs
        ),
        name="cross_forward",
    )(counts, cross_q, memory, middle, gain[None], bias[None], cross_out)


def cross_backward(counts, cross_q, memory, d_out, lse):
    items, rows, width = cross_q.shape
    many = memory.shape[1]
    pairs = items * rows * HEADS * many
    return pl.pallas_call(
        cross_backward_kernel,
        grid=(1,),
        in_specs=[IN_SMEM] + [whole(x.shape) for x in (cross_q, memory, d_out, lse)],
        out_specs=whole((items, rows, width)),
        out_shape=jax.ShapeDtypeStruct((items, rows, width), BF),
        compiler_params=pltpu.CompilerParams(vmem_limit_bytes=ROOM),
        cost_estimate=pl.CostEstimate(
            flops=pairs * 10 * WIDE, bytes_accessed=6 << 20, transcendentals=pairs
        ),
        name="cross_backward",
    )(counts, cross_q, memory, d_out, lse)


def memory_back_kernel(head_ref, count_ref, q_ref, do_ref, k_ref, v_ref, out_ref):
    items, many, _ = k_ref.shape
    odd = lax.rem(head_ref[0], 2)
    queries = q_ref[...].reshape(-1, LANES) * BF(HEAD_DIM**-0.5)
    grads = do_ref[...].reshape(-1, LANES)
    lane = lax.broadcasted_iota(jnp.int32, (many, LANES), 1) // HEAD_DIM
    row = lax.broadcasted_iota(jnp.int32, (many, queries.shape[0]), 0)

    def turn(ref, item):
        block = ref[item].astype(F32)
        block = jnp.where(odd == item, block, swap_half(block))
        return jnp.where(lane == item, block, 0.0).astype(BF)

    d_keys = None
    for item in range(items):
        scores = mm_nt(turn(k_ref, item), queries)
        scores = jnp.where(row < count_ref[item], scores, TINY)
        weights = jnp.exp(scores - jnp.max(scores, axis=0, keepdims=True))
        probs = weights * (1.0 / jnp.sum(weights, axis=0, keepdims=True))
        d_probs = mm_nt(turn(v_ref, item), grads)
        delta = jnp.sum(probs * d_probs, axis=0, keepdims=True)
        d_scores = (probs * (d_probs - delta)).astype(BF)
        new_k = mm(d_scores, queries)
        new_v = mm(probs.astype(BF), grads)
        d_values = new_v if d_keys is None else jnp.where(lane == item, new_v, d_values)
        d_keys = new_k if d_keys is None else jnp.where(lane == item, new_k, d_keys)
    shape = (out_ref.shape[0], 1) + out_ref.shape[2:]
    out_ref[:, 0:1] = d_keys.astype(out_ref.dtype).reshape(shape)
    out_ref[:, 1:2] = d_values.astype(out_ref.dtype).reshape(shape)


def memory_back(head, counts, got, memory, part, low):
    blocks, _, own, _ = got.shape
    items, many, double = memory.shape
    pairs = double // 2 // LANES
    work = items * many * blocks * own
    return pl.pallas_call(
        memory_back_kernel,
        grid_spec=pltpu.PrefetchScalarGridSpec(
            num_scalar_prefetch=2,
            grid=(1,),
            in_specs=[
                pl.BlockSpec((blocks, 1, own, LANES), lambda i, h, c: (0, 1, 0, 0)),
                pl.BlockSpec((blocks, 1, own, LANES), lambda i, h, c: (0, 2, 0, 0)),
                pl.BlockSpec((items, many, LANES), lambda i, h, c: (0, 0, lax.div(h[0], 2))),
                pl.BlockSpec(
                    (items, many, LANES), lambda i, h, c: (0, 0, pairs + lax.div(h[0], 2))
                ),
            ],
            out_specs=whole((many // part, 2, part, LANES)),
        ),
        out_shape=jax.ShapeDtypeStruct((many // part, 2, part, LANES), BF if low else F32),
        compiler_params=pltpu.CompilerParams(vmem_limit_bytes=ROOM),
        cost_estimate=pl.CostEstimate(
            flops=work * 8 * LANES, bytes_accessed=2 << 20, transcendentals=work
        ),
        name="memory_back",
    )(head, counts, got, got, memory, memory)


def swap_half(block):
    return pltpu.roll(block, HEAD_DIM, 1)


def first_half(shape):
    return lax.broadcasted_iota(jnp.int32, shape, 1) < HEAD_DIM


def pair_to_heads(block):
    own = block.shape[0] // 2
    left, right = block[:own], block[own:]
    low = first_half(left.shape)
    return (
        jnp.where(low, left, swap_half(right)),
        jnp.where(low, swap_half(left), right),
    )


def project_kernel(tri_ref, mod_ref, q_ref, k_ref, v_ref, out_ref, normed):
    items, own, width = tri_ref.shape

    @pl.when(pl.program_id(0) == 0)
    def _():
        for item in range(items):
            unit, unused = center_scale(tri_ref[item].astype(F32))
            scale = mod_ref[item : item + 1, width:]
            shift = mod_ref[item : item + 1, :width]
            normed[item * own : (item + 1) * own] = (unit * (1.0 + scale) + shift).astype(BF)

    for kind, ref in enumerate((q_ref, k_ref, v_ref)):
        block = mm(normed[...], ref[...])
        for pair in range(WIDE // LANES):
            first, second = pair_to_heads(block[:, pair * LANES : (pair + 1) * LANES])
            out_ref[2 * pair, kind] = first.astype(BF)
            out_ref[2 * pair + 1, kind] = second.astype(BF)


def project(triplane, modulation, qkv_weight):
    items, own, width = triplane.shape
    steps = width // WIDE
    return pl.pallas_call(
        project_kernel,
        grid=(steps,),
        in_specs=[
            pl.BlockSpec((items, own, width), lambda i: (0, 0, 0)),
            pl.BlockSpec((items, 2 * width), lambda i: (0, 0)),
            pl.BlockSpec((width, WIDE), lambda i: (0, i)),
            pl.BlockSpec((width, WIDE), lambda i: (0, steps + i)),
            pl.BlockSpec((width, WIDE), lambda i: (0, 2 * steps + i)),
        ],
        out_specs=pl.BlockSpec((GROUP, 3, own, LANES), lambda i: (i, 0, 0, 0)),
        out_shape=jax.ShapeDtypeStruct((HEADS, 3, own, LANES), BF),
        scratch_shapes=[pltpu.VMEM((items * own, width), BF)],
        compiler_params=pltpu.CompilerParams(vmem_limit_bytes=ROOM),
        cost_estimate=pl.CostEstimate(
            flops=6 * items * own * width * width, bytes_accessed=8 << 20, transcendentals=0
        ),
        name="project",
    )(triplane, modulation, qkv_weight, qkv_weight, qkv_weight)


def middle_kernel(
    got_ref,
    tri_ref,
    gain,
    bias,
    out_hbm,
    query_hbm,
    att_ref,
    mid_ref,
    normed_ref,
    query_ref,
    out_w,
    query_w,
    sems,
):
    fetch_out = pltpu.make_async_copy(out_hbm, out_w, sems.at[0])
    fetch_out.start()
    fetch_query = pltpu.make_async_copy(query_hbm, query_w, sems.at[1])
    fetch_query.start()
    heads, own, _ = got_ref.shape
    for pair in range(heads // 2):
        left = got_ref[2 * pair].astype(F32)
        right = got_ref[2 * pair + 1].astype(F32)
        low = first_half(left.shape)
        span = slice(pair * LANES, (pair + 1) * LANES)
        att_ref[:own, span] = jnp.where(low, left, swap_half(right)).astype(BF)
        att_ref[own:, span] = jnp.where(low, swap_half(left), right).astype(BF)
    fetch_out.wait()
    middle = tri_ref[...].astype(F32) + mm(att_ref[...], out_w[...])
    mid_ref[...] = middle
    unit, unused = center_scale(middle)
    normed = (unit * gain[...] + bias[...]).astype(BF)
    normed_ref[...] = normed
    fetch_query.wait()
    query_ref[...] = mm(normed, query_w[...]).astype(BF)


def middle_part(got, tri_rows, self_out, gain, bias, cross_query):
    rows, width = tri_rows.shape
    low = jax.ShapeDtypeStruct((rows, width), BF)
    return pl.pallas_call(
        middle_kernel,
        grid=(1,),
        in_specs=[whole(got.shape), whole((rows, width)), whole((1, width)), whole((1, width))]
        + [ANYWHERE] * 2,
        out_specs=[whole((rows, width))] * 4,
        out_shape=[low, jax.ShapeDtypeStruct((rows, width), F32), low, low],
        scratch_shapes=[
            pltpu.VMEM(self_out.shape, BF),
            pltpu.VMEM(cross_query.shape, BF),
            pltpu.SemaphoreType.DMA((2,)),
        ],
        compiler_params=pltpu.CompilerParams(vmem_limit_bytes=ROOM),
        cost_estimate=pl.CostEstimate(
            flops=4 * rows * width * width, bytes_accessed=5 << 20, transcendentals=0
        ),
        name="middle_part",
    )(got, tri_rows, gain[None], bias[None], self_out, cross_query)


def middle_back_kernel(
    dq_ref,
    mid_ref,
    gain,
    later_ref,
    query_ref,
    crossed_ref,
    query_hbm,
    out_hbm,
    d_mid_ref,
    low_ref,
    heads_ref,
    sums_ref,
    query_w,
    out_w,
    sems,
):
    fetch_query = pltpu.make_async_copy(query_hbm, query_w, sems.at[0])
    fetch_query.start()
    fetch_out = pltpu.make_async_copy(out_hbm, out_w, sems.at[1])
    fetch_out.start()

    def by_head(values, kind):
        for pair in range(values.shape[1] // LANES):
            block = values[:, pair * LANES : (pair + 1) * LANES].astype(F32)
            first, second = pair_to_heads(block)
            heads_ref[2 * pair, kind] = first.astype(BF)
            heads_ref[2 * pair + 1, kind] = second.astype(BF)

    by_head(query_ref[...], 1)
    by_head(crossed_ref[...], 2)
    fetch_query.wait()
    d_normed = mm_nt(dq_ref[...], query_w[...])
    unit, rstd = center_scale(mid_ref[...])
    sums_ref[0:1] = jnp.sum(d_normed * unit, axis=0, keepdims=True)
    sums_ref[1:2] = jnp.sum(d_normed, axis=0, keepdims=True)
    d_middle = later_ref[...] + norm_back(unit, rstd, d_normed * gain[...])
    d_mid_ref[...] = d_middle
    low = d_middle.astype(BF)
    low_ref[...] = low
    fetch_out.wait()
    by_head(mm_nt(low, out_w[...]), 0)


def middle_back(own, d_query, cross_query, middle, gain, d_later, self_out, cross_q, d_crossed):
    rows, width = middle.shape
    return pl.pallas_call(
        middle_back_kernel,
        grid=(1,),
        in_specs=[whole((rows, width)), whole((rows, width)), whole((1, width))]
        + [whole((rows, width))] * 3
        + [ANYWHERE] * 2,
        out_specs=[
            whole((rows, width)),
            whole((rows, width)),
            whole((HEADS, 3, own, LANES)),
            whole((2, width)),
        ],
        scratch_shapes=[
            pltpu.VMEM(cross_query.shape, BF),
            pltpu.VMEM(self_out.shape, BF),
            pltpu.SemaphoreType.DMA((2,)),
        ],
        out_shape=[
            jax.ShapeDtypeStruct((rows, width), F32),
            jax.ShapeDtypeStruct((rows, width), BF),
            jax.ShapeDtypeStruct((HEADS, 3, own, LANES), BF),
            jax.ShapeDtypeStruct((2, width), F32),
        ],
        compiler_params=pltpu.CompilerParams(vmem_limit_bytes=ROOM),
        cost_estimate=pl.CostEstimate(
            flops=4 * rows * width * width, bytes_accessed=6 << 20, transcendentals=0
        ),
        name="middle_back",
    )(d_query, middle, gain[None], d_later, cross_q, d_crossed, cross_query, self_out)


def first_back_kernel(
    steps, got_ref, q_ref, k_ref, v_ref, tri_ref, mod_ref, mid_ref, out_ref, total
):
    items, own, width = tri_ref.shape
    step = pl.program_id(0)
    added = None
    for kind, ref in enumerate((q_ref, k_ref, v_ref)):
        columns = []
        for pair in range(WIDE // LANES):
            at = slice(kind * own, (kind + 1) * own)
            left = got_ref[2 * pair, at].astype(F32)
            right = got_ref[2 * pair + 1, at].astype(F32)
            low = first_half(left.shape)
            columns.append(
                jnp.concatenate(
                    [
                        jnp.where(low, left, swap_half(right)),
                        jnp.where(low, swap_half(left), right),
                    ],
                    axis=0,
                )
            )
        term = mm_nt(jnp.concatenate(columns, axis=1).astype(BF), ref[...])
        added = term if added is None else added + term

    @pl.when(step == 0)
    def _():
        total[...] = added

    @pl.when(step > 0)
    def _():
        total[...] += added

    @pl.when(step == steps - 1)
    def _():
        for item in range(items):
            unit, rstd = center_scale(tri_ref[item].astype(F32))
            grad = total[item * own : (item + 1) * own] * (1.0 + mod_ref[item : item + 1, width:])
            out_ref[item] = mid_ref[item] + norm_back(unit, rstd, grad)


def first_back(got, qkv_weight, triplane, modulation, d_middle):
    items, own, width = triplane.shape
    steps = width // WIDE
    return pl.pallas_call(
        functools.partial(first_back_kernel, steps),
        grid=(steps,),
        in_specs=[
            pl.BlockSpec((GROUP,) + got.shape[1:], lambda i: (i, 0, 0)),
            pl.BlockSpec((width, WIDE), lambda i: (0, i)),
            pl.BlockSpec((width, WIDE), lambda i: (0, steps + i)),
            pl.BlockSpec((width, WIDE), lambda i: (0, 2 * steps + i)),
            pl.BlockSpec((items, own, width), lambda i: (0, 0, 0)),
            pl.BlockSpec((items, 2 * width), lambda i: (0, 0)),
            pl.BlockSpec((items, own, width), lambda i: (0, 0, 0)),
        ],
        out_specs=pl.BlockSpec((items, own, width), lambda i: (0, 0, 0)),
        out_shape=jax.ShapeDtypeStruct((items, own, width), F32),
        scratch_shapes=[pltpu.VMEM((items * own, width), F32)],
        compiler_params=pltpu.CompilerParams(vmem_limit_bytes=ROOM),
        cost_estimate=pl.CostEstimate(
            flops=6 * items * own * width * width, bytes_accessed=8 << 20, transcendentals=0
        ),
        name="first_back",
    )(got, qkv_weight, qkv_weight, qkv_weight, triplane, modulation, d_middle)


def head_back_kernel(
    packed,
    head_ref,
    dq_ref,
    dkv_ref,
    dmem_ref,
    tri_ref,
    patch_ref,
    q_ref,
    k_ref,
    v_ref,
    mod_ref,
    *rest,
):
    units = rest[-1]
    items, many, width = tri_ref.shape
    odd = lax.rem(head_ref[0], 2) == 1
    grads = [
        dq_ref[:, 0].reshape(many, LANES).astype(F32).T,
        dkv_ref[:, 0].reshape(many, LANES).astype(F32).T,
        dkv_ref[:, 1].reshape(many, LANES).astype(F32).T,
    ]
    weight = []
    for ref in (q_ref, k_ref, v_ref):
        turned = ref[...].astype(F32).T
        weight.append(jnp.where(odd, turned[HEAD_DIM:], turned[:HEAD_DIM]))
    weight = jnp.concatenate(weight, axis=0)
    product = None
    terms = []
    for item in range(items):
        unit, unused = center_scale(tri_ref[item].astype(F32))
        units[...] = unit.astype(BF)
        span = slice(item * HEAD_DIM, (item + 1) * HEAD_DIM)
        mine = jnp.concatenate([part[span] for part in grads], axis=0)
        outer = mm(mine.astype(BF), units[...])
        column = jnp.sum(mine, axis=1, keepdims=True)
        shift = mod_ref[item : item + 1, :width]
        scale = mod_ref[item : item + 1, width:]
        terms.append(jnp.sum(column * weight, axis=0, keepdims=True))
        terms.append(jnp.sum(outer * weight, axis=0, keepdims=True))
        term = outer * (1.0 + scale) + column * shift
        product = term if product is None else product + term
    product = product.T
    patch_rows = patch_ref.shape[1]
    grads = [dmem_ref[:, kind].reshape(patch_rows, LANES).astype(F32).T for kind in range(2)]
    memory = None
    for item in range(items):
        span = slice(item * HEAD_DIM, (item + 1) * HEAD_DIM)
        mine = jnp.concatenate([part[span] for part in grads], axis=0).astype(BF)
        term = mm(mine, patch_ref[item])
        memory = term if memory is None else memory + term
    memory = memory.T
    if not packed:
        out_ref, memory_ref, terms_ref = rest[:3]
        out_ref[...] = product.astype(BF)
        memory_ref[...] = memory.astype(BF)
        for item in range(items):
            terms_ref[item : item + 1, :width] = terms[2 * item]
            terms_ref[item : item + 1, width:] = terms[2 * item + 1]
        return
    ends_ref, out_ref, terms_ref, unused = rest
    devices = out_ref.shape[0]
    span = width // devices
    product = product.reshape(devices, span, 3 * HEAD_DIM).astype(BF)
    out_ref[:, :span] = memory.reshape(devices, span, LANES).astype(BF)
    out_ref[:, span : 2 * span] = product[:, :, :LANES]
    last = product[:, :, LANES:]
    at = 2 * span + span // 2
    out_ref[:, 2 * span : at] = jnp.concatenate(
        [last[:, : span // 2], last[:, span // 2 :]], axis=2
    )
    out_ref[:, at:] = ends_ref[...]
    lines = [
        term[:, k * LANES : (k + 1) * LANES] for term in terms for k in range(width // LANES)
    ]
    terms_ref[...] = jnp.concatenate(lines, axis=0).astype(BF)


def head_back(head, d_q, d_kv, d_mem, rows_all, patch_part, qkv_weight, modulation, ends):
    items, many, width = rows_all.shape
    blocks, _, own, _ = d_q.shape
    pairs = width // LANES
    product = jax.ShapeDtypeStruct((width, 3 * HEAD_DIM), BF)
    if ends is None:
        more = []
        shapes = [
            product,
            jax.ShapeDtypeStruct((width, LANES), BF),
            jax.ShapeDtypeStruct((items, 2 * width), F32),
        ]
    else:
        devices, tail, _ = ends.shape
        more = [ends]
        many_rows = 5 * width // devices // 2 + tail
        shapes = [
            jax.ShapeDtypeStruct((devices, many_rows, LANES), BF),
            jax.ShapeDtypeStruct((2 * items * pairs, LANES), BF),
        ]

    def whole_block(shape):
        return pl.BlockSpec(shape, lambda i, h: (0,) * len(shape))

    return pl.pallas_call(
        functools.partial(head_back_kernel, ends is not None),
        grid_spec=pltpu.PrefetchScalarGridSpec(
            num_scalar_prefetch=1,
            grid=(1,),
            in_specs=[
                pl.BlockSpec((blocks, 1, own, LANES), lambda i, h: (0, 0, 0, 0)),
                pl.BlockSpec((blocks, 2, own, LANES), lambda i, h: (0, 0, 0, 0)),
                whole_block(d_mem.shape),
                pl.BlockSpec((items, many, width), lambda i, h: (0, 0, 0)),
                whole_block(patch_part.shape),
                pl.BlockSpec((width, LANES), lambda i, h: (0, lax.div(h[0], 2))),
                pl.BlockSpec((width, LANES), lambda i, h: (0, pairs + lax.div(h[0], 2))),
                pl.BlockSpec((width, LANES), lambda i, h: (0, 2 * pairs + lax.div(h[0], 2))),
                whole_block((items, 2 * width)),
            ]
            + [whole_block(array.shape) for array in more],
            out_specs=[whole_block(shape.shape) for shape in shapes],
            scratch_shapes=[pltpu.VMEM((many, width), BF)],
        ),
        out_shape=shapes,
        compiler_params=pltpu.CompilerParams(vmem_limit_bytes=ROOM),
        cost_estimate=pl.CostEstimate(
            flops=6 * items * many * width * HEAD_DIM, bytes_accessed=5 << 20, transcendentals=0
        ),
        name="head_back",
    )(
        head,
        d_q,
        d_kv,
        d_mem,
        rows_all,
        patch_part,
        qkv_weight,
        qkv_weight,
        qkv_weight,
        modulation,
        *more,
    )


def by_heads_kernel(got_ref, out_ref):
    parts, heads, rows, _ = got_ref.shape
    width = heads * HEAD_DIM
    for pair in range(heads // 2):
        left = got_ref[0, 2 * pair].astype(F32)
        right = got_ref[0, 2 * pair + 1].astype(F32)
        for part in range(1, parts):
            left = left + got_ref[part, 2 * pair].astype(F32)
            right = right + got_ref[part, 2 * pair + 1].astype(F32)
        for kind in range(3):
            span = slice(kind * HEAD_DIM, (kind + 1) * HEAD_DIM)
            at = kind * width + pair * LANES
            out_ref[:, at : at + LANES] = jnp.concatenate([left[:, span], right[:, span]], axis=1)


def by_heads(got):
    parts, heads, rows, features = got.shape
    return pl.pallas_call(
        by_heads_kernel,
        grid=(1,),
        in_specs=[whole(got.shape)],
        out_specs=whole((rows, heads * features)),
        out_shape=jax.ShapeDtypeStruct((rows, heads * features), F32),
        compiler_params=pltpu.CompilerParams(vmem_limit_bytes=ROOM),
        name="by_heads",
    )(got)


def unpack_kernel(tail, got_ref, mem_ref, qkv_ref, mod_ref, ends_ref):
    span = qkv_ref.shape[0]
    width = HEADS * HEAD_DIM
    at = 2 * span + span // 2

    def columns(head):
        full = got_ref[head, :at].astype(F32)
        last = full[2 * span :]
        last = jnp.concatenate([last[:, :HEAD_DIM], last[:, HEAD_DIM:]], axis=0)
        first, second = full[:span], full[span : 2 * span]
        return (
            first[:, :HEAD_DIM],
            first[:, HEAD_DIM:],
            second[:, :HEAD_DIM],
            second[:, HEAD_DIM:],
            last,
        )

    for pair in range(HEADS // 2):
        both = [
            jnp.concatenate(sides, axis=1)
            for sides in zip(columns(2 * pair), columns(2 * pair + 1))
        ]
        for kind in range(2):
            start = kind * width + pair * LANES
            mem_ref[:, start : start + LANES] = both[kind]
        for kind in range(3):
            start = kind * width + pair * LANES
            qkv_ref[:, start : start + LANES] = both[2 + kind]
    total = got_ref[0, at:].astype(F32)
    for head in range(1, HEADS):
        total = total + got_ref[head, at:].astype(F32)
    ends_ref[...] = total[:tail]
    mod_ref[...] = total[tail:]


def unpack(got, span, tail):
    _, many, _ = got.shape
    shapes = [
        (span, 2 * HEADS * HEAD_DIM),
        (span, 3 * HEADS * HEAD_DIM),
        (many - tail - 2 * span - span // 2, LANES),
        (tail, LANES),
    ]
    return pl.pallas_call(
        functools.partial(unpack_kernel, tail),
        grid=(1,),
        in_specs=[whole(got.shape)],
        out_specs=[whole(shape) for shape in shapes],
        out_shape=[jax.ShapeDtypeStruct(shape, F32) for shape in shapes],
        compiler_params=pltpu.CompilerParams(vmem_limit_bytes=ROOM),
        name="unpack",
    )(got)


def gather_lanes(block, starts, span):
    out = []
    lane = lax.broadcasted_iota(jnp.int32, (block.shape[0], LANES), 1)
    for at in range(0, len(starts) * span, LANES):
        merged = None
        for to in range(0, LANES, min(span, LANES)):
            start = starts[(at + to) // span] + (at + to) % span
            base = start // LANES * LANES
            part = block[:, base : base + LANES]
            shift = (to - (start - base)) % LANES
            if shift:
                part = pltpu.roll(part, shift, 1)
            if merged is None:
                merged = part
            else:
                merged = jnp.where((lane >= to) & (lane < to + span), part, merged)
        out.append(merged)
    return jnp.concatenate(out, axis=1)


def starts_y(features, devices, quarter):
    span = features // devices
    return [(group * 4 + quarter) * span for group in range(devices // 4)]


def starts_x(features, devices, half, low):
    span = features // devices
    many = devices // 2
    return [
        (half * many + rest * 4 + y * 2 + low) * span
        for y in range(2)
        for rest in range(many // 4)
    ]


def mlp_kernel(
    steps,
    devices,
    normed_ref,
    dh_ref,
    up_ref,
    later_ref,
    c_ref,
    gain,
    out_w,
    hidden_ref,
    pre_ref,
    up_piece_ref,
    down_piece_ref,
    d_later_ref,
    low_ref,
    d_crossed_ref,
    sums_ref,
    total,
):
    step = pl.program_id(0)

    @pl.when(step == 0)
    def _():
        values = normed_ref[...].astype(F32)
        for quarter in range(4):
            starts = starts_y(values.shape[1], devices, quarter)
            span = values.shape[1] // devices
            up_piece_ref[quarter] = gather_lanes(values, starts, span).astype(BF)

    pre = mm(normed_ref[...], up_ref[...])
    square = pre * pre
    slope = (2.0 / 3.141592653589793) ** 0.5
    turn = jnp.tanh(slope * (pre + 0.044715 * (pre * square)))
    hidden = 0.5 * pre * (1.0 + turn)
    hidden_ref[...] = hidden.astype(BF)
    part = hidden.shape[1]
    span = part * steps // devices
    half = lax.div(step, steps // 2)
    for low in range(2):
        for y in range(2):
            starts = [(rest * 4 + y * 2 + low) * span for rest in range(part // (4 * span))]
            at = y * (part * steps // 8) + lax.rem(step, steps // 2) * (part // 4)
            at = pl.ds(pl.multiple_of(at, LANES), part // 4)
            down_piece_ref[2 * half + low, :, at] = gather_lanes(hidden, starts, span).astype(BF)
    change = 0.5 * (1.0 + turn) + 0.5 * pre * (1.0 - turn * turn) * (
        slope * (1.0 + 3.0 * 0.044715 * square)
    )
    d_pre = (dh_ref[...] * change).astype(BF)
    pre_ref[...] = d_pre
    added = mm_nt(d_pre, up_ref[...])

    @pl.when(step == 0)
    def _():
        total[...] = added

    @pl.when(step > 0)
    def _():
        total[...] += added

    @pl.when(step == steps - 1)
    def _():
        d_normed = total[...]
        unit, rstd = center_scale(later_ref[...])
        sums_ref[0:1] = jnp.sum(d_normed * unit, axis=0, keepdims=True)
        sums_ref[1:2] = jnp.sum(d_normed, axis=0, keepdims=True)
        d_later = c_ref[...].astype(F32) + norm_back(unit, rstd, d_normed * gain[...])
        d_later_ref[...] = d_later
        low = d_later.astype(BF)
        low_ref[...] = low
        d_crossed_ref[...] = mm_nt(low, out_w[...]).astype(BF)


def mlp(devices, normed, d_hidden, up_weight, later, grad_out, gain, cross_out):
    rows, width = normed.shape
    hidden_width = up_weight.shape[1]
    part = min(1024, hidden_width)
    steps = hidden_width // part
    low = jax.ShapeDtypeStruct((rows, width), BF)
    return pl.pallas_call(
        functools.partial(mlp_kernel, steps, devices),
        grid=(steps,),
        in_specs=[
            whole((rows, width)),
            pl.BlockSpec((rows, part), lambda i: (0, i)),
            pl.BlockSpec((width, part), lambda i: (0, i)),
            whole((rows, width)),
            whole((rows, width)),
            whole((1, width)),
            whole((width, width)),
        ],
        out_specs=[
            pl.BlockSpec((rows, part), lambda i: (0, i)),
            pl.BlockSpec((rows, part), lambda i: (0, i)),
            whole((4, rows, width // 4)),
            whole((4, rows, hidden_width // 4)),
            whole((rows, width)),
            whole((rows, width)),
            whole((rows, width)),
            whole((2, width)),
        ],
        out_shape=[
            jax.ShapeDtypeStruct((rows, hidden_width), BF),
            jax.ShapeDtypeStruct((rows, hidden_width), BF),
            jax.ShapeDtypeStruct((4, rows, width // 4), BF),
            jax.ShapeDtypeStruct((4, rows, hidden_width // 4), BF),
            jax.ShapeDtypeStruct((rows, width), F32),
            low,
            low,
            jax.ShapeDtypeStruct((2, width), F32),
        ],
        scratch_shapes=[pltpu.VMEM((rows, width), F32)],
        compiler_params=pltpu.CompilerParams(vmem_limit_bytes=ROOM),
        cost_estimate=pl.CostEstimate(
            flops=4 * rows * width * hidden_width,
            bytes_accessed=12 << 20,
            transcendentals=rows * hidden_width,
        ),
        name="mlp",
    )(normed, d_hidden, up_weight, later, grad_out, gain[None], cross_out)


def pieces_kernel(devices, *refs):
    out_ref = refs[-1]
    for k, ref in enumerate(refs[:-1]):
        values = ref[...].astype(F32)
        span = values.shape[1] // devices
        for half in range(2):
            for low in range(2):
                starts = starts_x(values.shape[1], devices, half, low)
                out_ref[2 * half + low, k] = gather_lanes(values, starts, span).astype(BF)


def pieces(devices, *arrays):
    rows, width = arrays[0].shape
    return pl.pallas_call(
        functools.partial(pieces_kernel, devices),
        grid=(1,),
        in_specs=[whole((rows, width))] * len(arrays),
        out_specs=whole((4, len(arrays), rows, width // 4)),
        out_shape=jax.ShapeDtypeStruct((4, len(arrays), rows, width // 4), BF),
        compiler_params=pltpu.CompilerParams(vmem_limit_bytes=ROOM),
        name="pieces",
    )(*arrays)


def product_kernel(half_ref, *refs):
    x_refs, y_refs, (keep_ref, send_ref, left) = refs[:4], refs[4:8], refs[8:]

    @pl.when(pl.program_id(1) == 0)
    def _():
        left[...] = jnp.concatenate([ref[0] for ref in x_refs], axis=0).T

    right = jnp.concatenate([ref[0] for ref in y_refs], axis=0)
    quads, _, span, many = keep_ref.shape
    both = mm(left[...], right).reshape(2, quads, 1, span, many)

    @pl.when(half_ref[0] == 0)
    def _():
        keep_ref[...] = both[0].astype(BF)
        send_ref[...] = both[1].astype(BF)

    @pl.when(half_ref[0] == 1)
    def _():
        keep_ref[...] = both[1].astype(BF)
        send_ref[...] = both[0].astype(BF)


def product(half, quads, left, right):
    entries, rows, wide = left[0].shape
    columns = right[0].shape[2]
    span = wide // (2 * quads)
    part = min(columns, 512)
    shape = jax.ShapeDtypeStruct((quads, entries, span, columns), BF)
    spec = pl.BlockSpec((quads, 1, span, part), lambda e, i: (0, e, 0, i))
    return pl.pallas_call(
        product_kernel,
        grid=(entries, columns // part),
        in_specs=[IN_SMEM]
        + [pl.BlockSpec((1, rows, wide), lambda e, i: (e, 0, 0))] * 4
        + [pl.BlockSpec((1, rows, part), lambda e, i: (e, 0, i))] * 4,
        out_specs=[spec, spec],
        out_shape=[shape, shape],
        scratch_shapes=[pltpu.VMEM((wide, 4 * rows), BF)],
        compiler_params=pltpu.CompilerParams(vmem_limit_bytes=ROOM),
        cost_estimate=pl.CostEstimate(
            flops=8 * entries * rows * wide * columns, bytes_accessed=8 << 20, transcendentals=0
        ),
        name="product",
    )(half.reshape(1).astype(jnp.int32), *left, *right)


def xor_blk(values, bit, count):
    return lax.ppermute(values, "blk", [(i, i ^ bit) for i in range(count)])


def swap_batch(values):
    return lax.ppermute(values, "batch", [(0, 1), (1, 0)])


def after(values, *first):
    return lax.optimization_barrier((values, first))[0]


def take(values, index, axis):
    return lax.dynamic_index_in_dim(values, index, axis, keepdims=False)


def local(
    count_blk,
    triplane,
    patches,
    cotangent,
    camera_index,
    triplane_count,
    patch_count,
    camera_table,
    mod_weight,
    qkv_weight,
    self_out,
    gain_mid,
    bias_mid,
    cross_query,
    cross_memory,
    cross_out,
    gain_last,
    bias_last,
    up_weight,
    down_weight,
):
    items, own, width = triplane.shape
    own_patches = patches.shape[1]
    rows = items * own
    spare = count_blk // HEADS
    quads = count_blk // 4
    devices = 2 * count_blk
    row_groups = (
        None
        if spare == 1
        else [[part * HEADS + head for head in range(HEADS)] for part in range(spare)]
    )
    head_groups = [[part * HEADS + head for part in range(spare)] for head in range(HEADS)]
    batch_at = lax.axis_index("batch")
    blk_at = lax.axis_index("blk")
    head_at = lax.rem(blk_at, HEADS)
    place = batch_at * count_blk + blk_at

    def to_heads(values):
        return lax.all_to_all(values, "blk", 0, 0, axis_index_groups=row_groups, tiled=True)

    def swap_corner(values):
        return lax.ppermute(
            values,
            BOTH,
            [
                (b * count_blk + j, (1 - b) * count_blk + (j ^ 1))
                for b in range(2)
                for j in range(count_blk)
            ],
        )

    def quad_y(values):
        far = xor_blk(values, 2, count_blk)
        return [values, xor_blk(values, 1, count_blk), far, xor_blk(far, 1, count_blk)]

    def quad_x(values):
        far = swap_batch(values)
        return [values, xor_blk(values, 1, count_blk), far, xor_blk(far, 1, count_blk)]

    def exchange_y(cut):
        low = jnp.bitwise_and(blk_at, 3)
        got = [take(cut, low, 0)]
        for bit in (1, 2, 3):
            got.append(xor_blk(take(cut, jnp.bitwise_xor(low, bit), 0), bit, count_blk))
        return got

    def exchange_x(cut):
        low = jnp.bitwise_and(blk_at, 1)
        return [
            take(cut, 2 * batch_at + low, 0),
            xor_blk(take(cut, 2 * batch_at + 1 - low, 0), 1, count_blk),
            swap_batch(take(cut, 2 * (1 - batch_at) + low, 0)),
            swap_corner(take(cut, 2 * (1 - batch_at) + 1 - low, 0)),
        ]

    def half_x(values):
        given = swap_batch(take(values, 1 - batch_at, 0))
        return (take(values, batch_at, 0).astype(F32) + given.astype(F32)).astype(BF)

    def rest_sum(keep, given):
        many = quads
        bit = 4
        while many > 1:
            low = jnp.bitwise_and(lax.div(blk_at, bit), 1)
            shape = (many // 2, 2) + keep.shape[1:]
            keep, given = keep.reshape(shape), given.reshape(shape)

            def part(index):
                total = take(keep, index, 1).astype(F32) + take(given, index, 1).astype(F32)
                return total.astype(BF)

            keep, given = part(low), xor_blk(part(1 - low), bit, count_blk)
            many //= 2
            bit *= 2
        return (keep.astype(F32) + given.astype(F32))[0]

    views = camera_index.shape[1]
    table_rows = jnp.arange(camera_table.shape[0], dtype=jnp.int32)

    def pick_of(cams):
        return jnp.sum((cams[:, :, None] == table_rows[None, None, :]).astype(F32), axis=1)

    def code_of(pick):
        return (mm(pick.astype(BF), camera_table) / views).astype(BF)

    modulation = mm(code_of(pick_of(camera_index)), mod_weight)
    sent = project(triplane, modulation, qkv_weight)
    qkv = to_heads(sent)

    patches_all = lax.all_gather(patches, "blk", axis=1, tiled=True)
    bit_y = jnp.bitwise_and(lax.div(blk_at, 2), 1)
    many_patches = patches_all.shape[1]
    memory = (
        mm(patches_all.reshape(items * many_patches, width), cross_memory)
        .astype(BF)
        .reshape(items, many_patches, 2 * width)
    )
    grad_out = cotangent.reshape(rows, width)
    d_hidden = mm_nt(grad_out, down_weight)
    grad_quad = quad_x(lax.optimization_barrier((grad_out, sent))[0])

    qkv, d_hidden = lax.optimization_barrier((qkv, d_hidden))
    if spare == 1:
        kv, kv_first = qkv, 1
    else:
        kv = lax.all_gather(qkv[:, 1:], "blk", axis=0, axis_index_groups=head_groups, tiled=True)
        kv_first = 0
    attended_heads, self_lse = self_forward(triplane_count, qkv, kv, kv_first)
    attended_got = to_heads(attended_heads)
    kept = lax.optimization_barrier((triplane, attended_heads))[0]
    rows_all = lax.all_gather(kept, "blk", axis=1, axis_index_groups=row_groups, tiled=True)

    attended_got, memory, grad_quad = lax.optimization_barrier(
        (attended_got, memory, grad_quad)
    )
    attended_low, middle, normed_mid, cross_q = middle_part(
        attended_got, triplane.reshape(rows, width), self_out, gain_mid, bias_mid, cross_query
    )
    cross_q = cross_q.reshape(items, own, width)
    crossed, cross_lse, later, normed_last = cross_forward(
        patch_count, cross_q, memory, middle, cross_out, gain_last, bias_last
    )
    hidden, d_pre, last_pieces, hidden_pieces, d_later, d_later_low, d_crossed, sums_last = mlp(
        devices, normed_last, d_hidden, up_weight, later, grad_out, gain_last, cross_out
    )
    pre_far = xor_blk(d_pre, 2, count_blk)
    pre_near = xor_blk(d_pre, 1, count_blk)
    last_pieces = exchange_y(last_pieces)
    hidden_pieces = exchange_x(hidden_pieces)

    d_cross_q = cross_backward(
        patch_count, cross_q, memory, d_crossed.reshape(items, own, width), cross_lse
    )
    d_cross_low = d_cross_q.reshape(rows, width)
    d_middle, d_middle_low, back_heads, sums_mid = middle_back(
        own,
        d_cross_low,
        cross_query,
        middle,
        gain_mid,
        d_later,
        self_out,
        cross_q.reshape(rows, width),
        d_crossed,
    )
    pre_quad = [d_pre, pre_near, pre_far, xor_blk(pre_far, 1, count_blk)]
    back_heads = to_heads(back_heads)

    up_keep, up_send = product(
        batch_at, quads, [p[None] for p in last_pieces], [p[None] for p in pre_quad]
    )
    down_keep, down_send = product(
        bit_y, quads, [p[None] for p in hidden_pieces], [p[None] for p in grad_quad]
    )
    up_given = swap_batch(up_send)
    down_given = xor_blk(down_send, 2, count_blk)
    lefts, rights = after(
        (
            (crossed.reshape(rows, width), normed_mid, attended_low),
            (d_later_low, d_cross_low, d_middle_low),
        ),
        up_keep,
        down_keep,
    )
    squares = exchange_x(pieces(devices, *lefts))
    rights = jnp.stack(rights)
    rights_far = swap_batch(rights)
    rights_near = xor_blk(rights, 1, count_blk)

    back_heads = after(back_heads, up_keep, down_keep)
    d_q, d_kv = self_backward(
        triplane_count, qkv, kv, kv_first, back_heads, self_lse, spare == 1
    )
    head = head_at.reshape(1).astype(jnp.int32)
    d_mem = memory_back(head, patch_count, back_heads, memory, own_patches, spare == 1)
    if spare > 1:
        d_kv, d_mem = [
            lax.psum_scatter(
                values, "blk", scatter_dimension=0, axis_index_groups=head_groups, tiled=True
            ).astype(BF)
            for values in (d_kv, d_mem)
        ]
    d_got = to_heads(
        jnp.concatenate(
            [values.reshape(HEADS, -1, LANES) for values in (d_q, d_kv, d_mem)], axis=1
        )
    )

    mod_rows = width // devices
    ends = jnp.concatenate([sums_mid, sums_last], axis=0)
    ends = jnp.transpose(ends.reshape(4, devices, -1), (1, 0, 2)).reshape(devices, 1, -1)
    packed = mod_rows % 32 == 0 and ends.shape[2] == LANES and spare == 1
    if packed:
        high = ends.astype(BF)
        low = (ends - high.astype(F32)).astype(BF)
        ends = jnp.concatenate([high, low, jnp.zeros((devices, 14, LANES), BF)], axis=1)
    part_patches = HEADS * own_patches
    first_patch = lax.div(blk_at, HEADS) * part_patches
    payload = head_back(
        head,
        d_q,
        d_kv,
        d_mem,
        rows_all,
        lax.dynamic_slice_in_dim(patches_all, first_patch, part_patches, 1)
        if spare > 1
        else patches_all,
        qkv_weight,
        modulation,
        ends if packed else None,
    )
    later = after(later, payload)

    squares_quad = [rights, rights_near, rights_far, xor_blk(rights_far, 1, count_blk)]
    squares_keep, squares_send = product(bit_y, quads, squares, squares_quad)
    squares_given = xor_blk(squares_send, 2, count_blk)

    d_memory_rows = d_got[:, 3 * own :].reshape(HEADS, 2, own_patches, items, HEAD_DIM)
    d_memory_rows = jnp.transpose(d_memory_rows, (3, 2, 1, 0, 4)).reshape(-1, 2 * width)
    d_patches = mm_nt(d_memory_rows, cross_memory)

    def spread(values):
        span = values.shape[0] // devices
        return lax.all_to_all(
            values.reshape(devices, span, values.shape[1]), BOTH, 0, 0, tiled=True
        )

    if packed:
        own_part, terms = payload
        own_part = own_part.reshape((2, HEADS) + own_part.shape[1:])
        own_part = half_x(own_part)
        terms = jnp.broadcast_to(terms, (HEADS,) + terms.shape)
        got = to_heads(jnp.concatenate([own_part, terms], axis=1))
        g_cross_mem, g_qkv, d_modulation, ends = unpack(got, mod_rows, 16)
        ends = (ends[0] + ends[1]).reshape(4, -1)
        others = swap_batch(d_modulation)
        d_modulation = jnp.where(
            batch_at == 0,
            jnp.concatenate([d_modulation, others], axis=0),
            jnp.concatenate([others, d_modulation], axis=0),
        )
    else:
        qkv_product, memory_product, terms = payload
        g_qkv = by_heads(spread(qkv_product).reshape(2 * spare, HEADS, mod_rows, 3 * HEAD_DIM))
        terms = terms.reshape(1, -1, ends.shape[2])
        terms = jnp.broadcast_to(terms, (devices,) + terms.shape[1:])
        small = lax.all_to_all(jnp.concatenate([terms, ends], axis=1), BOTH, 0, 0, tiled=True)
        ends = jnp.sum(small[:, -1], axis=0).reshape(4, -1)
        d_modulation = jnp.sum(small[:, :-1].reshape(2, count_blk, -1), axis=1)
        memory_got = spread(memory_product).astype(F32)
        memory_got = memory_got.reshape(2 * spare, HEADS, mod_rows, 2, HEAD_DIM)
        memory_got = jnp.transpose(jnp.sum(memory_got, axis=0), (1, 2, 0, 3))
        g_cross_mem = memory_got.reshape(mod_rows, 2 * width)
    d_modulation = d_modulation.reshape(2 * items, 2 * width)
    own_cams = lax.optimization_barrier((camera_index, modulation))[0]
    others = swap_batch(own_cams)
    cams = jnp.where(
        batch_at == 0,
        jnp.concatenate([own_cams, others], axis=0),
        jnp.concatenate([others, own_cams], axis=0),
    )
    pick = pick_of(cams)
    code_low = code_of(pick)
    code_rows = lax.dynamic_slice_in_dim(code_low, place * mod_rows, mod_rows, 1).astype(F32)
    g_mod = jnp.sum(code_rows[:, :, None] * d_modulation[:, None, :], axis=0)
    d_code = mm_nt(d_modulation.astype(BF), mod_weight)
    cam_rows = camera_table.shape[0] // devices
    pick_rows = lax.dynamic_slice_in_dim(pick, place * cam_rows, cam_rows, 1)
    g_table = jnp.sum(pick_rows[:, :, None] * d_code[:, None, :], axis=0) / views

    d_triplane = first_back(
        d_got, qkv_weight, triplane, modulation, d_middle.reshape(items, own, width)
    )
    g_up = rest_sum(up_keep, up_given)[0]
    g_down = rest_sum(down_keep, down_given)[0]
    g_squares = rest_sum(squares_keep, squares_given)
    result = later + mm(hidden, down_weight)
    return (
        result.reshape(items, own, width),
        d_triplane,
        d_patches.reshape(items, own_patches, width),
        g_table,
        g_mod,
        g_qkv,
        g_squares[2],
        ends[0],
        ends[1],
        g_squares[1],
        g_cross_mem,
        g_squares[0],
        ends[2],
        ends[3],
        g_up,
        g_down,
    )


def solution(mesh):
    rows = P("batch", "blk", None)
    split = P(BOTH, None)
    line = P(BOTH)
    whole = P()
    return jax.shard_map(
        functools.partial(local, mesh.shape["blk"]),
        mesh=mesh,
        in_specs=(rows, rows, rows, P("batch", None), P("batch"), P("batch")) + (whole,) * 13,
        out_specs=(
            rows,
            rows,
            rows,
            split,
            split,
            split,
            split,
            line,
            line,
            split,
            split,
            split,
            line,
            line,
            split,
            split,
        ),
        check_vma=False,
    )
```

```python
import functools

import jax
import jax.numpy as jnp
from jax import lax
from jax.experimental import pallas as pl
from jax.experimental.pallas import tpu as pltpu
from jax.sharding import PartitionSpec as P

HEADS = 16
HEAD_DIM = 64
LANES = 128
PAIRS = HEADS * HEAD_DIM // LANES
BF = jnp.bfloat16
F32 = jnp.float32
BOTH = ("batch", "blk")
TINY = -1e30
GROUP = 4
WIDE = GROUP * HEAD_DIM
ANYWHERE = pl.BlockSpec(memory_space=pl.ANY)
ROOM = 60 << 20
IN_SMEM = pl.BlockSpec(memory_space=pltpu.SMEM)


def whole(shape):
    return pl.BlockSpec(shape, lambda *at: (0,) * len(shape))


def mm(a, b):
    return jnp.dot(a, b, preferred_element_type=F32)


def mm_nt(a, b):
    return lax.dot_general(a, b, (((1,), (1,)), ((), ())), preferred_element_type=F32)


def mm_tn(a, b):
    return lax.dot_general(a, b, (((0,), (0,)), ((), ())), preferred_element_type=F32)


def center_scale(values):
    center = values - jnp.mean(values, axis=-1, keepdims=True)
    rstd = lax.rsqrt(jnp.mean(center * center, axis=-1, keepdims=True) + 1e-05)
    return center * rstd, rstd


def norm_back(unit, rstd, grad):
    return rstd * (
        grad
        - jnp.mean(grad, axis=-1, keepdims=True)
        - unit * jnp.mean(grad * unit, axis=-1, keepdims=True)
    )


def self_forward_kernel(count_ref, q_ref, k_ref, v_ref, out_ref, lse_ref):
    queries = q_ref[...].reshape(-1, LANES) * BF(HEAD_DIM**-0.5)
    keys = k_ref[...].reshape(-1, LANES)
    values_t = v_ref[...].reshape(-1, LANES).T
    lane = lax.broadcasted_iota(jnp.int32, queries.shape, 1) // HEAD_DIM
    row = lax.broadcasted_iota(jnp.int32, (keys.shape[0], queries.shape[0]), 0)
    parts = []
    for item in range(2):
        mine = jnp.where(lane == item, queries, BF(0))
        scores = jnp.where(row < count_ref[item], mm_nt(keys, mine), TINY)
        top = jnp.max(scores, axis=0, keepdims=True)
        weights = jnp.exp(scores - top)
        total = jnp.sum(weights, axis=0, keepdims=True)
        span = slice(item * HEAD_DIM, (item + 1) * HEAD_DIM)
        parts.append(mm(values_t[span], weights.astype(BF)) / total)
        lse_ref[item : item + 1, :] = top + jnp.log(total)
    out = jnp.concatenate(parts, axis=0).T
    out_ref[...] = out.astype(BF).reshape(out_ref.shape)


def self_backward_kernel(
    steps, count_ref, q_ref, k_ref, v_ref, do_ref, lse_ref, *rest
):
    dq_ref, dkv_ref, dk_acc, dv_acc = rest[-4:]
    step = pl.program_id(0)
    queries = q_ref[...].reshape(-1, LANES) * BF(HEAD_DIM**-0.5)
    keys = k_ref[...].reshape(-1, LANES)
    values = v_ref[...].reshape(-1, LANES)
    keys_t = keys.T
    grads = do_ref[...].reshape(-1, LANES)
    lane = lax.broadcasted_iota(jnp.int32, queries.shape, 1) // HEAD_DIM
    row = lax.broadcasted_iota(jnp.int32, (keys.shape[0], queries.shape[0]), 0)
    parts = []
    d_keys = None
    for item in range(2):
        mine = jnp.where(lane == item, queries, BF(0))
        d_mine = jnp.where(lane == item, grads, BF(0))
        scores = mm_nt(keys, mine)
        probs = jnp.where(
            row < count_ref[item], jnp.exp(scores - lse_ref[item : item + 1, :]), 0.0
        )
        d_probs = mm_nt(values, d_mine)
        delta = jnp.sum(probs * d_probs, axis=0, keepdims=True)
        d_scores = (probs * (d_probs - delta)).astype(BF)
        new_v = mm(probs.astype(BF), d_mine)
        new_k = mm(d_scores, mine)
        d_values = new_v if d_keys is None else d_values + new_v
        d_keys = new_k if d_keys is None else d_keys + new_k
        span = slice(item * HEAD_DIM, (item + 1) * HEAD_DIM)
        parts.append(mm(keys_t[span], d_scores) * HEAD_DIM**-0.5)
    d_q = jnp.concatenate(parts, axis=0).T
    dq_ref[...] = d_q.astype(BF).reshape(dq_ref.shape)

    @pl.when(step == 0)
    def _():
        dk_acc[...] = d_keys
        dv_acc[...] = d_values

    @pl.when(step > 0)
    def _():
        dk_acc[...] += d_keys
        dv_acc[...] += d_values

    @pl.when(step == steps - 1)
    def _():
        shape = (dkv_ref.shape[0], 1) + dkv_ref.shape[2:]
        dkv_ref[:, 0:1] = dk_acc[...].astype(dkv_ref.dtype).reshape(shape)
        dkv_ref[:, 1:2] = dv_acc[...].astype(dkv_ref.dtype).reshape(shape)


def q_steps(blocks):
    return 2 if blocks % 2 == 0 else 1


def self_specs(q_arr, kv_arr, first):
    blocks, _, rows, _ = q_arr.shape
    steps = q_steps(blocks)
    part = blocks // steps
    many = kv_arr.shape[0]
    return steps, part, rows, many, [
        pl.BlockSpec(memory_space=pltpu.SMEM),
        pl.BlockSpec((part, 1, rows, LANES), lambda i: (i, 0, 0, 0)),
        pl.BlockSpec((many, 1, rows, LANES), lambda i: (0, first, 0, 0)),
        pl.BlockSpec((many, 1, rows, LANES), lambda i: (0, first + 1, 0, 0)),
    ]


def self_forward(counts, q_arr, kv_arr, first):
    steps, part, rows, many, specs = self_specs(q_arr, kv_arr, first)
    blocks = q_arr.shape[0]
    pairs = blocks * rows * many * rows * 2
    return pl.pallas_call(
        self_forward_kernel,
        grid=(steps,),
        in_specs=specs,
        out_specs=[
            pl.BlockSpec((part, rows, LANES), lambda i: (i, 0, 0)),
            pl.BlockSpec((2, part * rows), lambda i: (0, i)),
        ],
        out_shape=[
            jax.ShapeDtypeStruct((blocks, rows, LANES), BF),
            jax.ShapeDtypeStruct((2, blocks * rows), F32),
        ],
        compiler_params=pltpu.CompilerParams(vmem_limit_bytes=ROOM),
        cost_estimate=pl.CostEstimate(
            flops=pairs * 4 * LANES, bytes_accessed=1 << 20, transcendentals=pairs
        ),
        name="self_forward",
    )(counts, q_arr, kv_arr, kv_arr)


def self_backward(counts, q_arr, kv_arr, first, d_out, lse, low):
    steps, part, rows, many, specs = self_specs(q_arr, kv_arr, first)
    blocks = q_arr.shape[0]
    pairs = blocks * rows * many * rows * 2
    return pl.pallas_call(
        functools.partial(self_backward_kernel, steps),
        grid=(steps,),
        in_specs=specs
        + [
            pl.BlockSpec((part, 1, rows, LANES), lambda i: (i, 0, 0, 0)),
            pl.BlockSpec((2, part * rows), lambda i: (0, i)),
        ],
        out_specs=[
            pl.BlockSpec((part, 1, rows, LANES), lambda i: (i, 0, 0, 0)),
            pl.BlockSpec((many, 2, rows, LANES), lambda i: (0, 0, 0, 0)),
        ],
        out_shape=[
            jax.ShapeDtypeStruct((blocks, 1, rows, LANES), BF),
            jax.ShapeDtypeStruct((many, 2, rows, LANES), BF if low else F32),
        ],
        scratch_shapes=[
            pltpu.VMEM((many * rows, LANES), F32),
            pltpu.VMEM((many * rows, LANES), F32),
        ],
        compiler_params=pltpu.CompilerParams(vmem_limit_bytes=ROOM),
        cost_estimate=pl.CostEstimate(
            flops=pairs * 10 * LANES, bytes_accessed=2 << 20, transcendentals=pairs
        ),
        name="self_backward",
    )(counts, q_arr, kv_arr, kv_arr, d_out, lse)


def stack_heads(block, lane):
    zero = jnp.zeros((), block.dtype)
    return jnp.concatenate(
        [jnp.where(lane == head, block, zero) for head in range(GROUP)], axis=0
    )


def merge_heads(block, lane):
    rows = block.shape[0] // GROUP
    out = block[:rows]
    for head in range(1, GROUP):
        out = jnp.where(lane == head, block[head * rows : (head + 1) * rows], out)
    return out


def cross_forward_kernel(
    count_ref,
    q_ref,
    mem_ref,
    mid_ref,
    gain,
    bias,
    out_hbm,
    out_ref,
    lse_ref,
    later_ref,
    normed_ref,
    out_w,
    sem,
):
    fetch = pltpu.make_async_copy(out_hbm, out_w, sem)
    fetch.start()
    items, rows, width = q_ref.shape
    many = mem_ref.shape[1]
    lane = lax.broadcasted_iota(jnp.int32, (rows, WIDE), 1) // HEAD_DIM
    row = lax.broadcasted_iota(jnp.int32, (many, GROUP * rows), 0)

    def body(group, carry):
        span = pl.ds(pl.multiple_of(group * WIDE, WIDE), WIDE)
        over = pl.ds(pl.multiple_of(width + group * WIDE, WIDE), WIDE)
        for item in range(items):
            queries = stack_heads(q_ref[item, :, span] * BF(HEAD_DIM**-0.5), lane)
            scores = mm_nt(mem_ref[item, :, span], queries)
            scores = jnp.where(row < count_ref[item], scores, TINY)
            top = jnp.max(scores, axis=0, keepdims=True)
            weights = jnp.exp(scores - top)
            total = jnp.sum(weights, axis=0, keepdims=True)
            out = mm(mem_ref[item, :, over].T, weights.astype(BF)) / total
            out_ref[item, :, span] = merge_heads(out.T, lane).astype(BF)
            lse_ref[item, pl.ds(group, 1), : GROUP * rows] = top + jnp.log(total)
        return carry

    lax.fori_loop(0, width // WIDE, body, 0, unroll=2)
    fetch.wait()
    later = mid_ref[...] + mm(out_ref[...].reshape(items * rows, width), out_w[...])
    later_ref[...] = later
    unit, unused = center_scale(later)
    normed_ref[...] = (unit * gain[...] + bias[...]).astype(BF)


def cross_backward_kernel(count_ref, q_ref, mem_ref, do_ref, lse_ref, dq_ref):
    items, rows, width = q_ref.shape
    many = mem_ref.shape[1]
    lane = lax.broadcasted_iota(jnp.int32, (rows, WIDE), 1) // HEAD_DIM
    row = lax.broadcasted_iota(jnp.int32, (many, GROUP * rows), 0)

    def body(group, carry):
        span = pl.ds(pl.multiple_of(group * WIDE, WIDE), WIDE)
        over = pl.ds(pl.multiple_of(width + group * WIDE, WIDE), WIDE)
        for item in range(items):
            queries = stack_heads(q_ref[item, :, span] * BF(HEAD_DIM**-0.5), lane)
            grads = stack_heads(do_ref[item, :, span], lane)
            keys = mem_ref[item, :, span]
            scores = mm_nt(keys, queries)
            lse = lse_ref[item, pl.ds(group, 1), : GROUP * rows]
            probs = jnp.where(row < count_ref[item], jnp.exp(scores - lse), 0.0)
            d_probs = mm_nt(mem_ref[item, :, over], grads)
            delta = jnp.sum(probs * d_probs, axis=0, keepdims=True)
            d_scores = (probs * (d_probs - delta)).astype(BF)
            d_q = mm(keys.T, d_scores) * HEAD_DIM**-0.5
            dq_ref[item, :, span] = merge_heads(d_q.T, lane).astype(BF)
        return carry

    lax.fori_loop(0, width // WIDE, body, 0, unroll=2)


def cross_forward(counts, cross_q, memory, middle, cross_out, gain, bias):
    items, rows, width = cross_q.shape
    many = memory.shape[1]
    pairs = items * rows * HEADS * many
    return pl.pallas_call(
        cross_forward_kernel,
        grid=(1,),
        in_specs=[IN_SMEM]
        + [whole(x.shape) for x in (cross_q, memory, middle)]
        + [whole((1, width))] * 2
        + [ANYWHERE],
        out_specs=[
            whole((items, rows, width)),
            whole((items, width // WIDE, WIDE)),
            whole((items * rows, width)),
            whole((items * rows, width)),
        ],
        out_shape=[
            jax.ShapeDtypeStruct((items, rows, width), BF),
            jax.ShapeDtypeStruct((items, width // WIDE, WIDE), F32),
            jax.ShapeDtypeStruct((items * rows, width), F32),
            jax.ShapeDtypeStruct((items * rows, width), BF),
        ],
        scratch_shapes=[pltpu.VMEM(cross_out.shape, BF), pltpu.SemaphoreType.DMA],
        compiler_params=pltpu.CompilerParams(vmem_limit_bytes=ROOM),
        cost_estimate=pl.CostEstimate(
            flops=pairs * 4 * WIDE, bytes_accessed=3 << 20, transcendentals=pairs
        ),
        name="cross_forward",
    )(counts, cross_q, memory, middle, gain[None], bias[None], cross_out)


def cross_backward(counts, cross_q, memory, d_out, lse):
    items, rows, width = cross_q.shape
    many = memory.shape[1]
    pairs = items * rows * HEADS * many
    return pl.pallas_call(
        cross_backward_kernel,
        grid=(1,),
        in_specs=[IN_SMEM] + [whole(x.shape) for x in (cross_q, memory, d_out, lse)],
        out_specs=whole((items, rows, width)),
        out_shape=jax.ShapeDtypeStruct((items, rows, width), BF),
        compiler_params=pltpu.CompilerParams(vmem_limit_bytes=ROOM),
        cost_estimate=pl.CostEstimate(
            flops=pairs * 10 * WIDE, bytes_accessed=6 << 20, transcendentals=pairs
        ),
        name="cross_backward",
    )(counts, cross_q, memory, d_out, lse)


def memory_back_kernel(head_ref, count_ref, q_ref, do_ref, k_ref, v_ref, out_ref):
    items, many, _ = k_ref.shape
    odd = lax.rem(head_ref[0], 2)
    queries = q_ref[...].reshape(-1, LANES) * BF(HEAD_DIM**-0.5)
    grads = do_ref[...].reshape(-1, LANES)
    lane = lax.broadcasted_iota(jnp.int32, (many, LANES), 1) // HEAD_DIM
    row = lax.broadcasted_iota(jnp.int32, (many, queries.shape[0]), 0)

    def turn(ref, item):
        block = ref[item].astype(F32)
        block = jnp.where(odd == item, block, swap_half(block))
        return jnp.where(lane == item, block, 0.0).astype(BF)

    d_keys = None
    for item in range(items):
        scores = mm_nt(turn(k_ref, item), queries)
        scores = jnp.where(row < count_ref[item], scores, TINY)
        weights = jnp.exp(scores - jnp.max(scores, axis=0, keepdims=True))
        probs = weights * (1.0 / jnp.sum(weights, axis=0, keepdims=True))
        d_probs = mm_nt(turn(v_ref, item), grads)
        delta = jnp.sum(probs * d_probs, axis=0, keepdims=True)
        d_scores = (probs * (d_probs - delta)).astype(BF)
        new_k = mm(d_scores, queries)
        new_v = mm(probs.astype(BF), grads)
        d_values = new_v if d_keys is None else jnp.where(lane == item, new_v, d_values)
        d_keys = new_k if d_keys is None else jnp.where(lane == item, new_k, d_keys)
    shape = (out_ref.shape[0], 1) + out_ref.shape[2:]
    out_ref[:, 0:1] = d_keys.astype(out_ref.dtype).reshape(shape)
    out_ref[:, 1:2] = d_values.astype(out_ref.dtype).reshape(shape)


def memory_back(head, counts, got, memory, part, low):
    blocks, _, own, _ = got.shape
    items, many, double = memory.shape
    pairs = double // 2 // LANES
    work = items * many * blocks * own
    return pl.pallas_call(
        memory_back_kernel,
        grid_spec=pltpu.PrefetchScalarGridSpec(
            num_scalar_prefetch=2,
            grid=(1,),
            in_specs=[
                pl.BlockSpec((blocks, 1, own, LANES), lambda i, h, c: (0, 1, 0, 0)),
                pl.BlockSpec((blocks, 1, own, LANES), lambda i, h, c: (0, 2, 0, 0)),
                pl.BlockSpec((items, many, LANES), lambda i, h, c: (0, 0, lax.div(h[0], 2))),
                pl.BlockSpec(
                    (items, many, LANES), lambda i, h, c: (0, 0, pairs + lax.div(h[0], 2))
                ),
            ],
            out_specs=whole((many // part, 2, part, LANES)),
        ),
        out_shape=jax.ShapeDtypeStruct((many // part, 2, part, LANES), BF if low else F32),
        compiler_params=pltpu.CompilerParams(vmem_limit_bytes=ROOM),
        cost_estimate=pl.CostEstimate(
            flops=work * 8 * LANES, bytes_accessed=2 << 20, transcendentals=work
        ),
        name="memory_back",
    )(head, counts, got, got, memory, memory)


def swap_half(block):
    return pltpu.roll(block, HEAD_DIM, 1)


def first_half(shape):
    return lax.broadcasted_iota(jnp.int32, shape, 1) < HEAD_DIM


def pair_to_heads(block):
    own = block.shape[0] // 2
    left, right = block[:own], block[own:]
    low = first_half(left.shape)
    return (
        jnp.where(low, left, swap_half(right)),
        jnp.where(low, swap_half(left), right),
    )


def project_kernel(tri_ref, mod_ref, q_ref, k_ref, v_ref, out_ref, normed):
    items, own, width = tri_ref.shape

    @pl.when(pl.program_id(0) == 0)
    def _():
        for item in range(items):
            unit, unused = center_scale(tri_ref[item].astype(F32))
            scale = mod_ref[item : item + 1, width:]
            shift = mod_ref[item : item + 1, :width]
            normed[item * own : (item + 1) * own] = (unit * (1.0 + scale) + shift).astype(BF)

    for kind, ref in enumerate((q_ref, k_ref, v_ref)):
        block = mm(normed[...], ref[...])
        for pair in range(WIDE // LANES):
            first, second = pair_to_heads(block[:, pair * LANES : (pair + 1) * LANES])
            out_ref[2 * pair, kind] = first.astype(BF)
            out_ref[2 * pair + 1, kind] = second.astype(BF)


def project(triplane, modulation, qkv_weight):
    items, own, width = triplane.shape
    steps = width // WIDE
    return pl.pallas_call(
        project_kernel,
        grid=(steps,),
        in_specs=[
            pl.BlockSpec((items, own, width), lambda i: (0, 0, 0)),
            pl.BlockSpec((items, 2 * width), lambda i: (0, 0)),
            pl.BlockSpec((width, WIDE), lambda i: (0, i)),
            pl.BlockSpec((width, WIDE), lambda i: (0, steps + i)),
            pl.BlockSpec((width, WIDE), lambda i: (0, 2 * steps + i)),
        ],
        out_specs=pl.BlockSpec((GROUP, 3, own, LANES), lambda i: (i, 0, 0, 0)),
        out_shape=jax.ShapeDtypeStruct((HEADS, 3, own, LANES), BF),
        scratch_shapes=[pltpu.VMEM((items * own, width), BF)],
        compiler_params=pltpu.CompilerParams(vmem_limit_bytes=ROOM),
        cost_estimate=pl.CostEstimate(
            flops=6 * items * own * width * width, bytes_accessed=8 << 20, transcendentals=0
        ),
        name="project",
    )(triplane, modulation, qkv_weight, qkv_weight, qkv_weight)


def middle_kernel(
    got_ref,
    tri_ref,
    gain,
    bias,
    out_hbm,
    query_hbm,
    att_ref,
    mid_ref,
    normed_ref,
    query_ref,
    out_w,
    query_w,
    sems,
):
    fetch_out = pltpu.make_async_copy(out_hbm, out_w, sems.at[0])
    fetch_out.start()
    fetch_query = pltpu.make_async_copy(query_hbm, query_w, sems.at[1])
    fetch_query.start()
    heads, own, _ = got_ref.shape
    for pair in range(heads // 2):
        left = got_ref[2 * pair].astype(F32)
        right = got_ref[2 * pair + 1].astype(F32)
        low = first_half(left.shape)
        span = slice(pair * LANES, (pair + 1) * LANES)
        att_ref[:own, span] = jnp.where(low, left, swap_half(right)).astype(BF)
        att_ref[own:, span] = jnp.where(low, swap_half(left), right).astype(BF)
    fetch_out.wait()
    middle = tri_ref[...].astype(F32) + mm(att_ref[...], out_w[...])
    mid_ref[...] = middle
    unit, unused = center_scale(middle)
    normed = (unit * gain[...] + bias[...]).astype(BF)
    normed_ref[...] = normed
    fetch_query.wait()
    query_ref[...] = mm(normed, query_w[...]).astype(BF)


def middle_part(got, tri_rows, self_out, gain, bias, cross_query):
    rows, width = tri_rows.shape
    low = jax.ShapeDtypeStruct((rows, width), BF)
    return pl.pallas_call(
        middle_kernel,
        grid=(1,),
        in_specs=[whole(got.shape), whole((rows, width)), whole((1, width)), whole((1, width))]
        + [ANYWHERE] * 2,
        out_specs=[whole((rows, width))] * 4,
        out_shape=[low, jax.ShapeDtypeStruct((rows, width), F32), low, low],
        scratch_shapes=[
            pltpu.VMEM(self_out.shape, BF),
            pltpu.VMEM(cross_query.shape, BF),
            pltpu.SemaphoreType.DMA((2,)),
        ],
        compiler_params=pltpu.CompilerParams(vmem_limit_bytes=ROOM),
        cost_estimate=pl.CostEstimate(
            flops=4 * rows * width * width, bytes_accessed=5 << 20, transcendentals=0
        ),
        name="middle_part",
    )(got, tri_rows, gain[None], bias[None], self_out, cross_query)


def middle_back_kernel(
    dq_ref,
    mid_ref,
    gain,
    later_ref,
    query_ref,
    crossed_ref,
    query_hbm,
    out_hbm,
    d_mid_ref,
    low_ref,
    heads_ref,
    sums_ref,
    query_w,
    out_w,
    sems,
):
    fetch_query = pltpu.make_async_copy(query_hbm, query_w, sems.at[0])
    fetch_query.start()
    fetch_out = pltpu.make_async_copy(out_hbm, out_w, sems.at[1])
    fetch_out.start()

    def by_head(values, kind):
        for pair in range(values.shape[1] // LANES):
            block = values[:, pair * LANES : (pair + 1) * LANES].astype(F32)
            first, second = pair_to_heads(block)
            heads_ref[2 * pair, kind] = first.astype(BF)
            heads_ref[2 * pair + 1, kind] = second.astype(BF)

    by_head(query_ref[...], 1)
    by_head(crossed_ref[...], 2)
    fetch_query.wait()
    d_normed = mm_nt(dq_ref[...], query_w[...])
    unit, rstd = center_scale(mid_ref[...])
    sums_ref[0:1] = jnp.sum(d_normed * unit, axis=0, keepdims=True)
    sums_ref[1:2] = jnp.sum(d_normed, axis=0, keepdims=True)
    d_middle = later_ref[...] + norm_back(unit, rstd, d_normed * gain[...])
    d_mid_ref[...] = d_middle
    low = d_middle.astype(BF)
    low_ref[...] = low
    fetch_out.wait()
    by_head(mm_nt(low, out_w[...]), 0)


def middle_back(own, d_query, cross_query, middle, gain, d_later, self_out, cross_q, d_crossed):
    rows, width = middle.shape
    return pl.pallas_call(
        middle_back_kernel,
        grid=(1,),
        in_specs=[whole((rows, width)), whole((rows, width)), whole((1, width))]
        + [whole((rows, width))] * 3
        + [ANYWHERE] * 2,
        out_specs=[
            whole((rows, width)),
            whole((rows, width)),
            whole((HEADS, 3, own, LANES)),
            whole((2, width)),
        ],
        scratch_shapes=[
            pltpu.VMEM(cross_query.shape, BF),
            pltpu.VMEM(self_out.shape, BF),
            pltpu.SemaphoreType.DMA((2,)),
        ],
        out_shape=[
            jax.ShapeDtypeStruct((rows, width), F32),
            jax.ShapeDtypeStruct((rows, width), BF),
            jax.ShapeDtypeStruct((HEADS, 3, own, LANES), BF),
            jax.ShapeDtypeStruct((2, width), F32),
        ],
        compiler_params=pltpu.CompilerParams(vmem_limit_bytes=ROOM),
        cost_estimate=pl.CostEstimate(
            flops=4 * rows * width * width, bytes_accessed=6 << 20, transcendentals=0
        ),
        name="middle_back",
    )(d_query, middle, gain[None], d_later, cross_q, d_crossed, cross_query, self_out)


def first_back_kernel(
    steps, got_ref, q_ref, k_ref, v_ref, tri_ref, mod_ref, mid_ref, out_ref, total
):
    items, own, width = tri_ref.shape
    step = pl.program_id(0)
    added = None
    for kind, ref in enumerate((q_ref, k_ref, v_ref)):
        columns = []
        for pair in range(WIDE // LANES):
            at = slice(kind * own, (kind + 1) * own)
            left = got_ref[2 * pair, at].astype(F32)
            right = got_ref[2 * pair + 1, at].astype(F32)
            low = first_half(left.shape)
            columns.append(
                jnp.concatenate(
                    [
                        jnp.where(low, left, swap_half(right)),
                        jnp.where(low, swap_half(left), right),
                    ],
                    axis=0,
                )
            )
        term = mm_nt(jnp.concatenate(columns, axis=1).astype(BF), ref[...])
        added = term if added is None else added + term

    @pl.when(step == 0)
    def _():
        total[...] = added

    @pl.when(step > 0)
    def _():
        total[...] += added

    @pl.when(step == steps - 1)
    def _():
        for item in range(items):
            unit, rstd = center_scale(tri_ref[item].astype(F32))
            grad = total[item * own : (item + 1) * own] * (1.0 + mod_ref[item : item + 1, width:])
            out_ref[item] = mid_ref[item] + norm_back(unit, rstd, grad)


def first_back(got, qkv_weight, triplane, modulation, d_middle):
    items, own, width = triplane.shape
    steps = width // WIDE
    return pl.pallas_call(
        functools.partial(first_back_kernel, steps),
        grid=(steps,),
        in_specs=[
            pl.BlockSpec((GROUP,) + got.shape[1:], lambda i: (i, 0, 0)),
            pl.BlockSpec((width, WIDE), lambda i: (0, i)),
            pl.BlockSpec((width, WIDE), lambda i: (0, steps + i)),
            pl.BlockSpec((width, WIDE), lambda i: (0, 2 * steps + i)),
            pl.BlockSpec((items, own, width), lambda i: (0, 0, 0)),
            pl.BlockSpec((items, 2 * width), lambda i: (0, 0)),
            pl.BlockSpec((items, own, width), lambda i: (0, 0, 0)),
        ],
        out_specs=pl.BlockSpec((items, own, width), lambda i: (0, 0, 0)),
        out_shape=jax.ShapeDtypeStruct((items, own, width), F32),
        scratch_shapes=[pltpu.VMEM((items * own, width), F32)],
        compiler_params=pltpu.CompilerParams(vmem_limit_bytes=ROOM),
        cost_estimate=pl.CostEstimate(
            flops=6 * items * own * width * width, bytes_accessed=8 << 20, transcendentals=0
        ),
        name="first_back",
    )(got, qkv_weight, qkv_weight, qkv_weight, triplane, modulation, d_middle)


def head_back_kernel(
    packed,
    head_ref,
    dq_ref,
    dkv_ref,
    dmem_ref,
    tri_ref,
    patch_ref,
    q_ref,
    k_ref,
    v_ref,
    mod_ref,
    *rest,
):
    units = rest[-1]
    items, many, width = tri_ref.shape
    odd = lax.rem(head_ref[0], 2) == 1
    grads = [
        dq_ref[:, 0].reshape(many, LANES).astype(F32).T,
        dkv_ref[:, 0].reshape(many, LANES).astype(F32).T,
        dkv_ref[:, 1].reshape(many, LANES).astype(F32).T,
    ]
    weight = []
    for ref in (q_ref, k_ref, v_ref):
        turned = ref[...].astype(F32).T
        weight.append(jnp.where(odd, turned[HEAD_DIM:], turned[:HEAD_DIM]))
    weight = jnp.concatenate(weight, axis=0)
    product = None
    terms = []
    for item in range(items):
        unit, unused = center_scale(tri_ref[item].astype(F32))
        units[...] = unit.astype(BF)
        span = slice(item * HEAD_DIM, (item + 1) * HEAD_DIM)
        mine = jnp.concatenate([part[span] for part in grads], axis=0)
        outer = mm(mine.astype(BF), units[...])
        column = jnp.sum(mine, axis=1, keepdims=True)
        shift = mod_ref[item : item + 1, :width]
        scale = mod_ref[item : item + 1, width:]
        terms.append(jnp.sum(column * weight, axis=0, keepdims=True))
        terms.append(jnp.sum(outer * weight, axis=0, keepdims=True))
        term = outer * (1.0 + scale) + column * shift
        product = term if product is None else product + term
    product = product.T
    patch_rows = patch_ref.shape[1]
    grads = [dmem_ref[:, kind].reshape(patch_rows, LANES).astype(F32).T for kind in range(2)]
    memory = None
    for item in range(items):
        span = slice(item * HEAD_DIM, (item + 1) * HEAD_DIM)
        mine = jnp.concatenate([part[span] for part in grads], axis=0).astype(BF)
        term = mm(mine, patch_ref[item])
        memory = term if memory is None else memory + term
    memory = memory.T
    if not packed:
        out_ref, memory_ref, terms_ref = rest[:3]
        out_ref[...] = product.astype(BF)
        memory_ref[...] = memory.astype(BF)
        for item in range(items):
            terms_ref[item : item + 1, :width] = terms[2 * item]
            terms_ref[item : item + 1, width:] = terms[2 * item + 1]
        return
    ends_ref, out_ref, terms_ref, unused = rest
    devices = out_ref.shape[0]
    span = width // devices
    product = product.reshape(devices, span, 3 * HEAD_DIM).astype(BF)
    out_ref[:, :span] = memory.reshape(devices, span, LANES).astype(BF)
    out_ref[:, span : 2 * span] = product[:, :, :LANES]
    last = product[:, :, LANES:]
    at = 2 * span + span // 2
    out_ref[:, 2 * span : at] = jnp.concatenate(
        [last[:, : span // 2], last[:, span // 2 :]], axis=2
    )
    out_ref[:, at:] = ends_ref[...]
    lines = [
        term[:, k * LANES : (k + 1) * LANES] for term in terms for k in range(width // LANES)
    ]
    terms_ref[...] = jnp.concatenate(lines, axis=0).astype(BF)


def head_back(head, d_q, d_kv, d_mem, rows_all, patch_part, qkv_weight, modulation, ends):
    items, many, width = rows_all.shape
    blocks, _, own, _ = d_q.shape
    pairs = width // LANES
    product = jax.ShapeDtypeStruct((width, 3 * HEAD_DIM), BF)
    if ends is None:
        more = []
        shapes = [
            product,
            jax.ShapeDtypeStruct((width, LANES), BF),
            jax.ShapeDtypeStruct((items, 2 * width), F32),
        ]
    else:
        devices, tail, _ = ends.shape
        more = [ends]
        many_rows = 5 * width // devices // 2 + tail
        shapes = [
            jax.ShapeDtypeStruct((devices, many_rows, LANES), BF),
            jax.ShapeDtypeStruct((2 * items * pairs, LANES), BF),
        ]

    def whole_block(shape):
        return pl.BlockSpec(shape, lambda i, h: (0,) * len(shape))

    return pl.pallas_call(
        functools.partial(head_back_kernel, ends is not None),
        grid_spec=pltpu.PrefetchScalarGridSpec(
            num_scalar_prefetch=1,
            grid=(1,),
            in_specs=[
                pl.BlockSpec((blocks, 1, own, LANES), lambda i, h: (0, 0, 0, 0)),
                pl.BlockSpec((blocks, 2, own, LANES), lambda i, h: (0, 0, 0, 0)),
                whole_block(d_mem.shape),
                pl.BlockSpec((items, many, width), lambda i, h: (0, 0, 0)),
                whole_block(patch_part.shape),
                pl.BlockSpec((width, LANES), lambda i, h: (0, lax.div(h[0], 2))),
                pl.BlockSpec((width, LANES), lambda i, h: (0, pairs + lax.div(h[0], 2))),
                pl.BlockSpec((width, LANES), lambda i, h: (0, 2 * pairs + lax.div(h[0], 2))),
                whole_block((items, 2 * width)),
            ]
            + [whole_block(array.shape) for array in more],
            out_specs=[whole_block(shape.shape) for shape in shapes],
            scratch_shapes=[pltpu.VMEM((many, width), BF)],
        ),
        out_shape=shapes,
        compiler_params=pltpu.CompilerParams(vmem_limit_bytes=ROOM),
        cost_estimate=pl.CostEstimate(
            flops=6 * items * many * width * HEAD_DIM, bytes_accessed=5 << 20, transcendentals=0
        ),
        name="head_back",
    )(
        head,
        d_q,
        d_kv,
        d_mem,
        rows_all,
        patch_part,
        qkv_weight,
        qkv_weight,
        qkv_weight,
        modulation,
        *more,
    )


def by_heads_kernel(got_ref, out_ref):
    parts, heads, rows, _ = got_ref.shape
    width = heads * HEAD_DIM
    for pair in range(heads // 2):
        left = got_ref[0, 2 * pair].astype(F32)
        right = got_ref[0, 2 * pair + 1].astype(F32)
        for part in range(1, parts):
            left = left + got_ref[part, 2 * pair].astype(F32)
            right = right + got_ref[part, 2 * pair + 1].astype(F32)
        for kind in range(3):
            span = slice(kind * HEAD_DIM, (kind + 1) * HEAD_DIM)
            at = kind * width + pair * LANES
            out_ref[:, at : at + LANES] = jnp.concatenate([left[:, span], right[:, span]], axis=1)


def by_heads(got):
    parts, heads, rows, features = got.shape
    return pl.pallas_call(
        by_heads_kernel,
        grid=(1,),
        in_specs=[whole(got.shape)],
        out_specs=whole((rows, heads * features)),
        out_shape=jax.ShapeDtypeStruct((rows, heads * features), F32),
        compiler_params=pltpu.CompilerParams(vmem_limit_bytes=ROOM),
        name="by_heads",
    )(got)


def unpack_kernel(tail, got_ref, mem_ref, qkv_ref, mod_ref, ends_ref):
    span = qkv_ref.shape[0]
    width = HEADS * HEAD_DIM
    at = 2 * span + span // 2

    def columns(head):
        full = got_ref[head, :at].astype(F32)
        last = full[2 * span :]
        last = jnp.concatenate([last[:, :HEAD_DIM], last[:, HEAD_DIM:]], axis=0)
        first, second = full[:span], full[span : 2 * span]
        return (
            first[:, :HEAD_DIM],
            first[:, HEAD_DIM:],
            second[:, :HEAD_DIM],
            second[:, HEAD_DIM:],
            last,
        )

    for pair in range(HEADS // 2):
        both = [
            jnp.concatenate(sides, axis=1)
            for sides in zip(columns(2 * pair), columns(2 * pair + 1))
        ]
        for kind in range(2):
            start = kind * width + pair * LANES
            mem_ref[:, start : start + LANES] = both[kind]
        for kind in range(3):
            start = kind * width + pair * LANES
            qkv_ref[:, start : start + LANES] = both[2 + kind]
    total = got_ref[0, at:].astype(F32)
    for head in range(1, HEADS):
        total = total + got_ref[head, at:].astype(F32)
    ends_ref[...] = total[:tail]
    mod_ref[...] = total[tail:]


def unpack(got, span, tail):
    _, many, _ = got.shape
    shapes = [
        (span, 2 * HEADS * HEAD_DIM),
        (span, 3 * HEADS * HEAD_DIM),
        (many - tail - 2 * span - span // 2, LANES),
        (tail, LANES),
    ]
    return pl.pallas_call(
        functools.partial(unpack_kernel, tail),
        grid=(1,),
        in_specs=[whole(got.shape)],
        out_specs=[whole(shape) for shape in shapes],
        out_shape=[jax.ShapeDtypeStruct(shape, F32) for shape in shapes],
        compiler_params=pltpu.CompilerParams(vmem_limit_bytes=ROOM),
        name="unpack",
    )(got)


def gather_lanes(block, starts, span):
    out = []
    lane = lax.broadcasted_iota(jnp.int32, (block.shape[0], LANES), 1)
    for at in range(0, len(starts) * span, LANES):
        merged = None
        for to in range(0, LANES, min(span, LANES)):
            start = starts[(at + to) // span] + (at + to) % span
            base = start // LANES * LANES
            part = block[:, base : base + LANES]
            shift = (to - (start - base)) % LANES
            if shift:
                part = pltpu.roll(part, shift, 1)
            if merged is None:
                merged = part
            else:
                merged = jnp.where((lane >= to) & (lane < to + span), part, merged)
        out.append(merged)
    return jnp.concatenate(out, axis=1)


def starts_y(features, devices, quarter):
    span = features // devices
    return [(group * 4 + quarter) * span for group in range(devices // 4)]


def starts_x(features, devices, half, low):
    span = features // devices
    many = devices // 2
    return [
        (half * many + rest * 4 + y * 2 + low) * span
        for y in range(2)
        for rest in range(many // 4)
    ]


def mlp_kernel(
    steps,
    devices,
    normed_ref,
    dh_ref,
    up_ref,
    later_ref,
    c_ref,
    gain,
    out_w,
    hidden_ref,
    pre_ref,
    up_piece_ref,
    down_piece_ref,
    d_later_ref,
    low_ref,
    d_crossed_ref,
    sums_ref,
    total,
):
    step = pl.program_id(0)

    @pl.when(step == 0)
    def _():
        values = normed_ref[...].astype(F32)
        for quarter in range(4):
            starts = starts_y(values.shape[1], devices, quarter)
            span = values.shape[1] // devices
            up_piece_ref[quarter] = gather_lanes(values, starts, span).astype(BF)

    pre = mm(normed_ref[...], up_ref[...])
    square = pre * pre
    slope = (2.0 / 3.141592653589793) ** 0.5
    turn = jnp.tanh(slope * (pre + 0.044715 * (pre * square)))
    hidden = 0.5 * pre * (1.0 + turn)
    hidden_ref[...] = hidden.astype(BF)
    part = hidden.shape[1]
    span = part * steps // devices
    half = lax.div(step, steps // 2)
    for low in range(2):
        for y in range(2):
            starts = [(rest * 4 + y * 2 + low) * span for rest in range(part // (4 * span))]
            at = y * (part * steps // 8) + lax.rem(step, steps // 2) * (part // 4)
            at = pl.ds(pl.multiple_of(at, LANES), part // 4)
            down_piece_ref[2 * half + low, :, at] = gather_lanes(hidden, starts, span).astype(BF)
    change = 0.5 * (1.0 + turn) + 0.5 * pre * (1.0 - turn * turn) * (
        slope * (1.0 + 3.0 * 0.044715 * square)
    )
    d_pre = (dh_ref[...] * change).astype(BF)
    pre_ref[...] = d_pre
    added = mm_nt(d_pre, up_ref[...])

    @pl.when(step == 0)
    def _():
        total[...] = added

    @pl.when(step > 0)
    def _():
        total[...] += added

    @pl.when(step == steps - 1)
    def _():
        d_normed = total[...]
        unit, rstd = center_scale(later_ref[...])
        sums_ref[0:1] = jnp.sum(d_normed * unit, axis=0, keepdims=True)
        sums_ref[1:2] = jnp.sum(d_normed, axis=0, keepdims=True)
        d_later = c_ref[...].astype(F32) + norm_back(unit, rstd, d_normed * gain[...])
        d_later_ref[...] = d_later
        low = d_later.astype(BF)
        low_ref[...] = low
        d_crossed_ref[...] = mm_nt(low, out_w[...]).astype(BF)


def mlp(devices, normed, d_hidden, up_weight, later, grad_out, gain, cross_out):
    rows, width = normed.shape
    hidden_width = up_weight.shape[1]
    part = min(1024, hidden_width)
    steps = hidden_width // part
    low = jax.ShapeDtypeStruct((rows, width), BF)
    return pl.pallas_call(
        functools.partial(mlp_kernel, steps, devices),
        grid=(steps,),
        in_specs=[
            whole((rows, width)),
            pl.BlockSpec((rows, part), lambda i: (0, i)),
            pl.BlockSpec((width, part), lambda i: (0, i)),
            whole((rows, width)),
            whole((rows, width)),
            whole((1, width)),
            whole((width, width)),
        ],
        out_specs=[
            pl.BlockSpec((rows, part), lambda i: (0, i)),
            pl.BlockSpec((rows, part), lambda i: (0, i)),
            whole((4, rows, width // 4)),
            whole((4, rows, hidden_width // 4)),
            whole((rows, width)),
            whole((rows, width)),
            whole((rows, width)),
            whole((2, width)),
        ],
        out_shape=[
            jax.ShapeDtypeStruct((rows, hidden_width), BF),
            jax.ShapeDtypeStruct((rows, hidden_width), BF),
            jax.ShapeDtypeStruct((4, rows, width // 4), BF),
            jax.ShapeDtypeStruct((4, rows, hidden_width // 4), BF),
            jax.ShapeDtypeStruct((rows, width), F32),
            low,
            low,
            jax.ShapeDtypeStruct((2, width), F32),
        ],
        scratch_shapes=[pltpu.VMEM((rows, width), F32)],
        compiler_params=pltpu.CompilerParams(vmem_limit_bytes=ROOM),
        cost_estimate=pl.CostEstimate(
            flops=4 * rows * width * hidden_width,
            bytes_accessed=12 << 20,
            transcendentals=rows * hidden_width,
        ),
        name="mlp",
    )(normed, d_hidden, up_weight, later, grad_out, gain[None], cross_out)


def pieces_kernel(devices, *refs):
    out_ref = refs[-1]
    for k, ref in enumerate(refs[:-1]):
        values = ref[...].astype(F32)
        span = values.shape[1] // devices
        for half in range(2):
            for low in range(2):
                starts = starts_x(values.shape[1], devices, half, low)
                out_ref[2 * half + low, k] = gather_lanes(values, starts, span).astype(BF)


def pieces(devices, *arrays):
    rows, width = arrays[0].shape
    return pl.pallas_call(
        functools.partial(pieces_kernel, devices),
        grid=(1,),
        in_specs=[whole((rows, width))] * len(arrays),
        out_specs=whole((4, len(arrays), rows, width // 4)),
        out_shape=jax.ShapeDtypeStruct((4, len(arrays), rows, width // 4), BF),
        compiler_params=pltpu.CompilerParams(vmem_limit_bytes=ROOM),
        name="pieces",
    )(*arrays)


def product_kernel(half_ref, *refs):
    x_refs, y_refs, (keep_ref, send_ref, left, right) = refs[:4], refs[4:8], refs[8:]
    rows = x_refs[0].shape[1]

    @pl.when(pl.program_id(1) == 0)
    def _():
        for k, ref in enumerate(x_refs):
            left[k * rows : (k + 1) * rows] = ref[0]

    for k, ref in enumerate(y_refs):
        right[k * rows : (k + 1) * rows] = ref[0]
    wide = left.shape[1] // 2
    half = half_ref[0]
    for ref, which in ((keep_ref, half), (send_ref, 1 - half)):
        at = pl.ds(pl.multiple_of(which * wide, LANES), wide)
        ref[...] = mm_tn(left[:, at], right[...]).astype(BF).reshape(ref.shape)


def product(half, quads, left, right):
    entries, rows, wide = left[0].shape
    columns = right[0].shape[2]
    span = wide // (2 * quads)
    part = min(columns, 1024)
    shape = jax.ShapeDtypeStruct((quads, entries, span, columns), BF)
    spec = pl.BlockSpec((quads, 1, span, part), lambda e, i: (0, e, 0, i))
    return pl.pallas_call(
        product_kernel,
        grid=(entries, columns // part),
        in_specs=[IN_SMEM]
        + [pl.BlockSpec((1, rows, wide), lambda e, i: (e, 0, 0))] * 4
        + [pl.BlockSpec((1, rows, part), lambda e, i: (e, 0, i))] * 4,
        out_specs=[spec, spec],
        out_shape=[shape, shape],
        scratch_shapes=[pltpu.VMEM((4 * rows, wide), BF), pltpu.VMEM((4 * rows, part), BF)],
        compiler_params=pltpu.CompilerParams(vmem_limit_bytes=ROOM),
        cost_estimate=pl.CostEstimate(
            flops=8 * entries * rows * wide * columns, bytes_accessed=8 << 20, transcendentals=0
        ),
        name="product",
    )(half.reshape(1).astype(jnp.int32), *left, *right)


def xor_blk(values, bit, count):
    return lax.ppermute(values, "blk", [(i, i ^ bit) for i in range(count)])


def swap_batch(values):
    return lax.ppermute(values, "batch", [(0, 1), (1, 0)])


def after(values, *first):
    return lax.optimization_barrier((values, first))[0]


def take(values, index, axis):
    return lax.dynamic_index_in_dim(values, index, axis, keepdims=False)


def local(
    count_blk,
    triplane,
    patches,
    cotangent,
    camera_index,
    triplane_count,
    patch_count,
    camera_table,
    mod_weight,
    qkv_weight,
    self_out,
    gain_mid,
    bias_mid,
    cross_query,
    cross_memory,
    cross_out,
    gain_last,
    bias_last,
    up_weight,
    down_weight,
):
    items, own, width = triplane.shape
    own_patches = patches.shape[1]
    rows = items * own
    spare = count_blk // HEADS
    quads = count_blk // 4
    devices = 2 * count_blk
    row_groups = (
        None
        if spare == 1
        else [[part * HEADS + head for head in range(HEADS)] for part in range(spare)]
    )
    head_groups = [[part * HEADS + head for part in range(spare)] for head in range(HEADS)]
    batch_at = lax.axis_index("batch")
    blk_at = lax.axis_index("blk")
    head_at = lax.rem(blk_at, HEADS)
    place = batch_at * count_blk + blk_at

    def to_heads(values):
        return lax.all_to_all(values, "blk", 0, 0, axis_index_groups=row_groups, tiled=True)

    def swap_corner(values):
        return lax.ppermute(
            values,
            BOTH,
            [
                (b * count_blk + j, (1 - b) * count_blk + (j ^ 1))
                for b in range(2)
                for j in range(count_blk)
            ],
        )

    def quad_y(values):
        far = xor_blk(values, 2, count_blk)
        return [values, xor_blk(values, 1, count_blk), far, xor_blk(far, 1, count_blk)]

    def quad_x(values):
        far = swap_batch(values)
        return [values, xor_blk(values, 1, count_blk), far, xor_blk(far, 1, count_blk)]

    def exchange_y(cut):
        low = jnp.bitwise_and(blk_at, 3)
        got = [take(cut, low, 0)]
        for bit in (1, 2, 3):
            got.append(xor_blk(take(cut, jnp.bitwise_xor(low, bit), 0), bit, count_blk))
        return got

    def exchange_x(cut):
        low = jnp.bitwise_and(blk_at, 1)
        return [
            take(cut, 2 * batch_at + low, 0),
            xor_blk(take(cut, 2 * batch_at + 1 - low, 0), 1, count_blk),
            swap_batch(take(cut, 2 * (1 - batch_at) + low, 0)),
            swap_corner(take(cut, 2 * (1 - batch_at) + 1 - low, 0)),
        ]

    def half_x(values):
        given = swap_batch(take(values, 1 - batch_at, 0))
        return (take(values, batch_at, 0).astype(F32) + given.astype(F32)).astype(BF)

    def rest_sum(keep, given):
        many = quads
        bit = 4
        while many > 1:
            low = jnp.bitwise_and(lax.div(blk_at, bit), 1)
            shape = (many // 2, 2) + keep.shape[1:]
            keep, given = keep.reshape(shape), given.reshape(shape)

            def part(index):
                total = take(keep, index, 1).astype(F32) + take(given, index, 1).astype(F32)
                return total.astype(BF)

            keep, given = part(low), xor_blk(part(1 - low), bit, count_blk)
            many //= 2
            bit *= 2
        return (keep.astype(F32) + given.astype(F32))[0]

    views = camera_index.shape[1]
    table_rows = jnp.arange(camera_table.shape[0], dtype=jnp.int32)

    def pick_of(cams):
        return jnp.sum((cams[:, :, None] == table_rows[None, None, :]).astype(F32), axis=1)

    def code_of(pick):
        return (mm(pick.astype(BF), camera_table) / views).astype(BF)

    modulation = mm(code_of(pick_of(camera_index)), mod_weight)
    sent = project(triplane, modulation, qkv_weight)
    qkv = to_heads(sent)

    patches_all = lax.all_gather(patches, "blk", axis=1, tiled=True)
    bit_y = jnp.bitwise_and(lax.div(blk_at, 2), 1)
    many_patches = patches_all.shape[1]
    memory = (
        mm(patches_all.reshape(items * many_patches, width), cross_memory)
        .astype(BF)
        .reshape(items, many_patches, 2 * width)
    )
    grad_out = cotangent.reshape(rows, width)
    d_hidden = mm_nt(grad_out, down_weight)
    grad_quad = quad_x(lax.optimization_barrier((grad_out, sent))[0])

    qkv, d_hidden = lax.optimization_barrier((qkv, d_hidden))
    if spare == 1:
        kv, kv_first = qkv, 1
    else:
        kv = lax.all_gather(qkv[:, 1:], "blk", axis=0, axis_index_groups=head_groups, tiled=True)
        kv_first = 0
    attended_heads, self_lse = self_forward(triplane_count, qkv, kv, kv_first)
    attended_got = to_heads(attended_heads)
    kept = lax.optimization_barrier((triplane, attended_heads))[0]
    rows_all = lax.all_gather(kept, "blk", axis=1, axis_index_groups=row_groups, tiled=True)

    attended_got, memory, grad_quad = lax.optimization_barrier(
        (attended_got, memory, grad_quad)
    )
    attended_low, middle, normed_mid, cross_q = middle_part(
        attended_got, triplane.reshape(rows, width), self_out, gain_mid, bias_mid, cross_query
    )
    cross_q = cross_q.reshape(items, own, width)
    crossed, cross_lse, later, normed_last = cross_forward(
        patch_count, cross_q, memory, middle, cross_out, gain_last, bias_last
    )
    hidden, d_pre, last_pieces, hidden_pieces, d_later, d_later_low, d_crossed, sums_last = mlp(
        devices, normed_last, d_hidden, up_weight, later, grad_out, gain_last, cross_out
    )
    pre_far = xor_blk(d_pre, 2, count_blk)
    pre_near = xor_blk(d_pre, 1, count_blk)
    last_pieces = exchange_y(last_pieces)
    hidden_pieces = exchange_x(hidden_pieces)

    d_cross_q = cross_backward(
        patch_count, cross_q, memory, d_crossed.reshape(items, own, width), cross_lse
    )
    d_cross_low = d_cross_q.reshape(rows, width)
    d_middle, d_middle_low, back_heads, sums_mid = middle_back(
        own,
        d_cross_low,
        cross_query,
        middle,
        gain_mid,
        d_later,
        self_out,
        cross_q.reshape(rows, width),
        d_crossed,
    )
    pre_quad = [d_pre, pre_near, pre_far, xor_blk(pre_far, 1, count_blk)]
    back_heads = to_heads(back_heads)

    up_keep, up_send = product(
        batch_at, quads, [p[None] for p in last_pieces], [p[None] for p in pre_quad]
    )
    down_keep, down_send = product(
        bit_y, quads, [p[None] for p in hidden_pieces], [p[None] for p in grad_quad]
    )
    up_given = swap_batch(up_send)
    down_given = xor_blk(down_send, 2, count_blk)
    lefts, rights = after(
        (
            (crossed.reshape(rows, width), normed_mid, attended_low),
            (d_later_low, d_cross_low, d_middle_low),
        ),
        back_heads,
    )
    squares = exchange_x(pieces(devices, *lefts))
    rights = jnp.stack(rights)
    rights_far = swap_batch(rights)
    rights_near = xor_blk(rights, 1, count_blk)

    d_q, d_kv = self_backward(
        triplane_count, qkv, kv, kv_first, back_heads, self_lse, spare == 1
    )
    head = head_at.reshape(1).astype(jnp.int32)
    d_mem = memory_back(head, patch_count, back_heads, memory, own_patches, spare == 1)
    if spare > 1:
        d_kv, d_mem = [
            lax.psum_scatter(
                values, "blk", scatter_dimension=0, axis_index_groups=head_groups, tiled=True
            ).astype(BF)
            for values in (d_kv, d_mem)
        ]
    d_got = to_heads(
        jnp.concatenate(
            [values.reshape(HEADS, -1, LANES) for values in (d_q, d_kv, d_mem)], axis=1
        )
    )

    mod_rows = width // devices
    ends = jnp.concatenate([sums_mid, sums_last], axis=0)
    ends = jnp.transpose(ends.reshape(4, devices, -1), (1, 0, 2)).reshape(devices, 1, -1)
    packed = mod_rows % 32 == 0 and ends.shape[2] == LANES and spare == 1
    if packed:
        high = ends.astype(BF)
        low = (ends - high.astype(F32)).astype(BF)
        ends = jnp.concatenate([high, low, jnp.zeros((devices, 14, LANES), BF)], axis=1)
    part_patches = HEADS * own_patches
    first_patch = lax.div(blk_at, HEADS) * part_patches
    payload = head_back(
        head,
        d_q,
        d_kv,
        d_mem,
        rows_all,
        lax.dynamic_slice_in_dim(patches_all, first_patch, part_patches, 1)
        if spare > 1
        else patches_all,
        qkv_weight,
        modulation,
        ends if packed else None,
    )
    later = after(later, payload)

    squares_quad = [rights, rights_near, rights_far, xor_blk(rights_far, 1, count_blk)]
    squares_keep, squares_send = product(bit_y, quads, squares, squares_quad)
    squares_given = xor_blk(squares_send, 2, count_blk)

    d_memory_rows = d_got[:, 3 * own :].reshape(HEADS, 2, own_patches, items, HEAD_DIM)
    d_memory_rows = jnp.transpose(d_memory_rows, (3, 2, 1, 0, 4)).reshape(-1, 2 * width)
    d_patches = mm_nt(d_memory_rows, cross_memory)

    def spread(values):
        span = values.shape[0] // devices
        return lax.all_to_all(
            values.reshape(devices, span, values.shape[1]), BOTH, 0, 0, tiled=True
        )

    if packed:
        own_part, terms = payload
        own_part = own_part.reshape((2, HEADS) + own_part.shape[1:])
        own_part = half_x(own_part)
        terms = jnp.broadcast_to(terms, (HEADS,) + terms.shape)
        got = to_heads(jnp.concatenate([own_part, terms], axis=1))
        g_cross_mem, g_qkv, d_modulation, ends = unpack(got, mod_rows, 16)
        ends = (ends[0] + ends[1]).reshape(4, -1)
        others = swap_batch(d_modulation)
        d_modulation = jnp.where(
            batch_at == 0,
            jnp.concatenate([d_modulation, others], axis=0),
            jnp.concatenate([others, d_modulation], axis=0),
        )
    else:
        qkv_product, memory_product, terms = payload
        g_qkv = by_heads(spread(qkv_product).reshape(2 * spare, HEADS, mod_rows, 3 * HEAD_DIM))
        terms = terms.reshape(1, -1, ends.shape[2])
        terms = jnp.broadcast_to(terms, (devices,) + terms.shape[1:])
        small = lax.all_to_all(jnp.concatenate([terms, ends], axis=1), BOTH, 0, 0, tiled=True)
        ends = jnp.sum(small[:, -1], axis=0).reshape(4, -1)
        d_modulation = jnp.sum(small[:, :-1].reshape(2, count_blk, -1), axis=1)
        memory_got = spread(memory_product).astype(F32)
        memory_got = memory_got.reshape(2 * spare, HEADS, mod_rows, 2, HEAD_DIM)
        memory_got = jnp.transpose(jnp.sum(memory_got, axis=0), (1, 2, 0, 3))
        g_cross_mem = memory_got.reshape(mod_rows, 2 * width)
    d_modulation = d_modulation.reshape(2 * items, 2 * width)
    own_cams = lax.optimization_barrier((camera_index, modulation))[0]
    others = swap_batch(own_cams)
    cams = jnp.where(
        batch_at == 0,
        jnp.concatenate([own_cams, others], axis=0),
        jnp.concatenate([others, own_cams], axis=0),
    )
    pick = pick_of(cams)
    code_low = code_of(pick)
    code_rows = lax.dynamic_slice_in_dim(code_low, place * mod_rows, mod_rows, 1).astype(F32)
    g_mod = jnp.sum(code_rows[:, :, None] * d_modulation[:, None, :], axis=0)
    d_code = mm_nt(d_modulation.astype(BF), mod_weight)
    cam_rows = camera_table.shape[0] // devices
    pick_rows = lax.dynamic_slice_in_dim(pick, place * cam_rows, cam_rows, 1)
    g_table = jnp.sum(pick_rows[:, :, None] * d_code[:, None, :], axis=0) / views

    d_triplane = first_back(
        d_got, qkv_weight, triplane, modulation, d_middle.reshape(items, own, width)
    )
    g_up = rest_sum(up_keep, up_given)[0]
    g_down = rest_sum(down_keep, down_given)[0]
    g_squares = rest_sum(squares_keep, squares_given)
    result = later + mm(hidden, down_weight)
    return (
        result.reshape(items, own, width),
        d_triplane,
        d_patches.reshape(items, own_patches, width),
        g_table,
        g_mod,
        g_qkv,
        g_squares[2],
        ends[0],
        ends[1],
        g_squares[1],
        g_cross_mem,
        g_squares[0],
        ends[2],
        ends[3],
        g_up,
        g_down,
    )


def solution(mesh):
    rows = P("batch", "blk", None)
    split = P(BOTH, None)
    line = P(BOTH)
    whole = P()
    return jax.shard_map(
        functools.partial(local, mesh.shape["blk"]),
        mesh=mesh,
        in_specs=(rows, rows, rows, P("batch", None), P("batch"), P("batch")) + (whole,) * 13,
        out_specs=(
            rows,
            rows,
            rows,
            split,
            split,
            split,
            split,
            line,
            line,
            split,
            split,
            split,
            line,
            line,
            split,
            split,
        ),
        check_vma=False,
    )
```

```python
import functools

import jax
import jax.numpy as jnp
from jax import lax
from jax.experimental import pallas as pl
from jax.experimental.pallas import tpu as pltpu
from jax.sharding import PartitionSpec as P

HEADS = 16
HEAD_DIM = 64
LANES = 128
PAIRS = HEADS * HEAD_DIM // LANES
BF = jnp.bfloat16
F32 = jnp.float32
BOTH = ("batch", "blk")
TINY = -1e30
GROUP = 4
WIDE = GROUP * HEAD_DIM
ANYWHERE = pl.BlockSpec(memory_space=pl.ANY)
ROOM = 60 << 20
IN_SMEM = pl.BlockSpec(memory_space=pltpu.SMEM)


def whole(shape):
    return pl.BlockSpec(shape, lambda *at: (0,) * len(shape))


def mm(a, b):
    return jnp.dot(a, b, preferred_element_type=F32)


def mm_nt(a, b):
    return lax.dot_general(a, b, (((1,), (1,)), ((), ())), preferred_element_type=F32)


def mm_tn(a, b):
    return lax.dot_general(a, b, (((0,), (0,)), ((), ())), preferred_element_type=F32)


def center_scale(values):
    center = values - jnp.mean(values, axis=-1, keepdims=True)
    rstd = lax.rsqrt(jnp.mean(center * center, axis=-1, keepdims=True) + 1e-05)
    return center * rstd, rstd


def norm_back(unit, rstd, grad):
    return rstd * (
        grad
        - jnp.mean(grad, axis=-1, keepdims=True)
        - unit * jnp.mean(grad * unit, axis=-1, keepdims=True)
    )


def self_forward_kernel(count_ref, q_ref, k_ref, v_ref, out_ref, lse_ref):
    queries = q_ref[...].reshape(-1, LANES) * BF(HEAD_DIM**-0.5)
    keys = k_ref[...].reshape(-1, LANES)
    values_t = v_ref[...].reshape(-1, LANES).T
    lane = lax.broadcasted_iota(jnp.int32, queries.shape, 1) // HEAD_DIM
    row = lax.broadcasted_iota(jnp.int32, (keys.shape[0], queries.shape[0]), 0)
    parts = []
    for item in range(2):
        mine = jnp.where(lane == item, queries, BF(0))
        scores = jnp.where(row < count_ref[item], mm_nt(keys, mine), TINY)
        top = jnp.max(scores, axis=0, keepdims=True)
        weights = jnp.exp(scores - top)
        total = jnp.sum(weights, axis=0, keepdims=True)
        span = slice(item * HEAD_DIM, (item + 1) * HEAD_DIM)
        parts.append(mm(values_t[span], weights.astype(BF)) / total)
        lse_ref[item : item + 1, :] = top + jnp.log(total)
    out = jnp.concatenate(parts, axis=0).T
    out_ref[...] = out.astype(BF).reshape(out_ref.shape)


def self_backward_kernel(
    steps, count_ref, q_ref, k_ref, v_ref, do_ref, lse_ref, *rest
):
    joined = len(rest) == 4 and len(rest[1].shape) == 3
    dk_acc, dv_acc = rest[-2:]
    step = pl.program_id(0)
    queries = q_ref[...].reshape(-1, LANES) * BF(HEAD_DIM**-0.5)
    keys = k_ref[...].reshape(-1, LANES)
    values = v_ref[...].reshape(-1, LANES)
    keys_t = keys.T
    grads = do_ref[...].reshape(-1, LANES)
    lane = lax.broadcasted_iota(jnp.int32, queries.shape, 1) // HEAD_DIM
    row = lax.broadcasted_iota(jnp.int32, (keys.shape[0], queries.shape[0]), 0)
    parts = []
    d_keys = None
    for item in range(2):
        mine = jnp.where(lane == item, queries, BF(0))
        d_mine = jnp.where(lane == item, grads, BF(0))
        scores = mm_nt(keys, mine)
        probs = jnp.where(
            row < count_ref[item], jnp.exp(scores - lse_ref[item : item + 1, :]), 0.0
        )
        d_probs = mm_nt(values, d_mine)
        delta = jnp.sum(probs * d_probs, axis=0, keepdims=True)
        d_scores = (probs * (d_probs - delta)).astype(BF)
        new_v = mm(probs.astype(BF), d_mine)
        new_k = mm(d_scores, mine)
        d_values = new_v if d_keys is None else d_values + new_v
        d_keys = new_k if d_keys is None else d_keys + new_k
        span = slice(item * HEAD_DIM, (item + 1) * HEAD_DIM)
        parts.append(mm(keys_t[span], d_scores) * HEAD_DIM**-0.5)
    d_q = jnp.concatenate(parts, axis=0).T
    part, own = q_ref.shape[0], q_ref.shape[2]
    if joined:
        mem_ref, out_ref = rest[:2]
        out_ref[pl.ds(step * part, part), :own] = d_q.astype(BF).reshape(part, own, LANES)
    else:
        dq_ref, dkv_ref = rest[:2]
        dq_ref[...] = d_q.astype(BF).reshape(dq_ref.shape)

    @pl.when(step == 0)
    def _():
        dk_acc[...] = d_keys
        dv_acc[...] = d_values

    @pl.when(step > 0)
    def _():
        dk_acc[...] += d_keys
        dv_acc[...] += d_values

    @pl.when(step == steps - 1)
    def _():
        if joined:
            blocks = out_ref.shape[0]
            shape = (blocks, own, LANES)
            out_ref[:, own : 2 * own] = dk_acc[...].astype(BF).reshape(shape)
            out_ref[:, 2 * own : 3 * own] = dv_acc[...].astype(BF).reshape(shape)
            out_ref[:, 3 * own :] = mem_ref[...].reshape(blocks, -1, LANES)
            return
        shape = (dkv_ref.shape[0], 1) + dkv_ref.shape[2:]
        dkv_ref[:, 0:1] = dk_acc[...].astype(dkv_ref.dtype).reshape(shape)
        dkv_ref[:, 1:2] = dv_acc[...].astype(dkv_ref.dtype).reshape(shape)


def q_steps(blocks):
    return 2 if blocks % 2 == 0 else 1


def self_specs(q_arr, kv_arr, first):
    blocks, _, rows, _ = q_arr.shape
    steps = q_steps(blocks)
    part = blocks // steps
    many = kv_arr.shape[0]
    return steps, part, rows, many, [
        pl.BlockSpec(memory_space=pltpu.SMEM),
        pl.BlockSpec((part, 1, rows, LANES), lambda i: (i, 0, 0, 0)),
        pl.BlockSpec((many, 1, rows, LANES), lambda i: (0, first, 0, 0)),
        pl.BlockSpec((many, 1, rows, LANES), lambda i: (0, first + 1, 0, 0)),
    ]


def self_forward(counts, q_arr, kv_arr, first):
    steps, part, rows, many, specs = self_specs(q_arr, kv_arr, first)
    blocks = q_arr.shape[0]
    pairs = blocks * rows * many * rows * 2
    return pl.pallas_call(
        self_forward_kernel,
        grid=(steps,),
        in_specs=specs,
        out_specs=[
            pl.BlockSpec((part, rows, LANES), lambda i: (i, 0, 0)),
            pl.BlockSpec((2, part * rows), lambda i: (0, i)),
        ],
        out_shape=[
            jax.ShapeDtypeStruct((blocks, rows, LANES), BF),
            jax.ShapeDtypeStruct((2, blocks * rows), F32),
        ],
        compiler_params=pltpu.CompilerParams(vmem_limit_bytes=ROOM),
        cost_estimate=pl.CostEstimate(
            flops=pairs * 4 * LANES, bytes_accessed=1 << 20, transcendentals=pairs
        ),
        name="self_forward",
    )(counts, q_arr, kv_arr, kv_arr)


def self_backward(counts, q_arr, kv_arr, first, d_out, lse, d_mem):
    steps, part, rows, many, specs = self_specs(q_arr, kv_arr, first)
    blocks = q_arr.shape[0]
    pairs = blocks * rows * many * rows * 2
    if d_mem is None:
        more = []
        out_specs = [
            pl.BlockSpec((part, 1, rows, LANES), lambda i: (i, 0, 0, 0)),
            whole((many, 2, rows, LANES)),
        ]
        shapes = [
            jax.ShapeDtypeStruct((blocks, 1, rows, LANES), BF),
            jax.ShapeDtypeStruct((many, 2, rows, LANES), F32),
        ]
    else:
        more = [d_mem]
        shape = (blocks, 3 * rows + 2 * d_mem.shape[2], LANES)
        out_specs = whole(shape)
        shapes = jax.ShapeDtypeStruct(shape, BF)
    return pl.pallas_call(
        functools.partial(self_backward_kernel, steps),
        grid=(steps,),
        in_specs=specs
        + [
            pl.BlockSpec((part, 1, rows, LANES), lambda i: (i, 0, 0, 0)),
            pl.BlockSpec((2, part * rows), lambda i: (0, i)),
        ]
        + [whole(values.shape) for values in more],
        out_specs=out_specs,
        out_shape=shapes,
        scratch_shapes=[
            pltpu.VMEM((many * rows, LANES), F32),
            pltpu.VMEM((many * rows, LANES), F32),
        ],
        compiler_params=pltpu.CompilerParams(vmem_limit_bytes=ROOM),
        cost_estimate=pl.CostEstimate(
            flops=pairs * 10 * LANES, bytes_accessed=2 << 20, transcendentals=pairs
        ),
        name="self_backward",
    )(counts, q_arr, kv_arr, kv_arr, d_out, lse, *more)


def stack_heads(block, lane):
    zero = jnp.zeros((), block.dtype)
    return jnp.concatenate(
        [jnp.where(lane == head, block, zero) for head in range(GROUP)], axis=0
    )


def merge_heads(block, lane):
    rows = block.shape[0] // GROUP
    out = block[:rows]
    for head in range(1, GROUP):
        out = jnp.where(lane == head, block[head * rows : (head + 1) * rows], out)
    return out


def cross_forward_kernel(
    count_ref,
    q_ref,
    mem_ref,
    mid_ref,
    gain,
    bias,
    out_hbm,
    out_ref,
    lse_ref,
    later_ref,
    normed_ref,
    out_w,
    sem,
):
    fetch = pltpu.make_async_copy(out_hbm, out_w, sem)
    fetch.start()
    items, rows, width = q_ref.shape
    many = mem_ref.shape[1]
    lane = lax.broadcasted_iota(jnp.int32, (rows, WIDE), 1) // HEAD_DIM
    row = lax.broadcasted_iota(jnp.int32, (many, GROUP * rows), 0)

    def body(group, carry):
        span = pl.ds(pl.multiple_of(group * WIDE, WIDE), WIDE)
        over = pl.ds(pl.multiple_of(width + group * WIDE, WIDE), WIDE)
        for item in range(items):
            queries = stack_heads(q_ref[item, :, span] * BF(HEAD_DIM**-0.5), lane)
            scores = mm_nt(mem_ref[item, :, span], queries)
            scores = jnp.where(row < count_ref[item], scores, TINY)
            top = jnp.max(scores, axis=0, keepdims=True)
            weights = jnp.exp(scores - top)
            total = jnp.sum(weights, axis=0, keepdims=True)
            out = mm(mem_ref[item, :, over].T, weights.astype(BF)) / total
            out_ref[item, :, span] = merge_heads(out.T, lane).astype(BF)
            lse_ref[item, pl.ds(group, 1), : GROUP * rows] = top + jnp.log(total)
        return carry

    lax.fori_loop(0, width // WIDE, body, 0, unroll=2)
    fetch.wait()
    later = mid_ref[...] + mm(out_ref[...].reshape(items * rows, width), out_w[...])
    later_ref[...] = later
    unit, unused = center_scale(later)
    normed_ref[...] = (unit * gain[...] + bias[...]).astype(BF)


def cross_backward_kernel(count_ref, q_ref, mem_ref, do_ref, lse_ref, dq_ref):
    items, rows, width = q_ref.shape
    many = mem_ref.shape[1]
    lane = lax.broadcasted_iota(jnp.int32, (rows, WIDE), 1) // HEAD_DIM
    row = lax.broadcasted_iota(jnp.int32, (many, GROUP * rows), 0)

    def body(group, carry):
        span = pl.ds(pl.multiple_of(group * WIDE, WIDE), WIDE)
        over = pl.ds(pl.multiple_of(width + group * WIDE, WIDE), WIDE)
        for item in range(items):
            queries = stack_heads(q_ref[item, :, span] * BF(HEAD_DIM**-0.5), lane)
            grads = stack_heads(do_ref[item, :, span], lane)
            keys = mem_ref[item, :, span]
            scores = mm_nt(keys, queries)
            lse = lse_ref[item, pl.ds(group, 1), : GROUP * rows]
            probs = jnp.where(row < count_ref[item], jnp.exp(scores - lse), 0.0)
            d_probs = mm_nt(mem_ref[item, :, over], grads)
            delta = jnp.sum(probs * d_probs, axis=0, keepdims=True)
            d_scores = (probs * (d_probs - delta)).astype(BF)
            d_q = mm(keys.T, d_scores) * HEAD_DIM**-0.5
            dq_ref[item, :, span] = merge_heads(d_q.T, lane).astype(BF)
        return carry

    lax.fori_loop(0, width // WIDE, body, 0, unroll=2)


def cross_forward(counts, cross_q, memory, middle, cross_out, gain, bias):
    items, rows, width = cross_q.shape
    many = memory.shape[1]
    pairs = items * rows * HEADS * many
    return pl.pallas_call(
        cross_forward_kernel,
        grid=(1,),
        in_specs=[IN_SMEM]
        + [whole(x.shape) for x in (cross_q, memory, middle)]
        + [whole((1, width))] * 2
        + [ANYWHERE],
        out_specs=[
            whole((items, rows, width)),
            whole((items, width // WIDE, WIDE)),
            whole((items * rows, width)),
            whole((items * rows, width)),
        ],
        out_shape=[
            jax.ShapeDtypeStruct((items, rows, width), BF),
            jax.ShapeDtypeStruct((items, width // WIDE, WIDE), F32),
            jax.ShapeDtypeStruct((items * rows, width), F32),
            jax.ShapeDtypeStruct((items * rows, width), BF),
        ],
        scratch_shapes=[pltpu.VMEM(cross_out.shape, BF), pltpu.SemaphoreType.DMA],
        compiler_params=pltpu.CompilerParams(vmem_limit_bytes=ROOM),
        cost_estimate=pl.CostEstimate(
            flops=pairs * 4 * WIDE, bytes_accessed=3 << 20, transcendentals=pairs
        ),
        name="cross_forward",
    )(counts, cross_q, memory, middle, gain[None], bias[None], cross_out)


def cross_backward(counts, cross_q, memory, d_out, lse):
    items, rows, width = cross_q.shape
    many = memory.shape[1]
    pairs = items * rows * HEADS * many
    return pl.pallas_call(
        cross_backward_kernel,
        grid=(1,),
        in_specs=[IN_SMEM] + [whole(x.shape) for x in (cross_q, memory, d_out, lse)],
        out_specs=whole((items, rows, width)),
        out_shape=jax.ShapeDtypeStruct((items, rows, width), BF),
        compiler_params=pltpu.CompilerParams(vmem_limit_bytes=ROOM),
        cost_estimate=pl.CostEstimate(
            flops=pairs * 10 * WIDE, bytes_accessed=6 << 20, transcendentals=pairs
        ),
        name="cross_backward",
    )(counts, cross_q, memory, d_out, lse)


def memory_back_kernel(head_ref, count_ref, q_ref, do_ref, k_ref, v_ref, out_ref):
    items, many, _ = k_ref.shape
    odd = lax.rem(head_ref[0], 2)
    queries = q_ref[...].reshape(-1, LANES) * BF(HEAD_DIM**-0.5)
    grads = do_ref[...].reshape(-1, LANES)
    lane = lax.broadcasted_iota(jnp.int32, (many, LANES), 1) // HEAD_DIM
    row = lax.broadcasted_iota(jnp.int32, (many, queries.shape[0]), 0)

    def turn(ref, item):
        block = ref[item].astype(F32)
        block = jnp.where(odd == item, block, swap_half(block))
        return jnp.where(lane == item, block, 0.0).astype(BF)

    d_keys = None
    for item in range(items):
        scores = mm_nt(turn(k_ref, item), queries)
        scores = jnp.where(row < count_ref[item], scores, TINY)
        weights = jnp.exp(scores - jnp.max(scores, axis=0, keepdims=True))
        probs = weights * (1.0 / jnp.sum(weights, axis=0, keepdims=True))
        d_probs = mm_nt(turn(v_ref, item), grads)
        delta = jnp.sum(probs * d_probs, axis=0, keepdims=True)
        d_scores = (probs * (d_probs - delta)).astype(BF)
        new_k = mm(d_scores, queries)
        new_v = mm(probs.astype(BF), grads)
        d_values = new_v if d_keys is None else jnp.where(lane == item, new_v, d_values)
        d_keys = new_k if d_keys is None else jnp.where(lane == item, new_k, d_keys)
    shape = (out_ref.shape[0], 1) + out_ref.shape[2:]
    out_ref[:, 0:1] = d_keys.astype(out_ref.dtype).reshape(shape)
    out_ref[:, 1:2] = d_values.astype(out_ref.dtype).reshape(shape)


def memory_back(head, counts, got, memory, part, low):
    blocks, _, own, _ = got.shape
    items, many, double = memory.shape
    pairs = double // 2 // LANES
    work = items * many * blocks * own
    return pl.pallas_call(
        memory_back_kernel,
        grid_spec=pltpu.PrefetchScalarGridSpec(
            num_scalar_prefetch=2,
            grid=(1,),
            in_specs=[
                pl.BlockSpec((blocks, 1, own, LANES), lambda i, h, c: (0, 1, 0, 0)),
                pl.BlockSpec((blocks, 1, own, LANES), lambda i, h, c: (0, 2, 0, 0)),
                pl.BlockSpec((items, many, LANES), lambda i, h, c: (0, 0, lax.div(h[0], 2))),
                pl.BlockSpec(
                    (items, many, LANES), lambda i, h, c: (0, 0, pairs + lax.div(h[0], 2))
                ),
            ],
            out_specs=whole((many // part, 2, part, LANES)),
        ),
        out_shape=jax.ShapeDtypeStruct((many // part, 2, part, LANES), BF if low else F32),
        compiler_params=pltpu.CompilerParams(vmem_limit_bytes=ROOM),
        cost_estimate=pl.CostEstimate(
            flops=work * 8 * LANES, bytes_accessed=2 << 20, transcendentals=work
        ),
        name="memory_back",
    )(head, counts, got, got, memory, memory)


def swap_half(block):
    return pltpu.roll(block, HEAD_DIM, 1)


def first_half(shape):
    return lax.broadcasted_iota(jnp.int32, shape, 1) < HEAD_DIM


def pair_to_heads(block):
    own = block.shape[0] // 2
    left, right = block[:own], block[own:]
    low = first_half(left.shape)
    return (
        jnp.where(low, left, swap_half(right)),
        jnp.where(low, swap_half(left), right),
    )


def project_kernel(tri_ref, mod_ref, q_ref, k_ref, v_ref, out_ref, normed):
    items, own, width = tri_ref.shape

    @pl.when(pl.program_id(0) == 0)
    def _():
        for item in range(items):
            unit, unused = center_scale(tri_ref[item].astype(F32))
            scale = mod_ref[item : item + 1, width:]
            shift = mod_ref[item : item + 1, :width]
            normed[item * own : (item + 1) * own] = (unit * (1.0 + scale) + shift).astype(BF)

    for kind, ref in enumerate((q_ref, k_ref, v_ref)):
        block = mm(normed[...], ref[...])
        for pair in range(WIDE // LANES):
            first, second = pair_to_heads(block[:, pair * LANES : (pair + 1) * LANES])
            out_ref[2 * pair, kind] = first.astype(BF)
            out_ref[2 * pair + 1, kind] = second.astype(BF)


def project(triplane, modulation, qkv_weight):
    items, own, width = triplane.shape
    steps = width // WIDE
    return pl.pallas_call(
        project_kernel,
        grid=(steps,),
        in_specs=[
            pl.BlockSpec((items, own, width), lambda i: (0, 0, 0)),
            pl.BlockSpec((items, 2 * width), lambda i: (0, 0)),
            pl.BlockSpec((width, WIDE), lambda i: (0, i)),
            pl.BlockSpec((width, WIDE), lambda i: (0, steps + i)),
            pl.BlockSpec((width, WIDE), lambda i: (0, 2 * steps + i)),
        ],
        out_specs=pl.BlockSpec((GROUP, 3, own, LANES), lambda i: (i, 0, 0, 0)),
        out_shape=jax.ShapeDtypeStruct((HEADS, 3, own, LANES), BF),
        scratch_shapes=[pltpu.VMEM((items * own, width), BF)],
        compiler_params=pltpu.CompilerParams(vmem_limit_bytes=ROOM),
        cost_estimate=pl.CostEstimate(
            flops=6 * items * own * width * width, bytes_accessed=8 << 20, transcendentals=0
        ),
        name="project",
    )(triplane, modulation, qkv_weight, qkv_weight, qkv_weight)


def middle_kernel(
    got_ref,
    tri_ref,
    gain,
    bias,
    out_hbm,
    query_hbm,
    att_ref,
    mid_ref,
    normed_ref,
    query_ref,
    out_w,
    query_w,
    sems,
):
    fetch_out = pltpu.make_async_copy(out_hbm, out_w, sems.at[0])
    fetch_out.start()
    fetch_query = pltpu.make_async_copy(query_hbm, query_w, sems.at[1])
    fetch_query.start()
    heads, own, _ = got_ref.shape
    for pair in range(heads // 2):
        left = got_ref[2 * pair].astype(F32)
        right = got_ref[2 * pair + 1].astype(F32)
        low = first_half(left.shape)
        span = slice(pair * LANES, (pair + 1) * LANES)
        att_ref[:own, span] = jnp.where(low, left, swap_half(right)).astype(BF)
        att_ref[own:, span] = jnp.where(low, swap_half(left), right).astype(BF)
    fetch_out.wait()
    middle = tri_ref[...].astype(F32) + mm(att_ref[...], out_w[...])
    mid_ref[...] = middle
    unit, unused = center_scale(middle)
    normed = (unit * gain[...] + bias[...]).astype(BF)
    normed_ref[...] = normed
    fetch_query.wait()
    query_ref[...] = mm(normed, query_w[...]).astype(BF)


def middle_part(got, tri_rows, self_out, gain, bias, cross_query):
    rows, width = tri_rows.shape
    low = jax.ShapeDtypeStruct((rows, width), BF)
    return pl.pallas_call(
        middle_kernel,
        grid=(1,),
        in_specs=[whole(got.shape), whole((rows, width)), whole((1, width)), whole((1, width))]
        + [ANYWHERE] * 2,
        out_specs=[whole((rows, width))] * 4,
        out_shape=[low, jax.ShapeDtypeStruct((rows, width), F32), low, low],
        scratch_shapes=[
            pltpu.VMEM(self_out.shape, BF),
            pltpu.VMEM(cross_query.shape, BF),
            pltpu.SemaphoreType.DMA((2,)),
        ],
        compiler_params=pltpu.CompilerParams(vmem_limit_bytes=ROOM),
        cost_estimate=pl.CostEstimate(
            flops=4 * rows * width * width, bytes_accessed=5 << 20, transcendentals=0
        ),
        name="middle_part",
    )(got, tri_rows, gain[None], bias[None], self_out, cross_query)


def middle_back_kernel(
    dq_ref,
    mid_ref,
    gain,
    later_ref,
    query_ref,
    crossed_ref,
    query_hbm,
    out_hbm,
    d_mid_ref,
    low_ref,
    heads_ref,
    sums_ref,
    query_w,
    out_w,
    sems,
):
    fetch_query = pltpu.make_async_copy(query_hbm, query_w, sems.at[0])
    fetch_query.start()
    fetch_out = pltpu.make_async_copy(out_hbm, out_w, sems.at[1])
    fetch_out.start()

    def by_head(values, kind):
        for pair in range(values.shape[1] // LANES):
            block = values[:, pair * LANES : (pair + 1) * LANES].astype(F32)
            first, second = pair_to_heads(block)
            heads_ref[2 * pair, kind] = first.astype(BF)
            heads_ref[2 * pair + 1, kind] = second.astype(BF)

    by_head(query_ref[...], 1)
    by_head(crossed_ref[...], 2)
    fetch_query.wait()
    d_normed = mm_nt(dq_ref[...], query_w[...])
    unit, rstd = center_scale(mid_ref[...])
    sums_ref[0:1] = jnp.sum(d_normed * unit, axis=0, keepdims=True)
    sums_ref[1:2] = jnp.sum(d_normed, axis=0, keepdims=True)
    d_middle = later_ref[...] + norm_back(unit, rstd, d_normed * gain[...])
    d_mid_ref[...] = d_middle
    low = d_middle.astype(BF)
    low_ref[...] = low
    fetch_out.wait()
    by_head(mm_nt(low, out_w[...]), 0)


def middle_back(own, d_query, cross_query, middle, gain, d_later, self_out, cross_q, d_crossed):
    rows, width = middle.shape
    return pl.pallas_call(
        middle_back_kernel,
        grid=(1,),
        in_specs=[whole((rows, width)), whole((rows, width)), whole((1, width))]
        + [whole((rows, width))] * 3
        + [ANYWHERE] * 2,
        out_specs=[
            whole((rows, width)),
            whole((rows, width)),
            whole((HEADS, 3, own, LANES)),
            whole((2, width)),
        ],
        scratch_shapes=[
            pltpu.VMEM(cross_query.shape, BF),
            pltpu.VMEM(self_out.shape, BF),
            pltpu.SemaphoreType.DMA((2,)),
        ],
        out_shape=[
            jax.ShapeDtypeStruct((rows, width), F32),
            jax.ShapeDtypeStruct((rows, width), BF),
            jax.ShapeDtypeStruct((HEADS, 3, own, LANES), BF),
            jax.ShapeDtypeStruct((2, width), F32),
        ],
        compiler_params=pltpu.CompilerParams(vmem_limit_bytes=ROOM),
        cost_estimate=pl.CostEstimate(
            flops=4 * rows * width * width, bytes_accessed=6 << 20, transcendentals=0
        ),
        name="middle_back",
    )(d_query, middle, gain[None], d_later, cross_q, d_crossed, cross_query, self_out)


def first_back_kernel(
    steps, got_ref, q_ref, k_ref, v_ref, tri_ref, mod_ref, mid_ref, out_ref, total
):
    items, own, width = tri_ref.shape
    step = pl.program_id(0)
    added = None
    for kind, ref in enumerate((q_ref, k_ref, v_ref)):
        columns = []
        for pair in range(WIDE // LANES):
            at = slice(kind * own, (kind + 1) * own)
            left = got_ref[2 * pair, at].astype(F32)
            right = got_ref[2 * pair + 1, at].astype(F32)
            low = first_half(left.shape)
            columns.append(
                jnp.concatenate(
                    [
                        jnp.where(low, left, swap_half(right)),
                        jnp.where(low, swap_half(left), right),
                    ],
                    axis=0,
                )
            )
        term = mm_nt(jnp.concatenate(columns, axis=1).astype(BF), ref[...])
        added = term if added is None else added + term

    @pl.when(step == 0)
    def _():
        total[...] = added

    @pl.when(step > 0)
    def _():
        total[...] += added

    @pl.when(step == steps - 1)
    def _():
        for item in range(items):
            unit, rstd = center_scale(tri_ref[item].astype(F32))
            grad = total[item * own : (item + 1) * own] * (1.0 + mod_ref[item : item + 1, width:])
            out_ref[item] = mid_ref[item] + norm_back(unit, rstd, grad)


def first_back(got, qkv_weight, triplane, modulation, d_middle):
    items, own, width = triplane.shape
    steps = width // WIDE
    return pl.pallas_call(
        functools.partial(first_back_kernel, steps),
        grid=(steps,),
        in_specs=[
            pl.BlockSpec((GROUP,) + got.shape[1:], lambda i: (i, 0, 0)),
            pl.BlockSpec((width, WIDE), lambda i: (0, i)),
            pl.BlockSpec((width, WIDE), lambda i: (0, steps + i)),
            pl.BlockSpec((width, WIDE), lambda i: (0, 2 * steps + i)),
            pl.BlockSpec((items, own, width), lambda i: (0, 0, 0)),
            pl.BlockSpec((items, 2 * width), lambda i: (0, 0)),
            pl.BlockSpec((items, own, width), lambda i: (0, 0, 0)),
        ],
        out_specs=pl.BlockSpec((items, own, width), lambda i: (0, 0, 0)),
        out_shape=jax.ShapeDtypeStruct((items, own, width), F32),
        scratch_shapes=[pltpu.VMEM((items * own, width), F32)],
        compiler_params=pltpu.CompilerParams(vmem_limit_bytes=ROOM),
        cost_estimate=pl.CostEstimate(
            flops=6 * items * own * width * width, bytes_accessed=8 << 20, transcendentals=0
        ),
        name="first_back",
    )(got, qkv_weight, qkv_weight, qkv_weight, triplane, modulation, d_middle)


def head_back_kernel(
    packed,
    own,
    head_ref,
    grads_ref,
    tri_ref,
    patch_ref,
    q_ref,
    k_ref,
    v_ref,
    mod_ref,
    *rest,
):
    units = rest[-1]
    items, many, width = tri_ref.shape
    odd = lax.rem(head_ref[0], 2) == 1
    grads = [
        grads_ref[:, kind * own : (kind + 1) * own].reshape(many, LANES).astype(F32).T
        for kind in range(3)
    ]
    weight = []
    for ref in (q_ref, k_ref, v_ref):
        turned = ref[...].astype(F32).T
        weight.append(jnp.where(odd, turned[HEAD_DIM:], turned[:HEAD_DIM]))
    weight = jnp.concatenate(weight, axis=0)
    product = None
    terms = []
    for item in range(items):
        unit, unused = center_scale(tri_ref[item].astype(F32))
        units[...] = unit.astype(BF)
        span = slice(item * HEAD_DIM, (item + 1) * HEAD_DIM)
        mine = jnp.concatenate([part[span] for part in grads], axis=0)
        outer = mm(mine.astype(BF), units[...])
        column = jnp.sum(mine, axis=1, keepdims=True)
        shift = mod_ref[item : item + 1, :width]
        scale = mod_ref[item : item + 1, width:]
        terms.append(jnp.sum(column * weight, axis=0, keepdims=True))
        terms.append(jnp.sum(outer * weight, axis=0, keepdims=True))
        term = outer * (1.0 + scale) + column * shift
        product = term if product is None else product + term
    product = product.T
    patch_rows = patch_ref.shape[1]
    few = patch_rows // grads_ref.shape[0]
    grads = [
        grads_ref[:, 3 * own + kind * few : 3 * own + (kind + 1) * few]
        .reshape(patch_rows, LANES)
        .astype(F32)
        .T
        for kind in range(2)
    ]
    memory = None
    for item in range(items):
        span = slice(item * HEAD_DIM, (item + 1) * HEAD_DIM)
        mine = jnp.concatenate([part[span] for part in grads], axis=0).astype(BF)
        term = mm(mine, patch_ref[item])
        memory = term if memory is None else memory + term
    memory = memory.T
    if not packed:
        out_ref, memory_ref, terms_ref = rest[:3]
        out_ref[...] = product.astype(BF)
        memory_ref[...] = memory.astype(BF)
        for item in range(items):
            terms_ref[item : item + 1, :width] = terms[2 * item]
            terms_ref[item : item + 1, width:] = terms[2 * item + 1]
        return
    ends_ref, out_ref, terms_ref, unused = rest
    devices = out_ref.shape[0]
    span = width // devices
    product = product.reshape(devices, span, 3 * HEAD_DIM).astype(BF)
    out_ref[:, :span] = memory.reshape(devices, span, LANES).astype(BF)
    out_ref[:, span : 2 * span] = product[:, :, :LANES]
    last = product[:, :, LANES:]
    at = 2 * span + span // 2
    out_ref[:, 2 * span : at] = jnp.concatenate(
        [last[:, : span // 2], last[:, span // 2 :]], axis=2
    )
    out_ref[:, at:] = ends_ref[...]
    lines = [
        term[:, k * LANES : (k + 1) * LANES] for term in terms for k in range(width // LANES)
    ]
    terms_ref[...] = jnp.concatenate(lines, axis=0).astype(BF)


def head_back(head, grads, own, rows_all, patch_part, qkv_weight, modulation, ends):
    items, many, width = rows_all.shape
    pairs = width // LANES
    product = jax.ShapeDtypeStruct((width, 3 * HEAD_DIM), BF)
    if ends is None:
        more = []
        shapes = [
            product,
            jax.ShapeDtypeStruct((width, LANES), BF),
            jax.ShapeDtypeStruct((items, 2 * width), F32),
        ]
    else:
        devices, tail, _ = ends.shape
        more = [ends]
        many_rows = 5 * width // devices // 2 + tail
        shapes = [
            jax.ShapeDtypeStruct((devices, many_rows, LANES), BF),
            jax.ShapeDtypeStruct((2 * items * pairs, LANES), BF),
        ]

    def whole_block(shape):
        return pl.BlockSpec(shape, lambda i, h: (0,) * len(shape))

    return pl.pallas_call(
        functools.partial(head_back_kernel, ends is not None, own),
        grid_spec=pltpu.PrefetchScalarGridSpec(
            num_scalar_prefetch=1,
            grid=(1,),
            in_specs=[
                whole_block(grads.shape),
                pl.BlockSpec((items, many, width), lambda i, h: (0, 0, 0)),
                whole_block(patch_part.shape),
                pl.BlockSpec((width, LANES), lambda i, h: (0, lax.div(h[0], 2))),
                pl.BlockSpec((width, LANES), lambda i, h: (0, pairs + lax.div(h[0], 2))),
                pl.BlockSpec((width, LANES), lambda i, h: (0, 2 * pairs + lax.div(h[0], 2))),
                whole_block((items, 2 * width)),
            ]
            + [whole_block(array.shape) for array in more],
            out_specs=[whole_block(shape.shape) for shape in shapes],
            scratch_shapes=[pltpu.VMEM((many, width), BF)],
        ),
        out_shape=shapes,
        compiler_params=pltpu.CompilerParams(vmem_limit_bytes=ROOM),
        cost_estimate=pl.CostEstimate(
            flops=6 * items * many * width * HEAD_DIM, bytes_accessed=5 << 20, transcendentals=0
        ),
        name="head_back",
    )(
        head,
        grads,
        rows_all,
        patch_part,
        qkv_weight,
        qkv_weight,
        qkv_weight,
        modulation,
        *more,
    )


def by_heads_kernel(got_ref, out_ref):
    parts, heads, rows, _ = got_ref.shape
    width = heads * HEAD_DIM
    for pair in range(heads // 2):
        left = got_ref[0, 2 * pair].astype(F32)
        right = got_ref[0, 2 * pair + 1].astype(F32)
        for part in range(1, parts):
            left = left + got_ref[part, 2 * pair].astype(F32)
            right = right + got_ref[part, 2 * pair + 1].astype(F32)
        for kind in range(3):
            span = slice(kind * HEAD_DIM, (kind + 1) * HEAD_DIM)
            at = kind * width + pair * LANES
            out_ref[:, at : at + LANES] = jnp.concatenate([left[:, span], right[:, span]], axis=1)


def by_heads(got):
    parts, heads, rows, features = got.shape
    return pl.pallas_call(
        by_heads_kernel,
        grid=(1,),
        in_specs=[whole(got.shape)],
        out_specs=whole((rows, heads * features)),
        out_shape=jax.ShapeDtypeStruct((rows, heads * features), F32),
        compiler_params=pltpu.CompilerParams(vmem_limit_bytes=ROOM),
        name="by_heads",
    )(got)


def unpack_kernel(tail, got_ref, mem_ref, qkv_ref, mod_ref, ends_ref):
    span = qkv_ref.shape[0]
    width = HEADS * HEAD_DIM
    at = 2 * span + span // 2

    def columns(head):
        full = got_ref[head, :at].astype(F32)
        last = full[2 * span :]
        last = jnp.concatenate([last[:, :HEAD_DIM], last[:, HEAD_DIM:]], axis=0)
        first, second = full[:span], full[span : 2 * span]
        return (
            first[:, :HEAD_DIM],
            first[:, HEAD_DIM:],
            second[:, :HEAD_DIM],
            second[:, HEAD_DIM:],
            last,
        )

    for pair in range(HEADS // 2):
        both = [
            jnp.concatenate(sides, axis=1)
            for sides in zip(columns(2 * pair), columns(2 * pair + 1))
        ]
        for kind in range(2):
            start = kind * width + pair * LANES
            mem_ref[:, start : start + LANES] = both[kind]
        for kind in range(3):
            start = kind * width + pair * LANES
            qkv_ref[:, start : start + LANES] = both[2 + kind]
    total = got_ref[0, at:].astype(F32)
    for head in range(1, HEADS):
        total = total + got_ref[head, at:].astype(F32)
    ends_ref[...] = total[:tail]
    mod_ref[...] = total[tail:]


def unpack(got, span, tail):
    _, many, _ = got.shape
    shapes = [
        (span, 2 * HEADS * HEAD_DIM),
        (span, 3 * HEADS * HEAD_DIM),
        (many - tail - 2 * span - span // 2, LANES),
        (tail, LANES),
    ]
    return pl.pallas_call(
        functools.partial(unpack_kernel, tail),
        grid=(1,),
        in_specs=[whole(got.shape)],
        out_specs=[whole(shape) for shape in shapes],
        out_shape=[jax.ShapeDtypeStruct(shape, F32) for shape in shapes],
        compiler_params=pltpu.CompilerParams(vmem_limit_bytes=ROOM),
        name="unpack",
    )(got)


def gather_lanes(block, starts, span):
    out = []
    lane = lax.broadcasted_iota(jnp.int32, (block.shape[0], LANES), 1)
    for at in range(0, len(starts) * span, LANES):
        merged = None
        for to in range(0, LANES, min(span, LANES)):
            start = starts[(at + to) // span] + (at + to) % span
            base = start // LANES * LANES
            part = block[:, base : base + LANES]
            shift = (to - (start - base)) % LANES
            if shift:
                part = pltpu.roll(part, shift, 1)
            if merged is None:
                merged = part
            else:
                merged = jnp.where((lane >= to) & (lane < to + span), part, merged)
        out.append(merged)
    return jnp.concatenate(out, axis=1)


def starts_y(features, devices, quarter):
    span = features // devices
    return [(group * 4 + quarter) * span for group in range(devices // 4)]


def starts_x(features, devices, half, low):
    span = features // devices
    many = devices // 2
    return [
        (half * many + rest * 4 + y * 2 + low) * span
        for y in range(2)
        for rest in range(many // 4)
    ]


def mlp_kernel(
    steps,
    devices,
    normed_ref,
    dh_ref,
    up_ref,
    later_ref,
    c_ref,
    gain,
    out_hbm,
    hidden_ref,
    pre_ref,
    up_piece_ref,
    down_piece_ref,
    d_later_ref,
    low_ref,
    d_crossed_ref,
    sums_ref,
    total,
    out_w,
    sem,
):
    step = pl.program_id(0)
    fetch = pltpu.make_async_copy(out_hbm, out_w, sem)

    @pl.when(step == 0)
    def _():
        fetch.start()
        values = normed_ref[...].astype(F32)
        for quarter in range(4):
            starts = starts_y(values.shape[1], devices, quarter)
            span = values.shape[1] // devices
            up_piece_ref[quarter] = gather_lanes(values, starts, span).astype(BF)

    pre = mm(normed_ref[...], up_ref[...])
    square = pre * pre
    slope = (2.0 / 3.141592653589793) ** 0.5
    turn = jnp.tanh(slope * (pre + 0.044715 * (pre * square)))
    hidden = 0.5 * pre * (1.0 + turn)
    hidden_ref[...] = hidden.astype(BF)
    part = hidden.shape[1]
    span = part * steps // devices
    half = lax.div(step, steps // 2)
    for low in range(2):
        for y in range(2):
            starts = [(rest * 4 + y * 2 + low) * span for rest in range(part // (4 * span))]
            at = y * (part * steps // 8) + lax.rem(step, steps // 2) * (part // 4)
            at = pl.ds(pl.multiple_of(at, LANES), part // 4)
            down_piece_ref[2 * half + low, :, at] = gather_lanes(hidden, starts, span).astype(BF)
    change = 0.5 * (1.0 + turn) + 0.5 * pre * (1.0 - turn * turn) * (
        slope * (1.0 + 3.0 * 0.044715 * square)
    )
    d_pre = (dh_ref[...] * change).astype(BF)
    pre_ref[...] = d_pre
    added = mm_nt(d_pre, up_ref[...])

    @pl.when(step == 0)
    def _():
        total[...] = added

    @pl.when(step > 0)
    def _():
        total[...] += added

    @pl.when(step == steps - 1)
    def _():
        d_normed = total[...]
        unit, rstd = center_scale(later_ref[...])
        sums_ref[0:1] = jnp.sum(d_normed * unit, axis=0, keepdims=True)
        sums_ref[1:2] = jnp.sum(d_normed, axis=0, keepdims=True)
        d_later = c_ref[...].astype(F32) + norm_back(unit, rstd, d_normed * gain[...])
        d_later_ref[...] = d_later
        low = d_later.astype(BF)
        low_ref[...] = low
        fetch.wait()
        d_crossed_ref[...] = mm_nt(low, out_w[...]).astype(BF)


def mlp(devices, normed, d_hidden, up_weight, later, grad_out, gain, cross_out):
    rows, width = normed.shape
    hidden_width = up_weight.shape[1]
    part = min(1024, hidden_width)
    steps = hidden_width // part
    low = jax.ShapeDtypeStruct((rows, width), BF)
    return pl.pallas_call(
        functools.partial(mlp_kernel, steps, devices),
        grid=(steps,),
        in_specs=[
            whole((rows, width)),
            pl.BlockSpec((rows, part), lambda i: (0, i)),
            pl.BlockSpec((width, part), lambda i: (0, i)),
            whole((rows, width)),
            whole((rows, width)),
            whole((1, width)),
            ANYWHERE,
        ],
        out_specs=[
            pl.BlockSpec((rows, part), lambda i: (0, i)),
            pl.BlockSpec((rows, part), lambda i: (0, i)),
            whole((4, rows, width // 4)),
            whole((4, rows, hidden_width // 4)),
            whole((rows, width)),
            whole((rows, width)),
            whole((rows, width)),
            whole((2, width)),
        ],
        out_shape=[
            jax.ShapeDtypeStruct((rows, hidden_width), BF),
            jax.ShapeDtypeStruct((rows, hidden_width), BF),
            jax.ShapeDtypeStruct((4, rows, width // 4), BF),
            jax.ShapeDtypeStruct((4, rows, hidden_width // 4), BF),
            jax.ShapeDtypeStruct((rows, width), F32),
            low,
            low,
            jax.ShapeDtypeStruct((2, width), F32),
        ],
        scratch_shapes=[
            pltpu.VMEM((rows, width), F32),
            pltpu.VMEM((width, width), BF),
            pltpu.SemaphoreType.DMA,
        ],
        compiler_params=pltpu.CompilerParams(vmem_limit_bytes=ROOM),
        cost_estimate=pl.CostEstimate(
            flops=4 * rows * width * hidden_width,
            bytes_accessed=12 << 20,
            transcendentals=rows * hidden_width,
        ),
        name="mlp",
    )(normed, d_hidden, up_weight, later, grad_out, gain[None], cross_out)


def pieces_kernel(devices, *refs):
    out_ref = refs[-1]
    for k, ref in enumerate(refs[:-1]):
        values = ref[...].astype(F32)
        span = values.shape[1] // devices
        for half in range(2):
            for low in range(2):
                starts = starts_x(values.shape[1], devices, half, low)
                out_ref[2 * half + low, k] = gather_lanes(values, starts, span).astype(BF)


def pieces(devices, *arrays):
    rows, width = arrays[0].shape
    return pl.pallas_call(
        functools.partial(pieces_kernel, devices),
        grid=(1,),
        in_specs=[whole((rows, width))] * len(arrays),
        out_specs=whole((4, len(arrays), rows, width // 4)),
        out_shape=jax.ShapeDtypeStruct((4, len(arrays), rows, width // 4), BF),
        compiler_params=pltpu.CompilerParams(vmem_limit_bytes=ROOM),
        name="pieces",
    )(*arrays)


def product_kernel(half_ref, *refs):
    x_refs, y_refs, (keep_ref, send_ref, left, right) = refs[:4], refs[4:8], refs[8:]
    rows = x_refs[0].shape[1]

    @pl.when(pl.program_id(1) == 0)
    def _():
        for k, ref in enumerate(x_refs):
            left[k * rows : (k + 1) * rows] = ref[0]

    for k, ref in enumerate(y_refs):
        right[k * rows : (k + 1) * rows] = ref[0]
    wide = left.shape[1] // 2
    half = half_ref[0]
    for ref, which in ((keep_ref, half), (send_ref, 1 - half)):
        at = pl.ds(pl.multiple_of(which * wide, LANES), wide)
        ref[...] = mm_tn(left[:, at], right[...]).astype(BF).reshape(ref.shape)


def product(half, quads, left, right):
    entries, rows, wide = left[0].shape
    columns = right[0].shape[2]
    span = wide // (2 * quads)
    part = min(columns, 1024)
    shape = jax.ShapeDtypeStruct((quads, entries, span, columns), BF)
    spec = pl.BlockSpec((quads, 1, span, part), lambda e, i: (0, e, 0, i))
    return pl.pallas_call(
        product_kernel,
        grid=(entries, columns // part),
        in_specs=[IN_SMEM]
        + [pl.BlockSpec((1, rows, wide), lambda e, i: (e, 0, 0))] * 4
        + [pl.BlockSpec((1, rows, part), lambda e, i: (e, 0, i))] * 4,
        out_specs=[spec, spec],
        out_shape=[shape, shape],
        scratch_shapes=[pltpu.VMEM((4 * rows, wide), BF), pltpu.VMEM((4 * rows, part), BF)],
        compiler_params=pltpu.CompilerParams(vmem_limit_bytes=ROOM),
        cost_estimate=pl.CostEstimate(
            flops=8 * entries * rows * wide * columns, bytes_accessed=8 << 20, transcendentals=0
        ),
        name="product",
    )(half.reshape(1).astype(jnp.int32), *left, *right)


def xor_blk(values, bit, count):
    return lax.ppermute(values, "blk", [(i, i ^ bit) for i in range(count)])


def swap_batch(values):
    return lax.ppermute(values, "batch", [(0, 1), (1, 0)])


def after(values, *first):
    return lax.optimization_barrier((values, first))[0]


def take(values, index, axis):
    return lax.dynamic_index_in_dim(values, index, axis, keepdims=False)


def local(
    count_blk,
    triplane,
    patches,
    cotangent,
    camera_index,
    triplane_count,
    patch_count,
    camera_table,
    mod_weight,
    qkv_weight,
    self_out,
    gain_mid,
    bias_mid,
    cross_query,
    cross_memory,
    cross_out,
    gain_last,
    bias_last,
    up_weight,
    down_weight,
):
    items, own, width = triplane.shape
    own_patches = patches.shape[1]
    rows = items * own
    spare = count_blk // HEADS
    quads = count_blk // 4
    devices = 2 * count_blk
    row_groups = (
        None
        if spare == 1
        else [[part * HEADS + head for head in range(HEADS)] for part in range(spare)]
    )
    head_groups = [[part * HEADS + head for part in range(spare)] for head in range(HEADS)]
    batch_at = lax.axis_index("batch")
    blk_at = lax.axis_index("blk")
    head_at = lax.rem(blk_at, HEADS)
    place = batch_at * count_blk + blk_at

    def to_heads(values):
        return lax.all_to_all(values, "blk", 0, 0, axis_index_groups=row_groups, tiled=True)

    def swap_corner(values):
        return lax.ppermute(
            values,
            BOTH,
            [
                (b * count_blk + j, (1 - b) * count_blk + (j ^ 1))
                for b in range(2)
                for j in range(count_blk)
            ],
        )

    def quad_y(values):
        far = xor_blk(values, 2, count_blk)
        return [values, xor_blk(values, 1, count_blk), far, xor_blk(far, 1, count_blk)]

    def quad_x(values):
        far = swap_batch(values)
        return [values, xor_blk(values, 1, count_blk), far, xor_blk(far, 1, count_blk)]

    def exchange_y(cut):
        low = jnp.bitwise_and(blk_at, 3)
        got = [take(cut, low, 0)]
        for bit in (1, 2, 3):
            got.append(xor_blk(take(cut, jnp.bitwise_xor(low, bit), 0), bit, count_blk))
        return got

    def exchange_x(cut):
        low = jnp.bitwise_and(blk_at, 1)
        return [
            take(cut, 2 * batch_at + low, 0),
            xor_blk(take(cut, 2 * batch_at + 1 - low, 0), 1, count_blk),
            swap_batch(take(cut, 2 * (1 - batch_at) + low, 0)),
            swap_corner(take(cut, 2 * (1 - batch_at) + 1 - low, 0)),
        ]

    def half_x(values):
        given = swap_batch(take(values, 1 - batch_at, 0))
        return (take(values, batch_at, 0).astype(F32) + given.astype(F32)).astype(BF)

    def rest_sum(keep, given):
        many = quads
        bit = 4
        while many > 1:
            low = jnp.bitwise_and(lax.div(blk_at, bit), 1)
            shape = (many // 2, 2) + keep.shape[1:]
            keep, given = keep.reshape(shape), given.reshape(shape)

            def part(index):
                total = take(keep, index, 1).astype(F32) + take(given, index, 1).astype(F32)
                return total.astype(BF)

            keep, given = part(low), xor_blk(part(1 - low), bit, count_blk)
            many //= 2
            bit *= 2
        return (keep.astype(F32) + given.astype(F32))[0]

    views = camera_index.shape[1]
    table_rows = jnp.arange(camera_table.shape[0], dtype=jnp.int32)

    def pick_of(cams):
        return jnp.sum((cams[:, :, None] == table_rows[None, None, :]).astype(F32), axis=1)

    def code_of(pick):
        return (mm(pick.astype(BF), camera_table) / views).astype(BF)

    modulation = mm(code_of(pick_of(camera_index)), mod_weight)
    sent = project(triplane, modulation, qkv_weight)
    qkv = to_heads(sent)

    patches_all = lax.all_gather(patches, "blk", axis=1, tiled=True)
    bit_y = jnp.bitwise_and(lax.div(blk_at, 2), 1)
    many_patches = patches_all.shape[1]
    memory = (
        mm(patches_all.reshape(items * many_patches, width), cross_memory)
        .astype(BF)
        .reshape(items, many_patches, 2 * width)
    )
    grad_out = cotangent.reshape(rows, width)
    d_hidden = mm_nt(grad_out, down_weight)
    grad_quad = quad_x(lax.optimization_barrier((grad_out, sent))[0])

    qkv, d_hidden = lax.optimization_barrier((qkv, d_hidden))
    if spare == 1:
        kv, kv_first = qkv, 1
    else:
        kv = lax.all_gather(qkv[:, 1:], "blk", axis=0, axis_index_groups=head_groups, tiled=True)
        kv_first = 0
    attended_heads, self_lse = self_forward(triplane_count, qkv, kv, kv_first)
    attended_got = to_heads(attended_heads)
    kept = lax.optimization_barrier((triplane, attended_heads))[0]
    rows_all = lax.all_gather(kept, "blk", axis=1, axis_index_groups=row_groups, tiled=True)

    attended_got, memory, grad_quad = lax.optimization_barrier(
        (attended_got, memory, grad_quad)
    )
    attended_low, middle, normed_mid, cross_q = middle_part(
        attended_got, triplane.reshape(rows, width), self_out, gain_mid, bias_mid, cross_query
    )
    cross_q = cross_q.reshape(items, own, width)
    crossed, cross_lse, later, normed_last = cross_forward(
        patch_count, cross_q, memory, middle, cross_out, gain_last, bias_last
    )
    hidden, d_pre, last_pieces, hidden_pieces, d_later, d_later_low, d_crossed, sums_last = mlp(
        devices, normed_last, d_hidden, up_weight, later, grad_out, gain_last, cross_out
    )
    pre_far = xor_blk(d_pre, 2, count_blk)
    pre_near = xor_blk(d_pre, 1, count_blk)
    last_pieces = exchange_y(last_pieces)
    hidden_pieces = exchange_x(hidden_pieces)

    d_cross_q = cross_backward(
        patch_count, cross_q, memory, d_crossed.reshape(items, own, width), cross_lse
    )
    d_cross_low = d_cross_q.reshape(rows, width)
    d_middle, d_middle_low, back_heads, sums_mid = middle_back(
        own,
        d_cross_low,
        cross_query,
        middle,
        gain_mid,
        d_later,
        self_out,
        cross_q.reshape(rows, width),
        d_crossed,
    )
    pre_quad = [d_pre, pre_near, pre_far, xor_blk(pre_far, 1, count_blk)]
    back_heads = to_heads(back_heads)

    up_keep, up_send = product(
        batch_at, quads, [p[None] for p in last_pieces], [p[None] for p in pre_quad]
    )
    down_keep, down_send = product(
        bit_y, quads, [p[None] for p in hidden_pieces], [p[None] for p in grad_quad]
    )
    up_given = swap_batch(up_send)
    down_given = xor_blk(down_send, 2, count_blk)
    lefts, rights = after(
        (
            (crossed.reshape(rows, width), normed_mid, attended_low),
            (d_later_low, d_cross_low, d_middle_low),
        ),
        d_middle_low,
    )
    squares = exchange_x(pieces(devices, *lefts))
    rights = jnp.stack(rights)
    rights_far = swap_batch(rights)
    rights_near = xor_blk(rights, 1, count_blk)

    head = head_at.reshape(1).astype(jnp.int32)
    d_mem = memory_back(head, patch_count, back_heads, memory, own_patches, spare == 1)
    if spare == 1:
        d_heads = self_backward(triplane_count, qkv, kv, kv_first, back_heads, self_lse, d_mem)
    else:
        d_q, d_kv = self_backward(
            triplane_count, qkv, kv, kv_first, back_heads, self_lse, None
        )
        d_kv, d_mem = [
            lax.psum_scatter(
                values, "blk", scatter_dimension=0, axis_index_groups=head_groups, tiled=True
            ).astype(BF)
            for values in (d_kv, d_mem)
        ]
        d_heads = jnp.concatenate(
            [values.reshape(HEADS, -1, LANES) for values in (d_q, d_kv, d_mem)], axis=1
        )
    d_got = to_heads(d_heads)

    mod_rows = width // devices
    ends = jnp.concatenate([sums_mid, sums_last], axis=0)
    ends = jnp.transpose(ends.reshape(4, devices, -1), (1, 0, 2)).reshape(devices, 1, -1)
    packed = mod_rows % 32 == 0 and ends.shape[2] == LANES and spare == 1
    if packed:
        high = ends.astype(BF)
        low = (ends - high.astype(F32)).astype(BF)
        ends = jnp.concatenate([high, low, jnp.zeros((devices, 14, LANES), BF)], axis=1)
    part_patches = HEADS * own_patches
    first_patch = lax.div(blk_at, HEADS) * part_patches
    payload = head_back(
        head,
        d_heads,
        own,
        rows_all,
        lax.dynamic_slice_in_dim(patches_all, first_patch, part_patches, 1)
        if spare > 1
        else patches_all,
        qkv_weight,
        modulation,
        ends if packed else None,
    )
    later = after(later, payload)

    squares_quad = [rights, rights_near, rights_far, xor_blk(rights_far, 1, count_blk)]
    squares_keep, squares_send = product(bit_y, quads, squares, squares_quad)
    squares_given = xor_blk(squares_send, 2, count_blk)

    d_memory_rows = d_got[:, 3 * own :].reshape(HEADS, 2, own_patches, items, HEAD_DIM)
    d_memory_rows = jnp.transpose(d_memory_rows, (3, 2, 1, 0, 4)).reshape(-1, 2 * width)
    d_patches = mm_nt(d_memory_rows, cross_memory)

    def spread(values):
        span = values.shape[0] // devices
        return lax.all_to_all(
            values.reshape(devices, span, values.shape[1]), BOTH, 0, 0, tiled=True
        )

    if packed:
        own_part, terms = payload
        own_part = own_part.reshape((2, HEADS) + own_part.shape[1:])
        own_part = half_x(own_part)
        terms = jnp.broadcast_to(terms, (HEADS,) + terms.shape)
        got = to_heads(jnp.concatenate([own_part, terms], axis=1))
        g_cross_mem, g_qkv, d_modulation, ends = unpack(got, mod_rows, 16)
        ends = (ends[0] + ends[1]).reshape(4, -1)
        others = swap_batch(d_modulation)
        d_modulation = jnp.where(
            batch_at == 0,
            jnp.concatenate([d_modulation, others], axis=0),
            jnp.concatenate([others, d_modulation], axis=0),
        )
    else:
        qkv_product, memory_product, terms = payload
        g_qkv = by_heads(spread(qkv_product).reshape(2 * spare, HEADS, mod_rows, 3 * HEAD_DIM))
        terms = terms.reshape(1, -1, ends.shape[2])
        terms = jnp.broadcast_to(terms, (devices,) + terms.shape[1:])
        small = lax.all_to_all(jnp.concatenate([terms, ends], axis=1), BOTH, 0, 0, tiled=True)
        ends = jnp.sum(small[:, -1], axis=0).reshape(4, -1)
        d_modulation = jnp.sum(small[:, :-1].reshape(2, count_blk, -1), axis=1)
        memory_got = spread(memory_product).astype(F32)
        memory_got = memory_got.reshape(2 * spare, HEADS, mod_rows, 2, HEAD_DIM)
        memory_got = jnp.transpose(jnp.sum(memory_got, axis=0), (1, 2, 0, 3))
        g_cross_mem = memory_got.reshape(mod_rows, 2 * width)
    d_modulation = d_modulation.reshape(2 * items, 2 * width)
    own_cams = lax.optimization_barrier((camera_index, modulation))[0]
    others = swap_batch(own_cams)
    cams = jnp.where(
        batch_at == 0,
        jnp.concatenate([own_cams, others], axis=0),
        jnp.concatenate([others, own_cams], axis=0),
    )
    pick = pick_of(cams)
    code_low = code_of(pick)
    code_rows = lax.dynamic_slice_in_dim(code_low, place * mod_rows, mod_rows, 1).astype(F32)
    g_mod = jnp.sum(code_rows[:, :, None] * d_modulation[:, None, :], axis=0)
    d_code = mm_nt(d_modulation.astype(BF), mod_weight)
    cam_rows = camera_table.shape[0] // devices
    pick_rows = lax.dynamic_slice_in_dim(pick, place * cam_rows, cam_rows, 1)
    g_table = jnp.sum(pick_rows[:, :, None] * d_code[:, None, :], axis=0) / views

    d_triplane = first_back(
        d_got, qkv_weight, triplane, modulation, d_middle.reshape(items, own, width)
    )
    g_up = rest_sum(up_keep, up_given)[0]
    g_down = rest_sum(down_keep, down_given)[0]
    g_squares = rest_sum(squares_keep, squares_given)
    result = later + mm(hidden, down_weight)
    return (
        result.reshape(items, own, width),
        d_triplane,
        d_patches.reshape(items, own_patches, width),
        g_table,
        g_mod,
        g_qkv,
        g_squares[2],
        ends[0],
        ends[1],
        g_squares[1],
        g_cross_mem,
        g_squares[0],
        ends[2],
        ends[3],
        g_up,
        g_down,
    )


def solution(mesh):
    rows = P("batch", "blk", None)
    split = P(BOTH, None)
    line = P(BOTH)
    whole = P()
    return jax.shard_map(
        functools.partial(local, mesh.shape["blk"]),
        mesh=mesh,
        in_specs=(rows, rows, rows, P("batch", None), P("batch"), P("batch")) + (whole,) * 13,
        out_specs=(
            rows,
            rows,
            rows,
            split,
            split,
            split,
            split,
            line,
            line,
            split,
            split,
            split,
            line,
            line,
            split,
            split,
        ),
        check_vma=False,
    )
```

```python
import functools

import jax
import jax.numpy as jnp
from jax import lax
from jax.experimental import pallas as pl
from jax.experimental.pallas import tpu as pltpu
from jax.sharding import PartitionSpec as P

HEADS = 16
HEAD_DIM = 64
LANES = 128
PAIRS = HEADS * HEAD_DIM // LANES
BF = jnp.bfloat16
F32 = jnp.float32
BOTH = ("batch", "blk")
TINY = -1e30
GROUP = 4
WIDE = GROUP * HEAD_DIM
ANYWHERE = pl.BlockSpec(memory_space=pl.ANY)
ROOM = 60 << 20
IN_SMEM = pl.BlockSpec(memory_space=pltpu.SMEM)


def whole(shape):
    return pl.BlockSpec(shape, lambda *at: (0,) * len(shape))


def mm(a, b):
    return jnp.dot(a, b, preferred_element_type=F32)


def mm_nt(a, b):
    return lax.dot_general(a, b, (((1,), (1,)), ((), ())), preferred_element_type=F32)


def mm_tn(a, b):
    return lax.dot_general(a, b, (((0,), (0,)), ((), ())), preferred_element_type=F32)


def center_scale(values):
    center = values - jnp.mean(values, axis=-1, keepdims=True)
    rstd = lax.rsqrt(jnp.mean(center * center, axis=-1, keepdims=True) + 1e-05)
    return center * rstd, rstd


def norm_back(unit, rstd, grad):
    return rstd * (
        grad
        - jnp.mean(grad, axis=-1, keepdims=True)
        - unit * jnp.mean(grad * unit, axis=-1, keepdims=True)
    )


def self_forward_kernel(count_ref, q_ref, k_ref, v_ref, out_ref, lse_ref):
    queries = q_ref[...].reshape(-1, LANES) * BF(HEAD_DIM**-0.5)
    keys = k_ref[...].reshape(-1, LANES)
    values_t = v_ref[...].reshape(-1, LANES).T
    lane = lax.broadcasted_iota(jnp.int32, queries.shape, 1) // HEAD_DIM
    row = lax.broadcasted_iota(jnp.int32, (keys.shape[0], queries.shape[0]), 0)
    parts = []
    for item in range(2):
        mine = jnp.where(lane == item, queries, BF(0))
        scores = jnp.where(row < count_ref[item], mm_nt(keys, mine), TINY)
        top = jnp.max(scores, axis=0, keepdims=True)
        weights = jnp.exp(scores - top)
        total = jnp.sum(weights, axis=0, keepdims=True)
        span = slice(item * HEAD_DIM, (item + 1) * HEAD_DIM)
        parts.append(mm(values_t[span], weights.astype(BF)) / total)
        lse_ref[item : item + 1, :] = top + jnp.log(total)
    out = jnp.concatenate(parts, axis=0).T
    out_ref[...] = out.astype(BF).reshape(out_ref.shape)


def self_backward_kernel(
    steps, count_ref, q_ref, k_ref, v_ref, do_ref, lse_ref, *rest
):
    joined = len(rest) == 4 and len(rest[1].shape) == 3
    dk_acc, dv_acc = rest[-2:]
    step = pl.program_id(0)
    queries = q_ref[...].reshape(-1, LANES) * BF(HEAD_DIM**-0.5)
    keys = k_ref[...].reshape(-1, LANES)
    values = v_ref[...].reshape(-1, LANES)
    keys_t = keys.T
    grads = do_ref[...].reshape(-1, LANES)
    lane = lax.broadcasted_iota(jnp.int32, queries.shape, 1) // HEAD_DIM
    row = lax.broadcasted_iota(jnp.int32, (keys.shape[0], queries.shape[0]), 0)
    parts = []
    d_keys = None
    for item in range(2):
        mine = jnp.where(lane == item, queries, BF(0))
        d_mine = jnp.where(lane == item, grads, BF(0))
        scores = mm_nt(keys, mine)
        probs = jnp.where(
            row < count_ref[item], jnp.exp(scores - lse_ref[item : item + 1, :]), 0.0
        )
        d_probs = mm_nt(values, d_mine)
        delta = jnp.sum(probs * d_probs, axis=0, keepdims=True)
        d_scores = (probs * (d_probs - delta)).astype(BF)
        new_v = mm(probs.astype(BF), d_mine)
        new_k = mm(d_scores, mine)
        d_values = new_v if d_keys is None else d_values + new_v
        d_keys = new_k if d_keys is None else d_keys + new_k
        span = slice(item * HEAD_DIM, (item + 1) * HEAD_DIM)
        parts.append(mm(keys_t[span], d_scores) * HEAD_DIM**-0.5)
    d_q = jnp.concatenate(parts, axis=0).T
    part, own = q_ref.shape[0], q_ref.shape[2]
    if joined:
        mem_ref, out_ref = rest[:2]
        out_ref[pl.ds(step * part, part), :own] = d_q.astype(BF).reshape(part, own, LANES)
    else:
        dq_ref, dkv_ref = rest[:2]
        dq_ref[...] = d_q.astype(BF).reshape(dq_ref.shape)

    @pl.when(step == 0)
    def _():
        dk_acc[...] = d_keys
        dv_acc[...] = d_values

    @pl.when(step > 0)
    def _():
        dk_acc[...] += d_keys
        dv_acc[...] += d_values

    @pl.when(step == steps - 1)
    def _():
        if joined:
            blocks = out_ref.shape[0]
            shape = (blocks, own, LANES)
            out_ref[:, own : 2 * own] = dk_acc[...].astype(BF).reshape(shape)
            out_ref[:, 2 * own : 3 * own] = dv_acc[...].astype(BF).reshape(shape)
            out_ref[:, 3 * own :] = mem_ref[...].reshape(blocks, -1, LANES)
            return
        shape = (dkv_ref.shape[0], 1) + dkv_ref.shape[2:]
        dkv_ref[:, 0:1] = dk_acc[...].astype(dkv_ref.dtype).reshape(shape)
        dkv_ref[:, 1:2] = dv_acc[...].astype(dkv_ref.dtype).reshape(shape)


def q_steps(blocks):
    return 2 if blocks % 2 == 0 else 1


def self_specs(q_arr, kv_arr, first):
    blocks, _, rows, _ = q_arr.shape
    steps = q_steps(blocks)
    part = blocks // steps
    many = kv_arr.shape[0]
    return steps, part, rows, many, [
        pl.BlockSpec(memory_space=pltpu.SMEM),
        pl.BlockSpec((part, 1, rows, LANES), lambda i: (i, 0, 0, 0)),
        pl.BlockSpec((many, 1, rows, LANES), lambda i: (0, first, 0, 0)),
        pl.BlockSpec((many, 1, rows, LANES), lambda i: (0, first + 1, 0, 0)),
    ]


def self_forward(counts, q_arr, kv_arr, first):
    steps, part, rows, many, specs = self_specs(q_arr, kv_arr, first)
    blocks = q_arr.shape[0]
    pairs = blocks * rows * many * rows * 2
    return pl.pallas_call(
        self_forward_kernel,
        grid=(steps,),
        in_specs=specs,
        out_specs=[
            pl.BlockSpec((part, rows, LANES), lambda i: (i, 0, 0)),
            pl.BlockSpec((2, part * rows), lambda i: (0, i)),
        ],
        out_shape=[
            jax.ShapeDtypeStruct((blocks, rows, LANES), BF),
            jax.ShapeDtypeStruct((2, blocks * rows), F32),
        ],
        compiler_params=pltpu.CompilerParams(vmem_limit_bytes=ROOM),
        cost_estimate=pl.CostEstimate(
            flops=pairs * 4 * LANES, bytes_accessed=1 << 20, transcendentals=pairs
        ),
        name="self_forward",
    )(counts, q_arr, kv_arr, kv_arr)


def self_backward(counts, q_arr, kv_arr, first, d_out, lse, d_mem):
    steps, part, rows, many, specs = self_specs(q_arr, kv_arr, first)
    blocks = q_arr.shape[0]
    pairs = blocks * rows * many * rows * 2
    if d_mem is None:
        more = []
        out_specs = [
            pl.BlockSpec((part, 1, rows, LANES), lambda i: (i, 0, 0, 0)),
            whole((many, 2, rows, LANES)),
        ]
        shapes = [
            jax.ShapeDtypeStruct((blocks, 1, rows, LANES), BF),
            jax.ShapeDtypeStruct((many, 2, rows, LANES), F32),
        ]
    else:
        more = [d_mem]
        shape = (blocks, 3 * rows + 2 * d_mem.shape[2], LANES)
        out_specs = whole(shape)
        shapes = jax.ShapeDtypeStruct(shape, BF)
    return pl.pallas_call(
        functools.partial(self_backward_kernel, steps),
        grid=(steps,),
        in_specs=specs
        + [
            pl.BlockSpec((part, 1, rows, LANES), lambda i: (i, 0, 0, 0)),
            pl.BlockSpec((2, part * rows), lambda i: (0, i)),
        ]
        + [whole(values.shape) for values in more],
        out_specs=out_specs,
        out_shape=shapes,
        scratch_shapes=[
            pltpu.VMEM((many * rows, LANES), F32),
            pltpu.VMEM((many * rows, LANES), F32),
        ],
        compiler_params=pltpu.CompilerParams(vmem_limit_bytes=ROOM),
        cost_estimate=pl.CostEstimate(
            flops=pairs * 10 * LANES, bytes_accessed=2 << 20, transcendentals=pairs
        ),
        name="self_backward",
    )(counts, q_arr, kv_arr, kv_arr, d_out, lse, *more)


def stack_heads(block, lane):
    zero = jnp.zeros((), block.dtype)
    return jnp.concatenate(
        [jnp.where(lane == head, block, zero) for head in range(GROUP)], axis=0
    )


def merge_heads(block, lane):
    rows = block.shape[0] // GROUP
    out = block[:rows]
    for head in range(1, GROUP):
        out = jnp.where(lane == head, block[head * rows : (head + 1) * rows], out)
    return out


def cross_forward_kernel(
    count_ref,
    q_ref,
    mem_ref,
    mid_ref,
    gain,
    bias,
    out_hbm,
    out_ref,
    lse_ref,
    later_ref,
    normed_ref,
    out_w,
    sem,
):
    fetch = pltpu.make_async_copy(out_hbm, out_w, sem)
    fetch.start()
    items, rows, width = q_ref.shape
    many = mem_ref.shape[1]
    lane = lax.broadcasted_iota(jnp.int32, (rows, WIDE), 1) // HEAD_DIM
    row = lax.broadcasted_iota(jnp.int32, (many, GROUP * rows), 0)

    def body(group, carry):
        span = pl.ds(pl.multiple_of(group * WIDE, WIDE), WIDE)
        over = pl.ds(pl.multiple_of(width + group * WIDE, WIDE), WIDE)
        for item in range(items):
            queries = stack_heads(q_ref[item, :, span] * BF(HEAD_DIM**-0.5), lane)
            scores = mm_nt(mem_ref[item, :, span], queries)
            scores = jnp.where(row < count_ref[item], scores, TINY)
            top = jnp.max(scores, axis=0, keepdims=True)
            weights = jnp.exp(scores - top)
            total = jnp.sum(weights, axis=0, keepdims=True)
            out = mm(mem_ref[item, :, over].T, weights.astype(BF)) / total
            out_ref[item, :, span] = merge_heads(out.T, lane).astype(BF)
            lse_ref[item, pl.ds(group, 1), : GROUP * rows] = top + jnp.log(total)
        return carry

    lax.fori_loop(0, width // WIDE, body, 0, unroll=2)
    fetch.wait()
    later = mid_ref[...] + mm(out_ref[...].reshape(items * rows, width), out_w[...])
    later_ref[...] = later
    unit, unused = center_scale(later)
    normed_ref[...] = (unit * gain[...] + bias[...]).astype(BF)


def cross_backward_kernel(count_ref, q_ref, mem_ref, do_ref, lse_ref, dq_ref):
    items, rows, width = q_ref.shape
    many = mem_ref.shape[1]
    lane = lax.broadcasted_iota(jnp.int32, (rows, WIDE), 1) // HEAD_DIM
    row = lax.broadcasted_iota(jnp.int32, (many, GROUP * rows), 0)

    def body(group, carry):
        span = pl.ds(pl.multiple_of(group * WIDE, WIDE), WIDE)
        over = pl.ds(pl.multiple_of(width + group * WIDE, WIDE), WIDE)
        for item in range(items):
            queries = stack_heads(q_ref[item, :, span] * BF(HEAD_DIM**-0.5), lane)
            grads = stack_heads(do_ref[item, :, span], lane)
            keys = mem_ref[item, :, span]
            scores = mm_nt(keys, queries)
            lse = lse_ref[item, pl.ds(group, 1), : GROUP * rows]
            probs = jnp.where(row < count_ref[item], jnp.exp(scores - lse), 0.0)
            d_probs = mm_nt(mem_ref[item, :, over], grads)
            delta = jnp.sum(probs * d_probs, axis=0, keepdims=True)
            d_scores = (probs * (d_probs - delta)).astype(BF)
            d_q = mm(keys.T, d_scores) * HEAD_DIM**-0.5
            dq_ref[item, :, span] = merge_heads(d_q.T, lane).astype(BF)
        return carry

    lax.fori_loop(0, width // WIDE, body, 0, unroll=2)


def cross_forward(counts, cross_q, memory, middle, cross_out, gain, bias):
    items, rows, width = cross_q.shape
    many = memory.shape[1]
    pairs = items * rows * HEADS * many
    return pl.pallas_call(
        cross_forward_kernel,
        grid=(1,),
        in_specs=[IN_SMEM]
        + [whole(x.shape) for x in (cross_q, memory, middle)]
        + [whole((1, width))] * 2
        + [ANYWHERE],
        out_specs=[
            whole((items, rows, width)),
            whole((items, width // WIDE, WIDE)),
            whole((items * rows, width)),
            whole((items * rows, width)),
        ],
        out_shape=[
            jax.ShapeDtypeStruct((items, rows, width), BF),
            jax.ShapeDtypeStruct((items, width // WIDE, WIDE), F32),
            jax.ShapeDtypeStruct((items * rows, width), F32),
            jax.ShapeDtypeStruct((items * rows, width), BF),
        ],
        scratch_shapes=[pltpu.VMEM(cross_out.shape, BF), pltpu.SemaphoreType.DMA],
        compiler_params=pltpu.CompilerParams(vmem_limit_bytes=ROOM),
        cost_estimate=pl.CostEstimate(
            flops=pairs * 4 * WIDE, bytes_accessed=3 << 20, transcendentals=pairs
        ),
        name="cross_forward",
    )(counts, cross_q, memory, middle, gain[None], bias[None], cross_out)


def cross_backward(counts, cross_q, memory, d_out, lse):
    items, rows, width = cross_q.shape
    many = memory.shape[1]
    pairs = items * rows * HEADS * many
    return pl.pallas_call(
        cross_backward_kernel,
        grid=(1,),
        in_specs=[IN_SMEM] + [whole(x.shape) for x in (cross_q, memory, d_out, lse)],
        out_specs=whole((items, rows, width)),
        out_shape=jax.ShapeDtypeStruct((items, rows, width), BF),
        compiler_params=pltpu.CompilerParams(vmem_limit_bytes=ROOM),
        cost_estimate=pl.CostEstimate(
            flops=pairs * 10 * WIDE, bytes_accessed=6 << 20, transcendentals=pairs
        ),
        name="cross_backward",
    )(counts, cross_q, memory, d_out, lse)


def memory_back_kernel(head_ref, count_ref, q_ref, do_ref, k_ref, v_ref, out_ref):
    items, many, _ = k_ref.shape
    odd = lax.rem(head_ref[0], 2)
    queries = q_ref[...].reshape(-1, LANES) * BF(HEAD_DIM**-0.5)
    grads = do_ref[...].reshape(-1, LANES)
    lane = lax.broadcasted_iota(jnp.int32, (many, LANES), 1) // HEAD_DIM
    row = lax.broadcasted_iota(jnp.int32, (many, queries.shape[0]), 0)

    def turn(ref, item):
        block = ref[item].astype(F32)
        block = jnp.where(odd == item, block, swap_half(block))
        return jnp.where(lane == item, block, 0.0).astype(BF)

    d_keys = None
    for item in range(items):
        scores = mm_nt(turn(k_ref, item), queries)
        scores = jnp.where(row < count_ref[item], scores, TINY)
        weights = jnp.exp(scores - jnp.max(scores, axis=0, keepdims=True))
        probs = weights * (1.0 / jnp.sum(weights, axis=0, keepdims=True))
        d_probs = mm_nt(turn(v_ref, item), grads)
        delta = jnp.sum(probs * d_probs, axis=0, keepdims=True)
        d_scores = (probs * (d_probs - delta)).astype(BF)
        new_k = mm(d_scores, queries)
        new_v = mm(probs.astype(BF), grads)
        d_values = new_v if d_keys is None else jnp.where(lane == item, new_v, d_values)
        d_keys = new_k if d_keys is None else jnp.where(lane == item, new_k, d_keys)
    shape = (out_ref.shape[0], 1) + out_ref.shape[2:]
    out_ref[:, 0:1] = d_keys.astype(out_ref.dtype).reshape(shape)
    out_ref[:, 1:2] = d_values.astype(out_ref.dtype).reshape(shape)


def memory_back(head, counts, got, memory, part, low):
    blocks, _, own, _ = got.shape
    items, many, double = memory.shape
    pairs = double // 2 // LANES
    work = items * many * blocks * own
    return pl.pallas_call(
        memory_back_kernel,
        grid_spec=pltpu.PrefetchScalarGridSpec(
            num_scalar_prefetch=2,
            grid=(1,),
            in_specs=[
                pl.BlockSpec((blocks, 1, own, LANES), lambda i, h, c: (0, 1, 0, 0)),
                pl.BlockSpec((blocks, 1, own, LANES), lambda i, h, c: (0, 2, 0, 0)),
                pl.BlockSpec((items, many, LANES), lambda i, h, c: (0, 0, lax.div(h[0], 2))),
                pl.BlockSpec(
                    (items, many, LANES), lambda i, h, c: (0, 0, pairs + lax.div(h[0], 2))
                ),
            ],
            out_specs=whole((many // part, 2, part, LANES)),
        ),
        out_shape=jax.ShapeDtypeStruct((many // part, 2, part, LANES), BF if low else F32),
        compiler_params=pltpu.CompilerParams(vmem_limit_bytes=ROOM),
        cost_estimate=pl.CostEstimate(
            flops=work * 8 * LANES, bytes_accessed=2 << 20, transcendentals=work
        ),
        name="memory_back",
    )(head, counts, got, got, memory, memory)


def swap_half(block):
    return pltpu.roll(block, HEAD_DIM, 1)


def first_half(shape):
    return lax.broadcasted_iota(jnp.int32, shape, 1) < HEAD_DIM


def pair_to_heads(block):
    own = block.shape[0] // 2
    left, right = block[:own], block[own:]
    low = first_half(left.shape)
    return (
        jnp.where(low, left, swap_half(right)),
        jnp.where(low, swap_half(left), right),
    )


def project_kernel(tri_ref, mod_ref, q_ref, k_ref, v_ref, out_ref, normed):
    items, own, width = tri_ref.shape

    @pl.when(pl.program_id(0) == 0)
    def _():
        for item in range(items):
            unit, unused = center_scale(tri_ref[item].astype(F32))
            scale = mod_ref[item : item + 1, width:]
            shift = mod_ref[item : item + 1, :width]
            normed[item * own : (item + 1) * own] = (unit * (1.0 + scale) + shift).astype(BF)

    for kind, ref in enumerate((q_ref, k_ref, v_ref)):
        block = mm(normed[...], ref[...])
        for pair in range(WIDE // LANES):
            first, second = pair_to_heads(block[:, pair * LANES : (pair + 1) * LANES])
            out_ref[2 * pair, kind] = first.astype(BF)
            out_ref[2 * pair + 1, kind] = second.astype(BF)


def project(triplane, modulation, qkv_weight):
    items, own, width = triplane.shape
    steps = width // WIDE
    return pl.pallas_call(
        project_kernel,
        grid=(steps,),
        in_specs=[
            pl.BlockSpec((items, own, width), lambda i: (0, 0, 0)),
            pl.BlockSpec((items, 2 * width), lambda i: (0, 0)),
            pl.BlockSpec((width, WIDE), lambda i: (0, i)),
            pl.BlockSpec((width, WIDE), lambda i: (0, steps + i)),
            pl.BlockSpec((width, WIDE), lambda i: (0, 2 * steps + i)),
        ],
        out_specs=pl.BlockSpec((GROUP, 3, own, LANES), lambda i: (i, 0, 0, 0)),
        out_shape=jax.ShapeDtypeStruct((HEADS, 3, own, LANES), BF),
        scratch_shapes=[pltpu.VMEM((items * own, width), BF)],
        compiler_params=pltpu.CompilerParams(vmem_limit_bytes=ROOM),
        cost_estimate=pl.CostEstimate(
            flops=6 * items * own * width * width, bytes_accessed=8 << 20, transcendentals=0
        ),
        name="project",
    )(triplane, modulation, qkv_weight, qkv_weight, qkv_weight)


def middle_kernel(
    got_ref,
    tri_ref,
    gain,
    bias,
    out_hbm,
    query_hbm,
    att_ref,
    mid_ref,
    normed_ref,
    query_ref,
    out_w,
    query_w,
    sems,
):
    fetch_out = pltpu.make_async_copy(out_hbm, out_w, sems.at[0])
    fetch_out.start()
    fetch_query = pltpu.make_async_copy(query_hbm, query_w, sems.at[1])
    fetch_query.start()
    heads, own, _ = got_ref.shape
    for pair in range(heads // 2):
        left = got_ref[2 * pair].astype(F32)
        right = got_ref[2 * pair + 1].astype(F32)
        low = first_half(left.shape)
        span = slice(pair * LANES, (pair + 1) * LANES)
        att_ref[:own, span] = jnp.where(low, left, swap_half(right)).astype(BF)
        att_ref[own:, span] = jnp.where(low, swap_half(left), right).astype(BF)
    fetch_out.wait()
    middle = tri_ref[...].astype(F32) + mm(att_ref[...], out_w[...])
    mid_ref[...] = middle
    unit, unused = center_scale(middle)
    normed = (unit * gain[...] + bias[...]).astype(BF)
    normed_ref[...] = normed
    fetch_query.wait()
    query_ref[...] = mm(normed, query_w[...]).astype(BF)


def middle_part(got, tri_rows, self_out, gain, bias, cross_query):
    rows, width = tri_rows.shape
    low = jax.ShapeDtypeStruct((rows, width), BF)
    return pl.pallas_call(
        middle_kernel,
        grid=(1,),
        in_specs=[whole(got.shape), whole((rows, width)), whole((1, width)), whole((1, width))]
        + [ANYWHERE] * 2,
        out_specs=[whole((rows, width))] * 4,
        out_shape=[low, jax.ShapeDtypeStruct((rows, width), F32), low, low],
        scratch_shapes=[
            pltpu.VMEM(self_out.shape, BF),
            pltpu.VMEM(cross_query.shape, BF),
            pltpu.SemaphoreType.DMA((2,)),
        ],
        compiler_params=pltpu.CompilerParams(vmem_limit_bytes=ROOM),
        cost_estimate=pl.CostEstimate(
            flops=4 * rows * width * width, bytes_accessed=5 << 20, transcendentals=0
        ),
        name="middle_part",
    )(got, tri_rows, gain[None], bias[None], self_out, cross_query)


def middle_back_kernel(
    dq_ref,
    mid_ref,
    gain,
    later_ref,
    query_ref,
    crossed_ref,
    query_hbm,
    out_hbm,
    d_mid_ref,
    low_ref,
    heads_ref,
    sums_ref,
    query_w,
    out_w,
    sems,
):
    fetch_query = pltpu.make_async_copy(query_hbm, query_w, sems.at[0])
    fetch_query.start()
    fetch_out = pltpu.make_async_copy(out_hbm, out_w, sems.at[1])
    fetch_out.start()

    def by_head(values, kind):
        for pair in range(values.shape[1] // LANES):
            block = values[:, pair * LANES : (pair + 1) * LANES].astype(F32)
            first, second = pair_to_heads(block)
            heads_ref[2 * pair, kind] = first.astype(BF)
            heads_ref[2 * pair + 1, kind] = second.astype(BF)

    by_head(query_ref[...], 1)
    by_head(crossed_ref[...], 2)
    fetch_query.wait()
    d_normed = mm_nt(dq_ref[...], query_w[...])
    unit, rstd = center_scale(mid_ref[...])
    sums_ref[0:1] = jnp.sum(d_normed * unit, axis=0, keepdims=True)
    sums_ref[1:2] = jnp.sum(d_normed, axis=0, keepdims=True)
    d_middle = later_ref[...] + norm_back(unit, rstd, d_normed * gain[...])
    d_mid_ref[...] = d_middle
    low = d_middle.astype(BF)
    low_ref[...] = low
    fetch_out.wait()
    by_head(mm_nt(low, out_w[...]), 0)


def middle_back(own, d_query, cross_query, middle, gain, d_later, self_out, cross_q, d_crossed):
    rows, width = middle.shape
    return pl.pallas_call(
        middle_back_kernel,
        grid=(1,),
        in_specs=[whole((rows, width)), whole((rows, width)), whole((1, width))]
        + [whole((rows, width))] * 3
        + [ANYWHERE] * 2,
        out_specs=[
            whole((rows, width)),
            whole((rows, width)),
            whole((HEADS, 3, own, LANES)),
            whole((2, width)),
        ],
        scratch_shapes=[
            pltpu.VMEM(cross_query.shape, BF),
            pltpu.VMEM(self_out.shape, BF),
            pltpu.SemaphoreType.DMA((2,)),
        ],
        out_shape=[
            jax.ShapeDtypeStruct((rows, width), F32),
            jax.ShapeDtypeStruct((rows, width), BF),
            jax.ShapeDtypeStruct((HEADS, 3, own, LANES), BF),
            jax.ShapeDtypeStruct((2, width), F32),
        ],
        compiler_params=pltpu.CompilerParams(vmem_limit_bytes=ROOM),
        cost_estimate=pl.CostEstimate(
            flops=4 * rows * width * width, bytes_accessed=6 << 20, transcendentals=0
        ),
        name="middle_back",
    )(d_query, middle, gain[None], d_later, cross_q, d_crossed, cross_query, self_out)


def first_back_kernel(
    steps, got_ref, q_ref, k_ref, v_ref, tri_ref, mod_ref, mid_ref, out_ref, total
):
    items, own, width = tri_ref.shape
    step = pl.program_id(0)
    added = None
    for kind, ref in enumerate((q_ref, k_ref, v_ref)):
        columns = []
        for pair in range(WIDE // LANES):
            at = slice(kind * own, (kind + 1) * own)
            left = got_ref[2 * pair, at].astype(F32)
            right = got_ref[2 * pair + 1, at].astype(F32)
            low = first_half(left.shape)
            columns.append(
                jnp.concatenate(
                    [
                        jnp.where(low, left, swap_half(right)),
                        jnp.where(low, swap_half(left), right),
                    ],
                    axis=0,
                )
            )
        term = mm_nt(jnp.concatenate(columns, axis=1).astype(BF), ref[...])
        added = term if added is None else added + term

    @pl.when(step == 0)
    def _():
        total[...] = added

    @pl.when(step > 0)
    def _():
        total[...] += added

    @pl.when(step == steps - 1)
    def _():
        for item in range(items):
            unit, rstd = center_scale(tri_ref[item].astype(F32))
            grad = total[item * own : (item + 1) * own] * (1.0 + mod_ref[item : item + 1, width:])
            out_ref[item] = mid_ref[item] + norm_back(unit, rstd, grad)


def first_back(got, qkv_weight, triplane, modulation, d_middle):
    items, own, width = triplane.shape
    steps = width // WIDE
    return pl.pallas_call(
        functools.partial(first_back_kernel, steps),
        grid=(steps,),
        in_specs=[
            pl.BlockSpec((GROUP,) + got.shape[1:], lambda i: (i, 0, 0)),
            pl.BlockSpec((width, WIDE), lambda i: (0, i)),
            pl.BlockSpec((width, WIDE), lambda i: (0, steps + i)),
            pl.BlockSpec((width, WIDE), lambda i: (0, 2 * steps + i)),
            pl.BlockSpec((items, own, width), lambda i: (0, 0, 0)),
            pl.BlockSpec((items, 2 * width), lambda i: (0, 0)),
            pl.BlockSpec((items, own, width), lambda i: (0, 0, 0)),
        ],
        out_specs=pl.BlockSpec((items, own, width), lambda i: (0, 0, 0)),
        out_shape=jax.ShapeDtypeStruct((items, own, width), F32),
        scratch_shapes=[pltpu.VMEM((items * own, width), F32)],
        compiler_params=pltpu.CompilerParams(vmem_limit_bytes=ROOM),
        cost_estimate=pl.CostEstimate(
            flops=6 * items * own * width * width, bytes_accessed=8 << 20, transcendentals=0
        ),
        name="first_back",
    )(got, qkv_weight, qkv_weight, qkv_weight, triplane, modulation, d_middle)


def head_back_kernel(
    packed,
    own,
    head_ref,
    grads_ref,
    tri_ref,
    patch_ref,
    q_ref,
    k_ref,
    v_ref,
    mod_ref,
    *rest,
):
    units = rest[-1]
    items, many, width = tri_ref.shape
    odd = lax.rem(head_ref[0], 2) == 1
    grads = [
        grads_ref[:, kind * own : (kind + 1) * own].reshape(many, LANES).astype(F32).T
        for kind in range(3)
    ]
    weight = []
    for ref in (q_ref, k_ref, v_ref):
        turned = ref[...].astype(F32).T
        weight.append(jnp.where(odd, turned[HEAD_DIM:], turned[:HEAD_DIM]))
    weight = jnp.concatenate(weight, axis=0)
    product = None
    terms = []
    for item in range(items):
        unit, unused = center_scale(tri_ref[item].astype(F32))
        units[...] = unit.astype(BF)
        span = slice(item * HEAD_DIM, (item + 1) * HEAD_DIM)
        mine = jnp.concatenate([part[span] for part in grads], axis=0)
        outer = mm(mine.astype(BF), units[...])
        column = jnp.sum(mine, axis=1, keepdims=True)
        shift = mod_ref[item : item + 1, :width]
        scale = mod_ref[item : item + 1, width:]
        terms.append(jnp.sum(column * weight, axis=0, keepdims=True))
        terms.append(jnp.sum(outer * weight, axis=0, keepdims=True))
        term = outer * (1.0 + scale) + column * shift
        product = term if product is None else product + term
    product = product.T
    patch_rows = patch_ref.shape[1]
    few = patch_rows // grads_ref.shape[0]
    grads = [
        grads_ref[:, 3 * own + kind * few : 3 * own + (kind + 1) * few]
        .reshape(patch_rows, LANES)
        .astype(F32)
        .T
        for kind in range(2)
    ]
    memory = None
    for item in range(items):
        span = slice(item * HEAD_DIM, (item + 1) * HEAD_DIM)
        mine = jnp.concatenate([part[span] for part in grads], axis=0).astype(BF)
        term = mm(mine, patch_ref[item])
        memory = term if memory is None else memory + term
    memory = memory.T
    if not packed:
        out_ref, memory_ref, terms_ref = rest[:3]
        out_ref[...] = product.astype(BF)
        memory_ref[...] = memory.astype(BF)
        for item in range(items):
            terms_ref[item : item + 1, :width] = terms[2 * item]
            terms_ref[item : item + 1, width:] = terms[2 * item + 1]
        return
    ends_ref, out_ref, terms_ref, unused = rest
    devices = out_ref.shape[0]
    span = width // devices
    product = product.reshape(devices, span, 3 * HEAD_DIM).astype(BF)
    out_ref[:, :span] = memory.reshape(devices, span, LANES).astype(BF)
    out_ref[:, span : 2 * span] = product[:, :, :LANES]
    last = product[:, :, LANES:]
    at = 2 * span + span // 2
    out_ref[:, 2 * span : at] = jnp.concatenate(
        [last[:, : span // 2], last[:, span // 2 :]], axis=2
    )
    out_ref[:, at:] = ends_ref[...]
    lines = [
        term[:, k * LANES : (k + 1) * LANES] for term in terms for k in range(width // LANES)
    ]
    terms_ref[...] = jnp.concatenate(lines, axis=0).astype(BF)


def head_back(head, grads, own, rows_all, patch_part, qkv_weight, modulation, ends):
    items, many, width = rows_all.shape
    pairs = width // LANES
    product = jax.ShapeDtypeStruct((width, 3 * HEAD_DIM), BF)
    if ends is None:
        more = []
        shapes = [
            product,
            jax.ShapeDtypeStruct((width, LANES), BF),
            jax.ShapeDtypeStruct((items, 2 * width), F32),
        ]
    else:
        devices, tail, _ = ends.shape
        more = [ends]
        many_rows = 5 * width // devices // 2 + tail
        shapes = [
            jax.ShapeDtypeStruct((devices, many_rows, LANES), BF),
            jax.ShapeDtypeStruct((2 * items * pairs, LANES), BF),
        ]

    def whole_block(shape):
        return pl.BlockSpec(shape, lambda i, h: (0,) * len(shape))

    return pl.pallas_call(
        functools.partial(head_back_kernel, ends is not None, own),
        grid_spec=pltpu.PrefetchScalarGridSpec(
            num_scalar_prefetch=1,
            grid=(1,),
            in_specs=[
                whole_block(grads.shape),
                pl.BlockSpec((items, many, width), lambda i, h: (0, 0, 0)),
                whole_block(patch_part.shape),
                pl.BlockSpec((width, LANES), lambda i, h: (0, lax.div(h[0], 2))),
                pl.BlockSpec((width, LANES), lambda i, h: (0, pairs + lax.div(h[0], 2))),
                pl.BlockSpec((width, LANES), lambda i, h: (0, 2 * pairs + lax.div(h[0], 2))),
                whole_block((items, 2 * width)),
            ]
            + [whole_block(array.shape) for array in more],
            out_specs=[whole_block(shape.shape) for shape in shapes],
            scratch_shapes=[pltpu.VMEM((many, width), BF)],
        ),
        out_shape=shapes,
        compiler_params=pltpu.CompilerParams(vmem_limit_bytes=ROOM),
        cost_estimate=pl.CostEstimate(
            flops=6 * items * many * width * HEAD_DIM, bytes_accessed=5 << 20, transcendentals=0
        ),
        name="head_back",
    )(
        head,
        grads,
        rows_all,
        patch_part,
        qkv_weight,
        qkv_weight,
        qkv_weight,
        modulation,
        *more,
    )


def by_heads_kernel(got_ref, out_ref):
    parts, heads, rows, _ = got_ref.shape
    width = heads * HEAD_DIM
    for pair in range(heads // 2):
        left = got_ref[0, 2 * pair].astype(F32)
        right = got_ref[0, 2 * pair + 1].astype(F32)
        for part in range(1, parts):
            left = left + got_ref[part, 2 * pair].astype(F32)
            right = right + got_ref[part, 2 * pair + 1].astype(F32)
        for kind in range(3):
            span = slice(kind * HEAD_DIM, (kind + 1) * HEAD_DIM)
            at = kind * width + pair * LANES
            out_ref[:, at : at + LANES] = jnp.concatenate([left[:, span], right[:, span]], axis=1)


def by_heads(got):
    parts, heads, rows, features = got.shape
    return pl.pallas_call(
        by_heads_kernel,
        grid=(1,),
        in_specs=[whole(got.shape)],
        out_specs=whole((rows, heads * features)),
        out_shape=jax.ShapeDtypeStruct((rows, heads * features), F32),
        compiler_params=pltpu.CompilerParams(vmem_limit_bytes=ROOM),
        name="by_heads",
    )(got)


def unpack_kernel(tail, got_ref, mem_ref, qkv_ref, mod_ref, ends_ref):
    span = qkv_ref.shape[0]
    width = HEADS * HEAD_DIM
    at = 2 * span + span // 2

    def columns(head):
        full = got_ref[head, :at].astype(F32)
        last = full[2 * span :]
        last = jnp.concatenate([last[:, :HEAD_DIM], last[:, HEAD_DIM:]], axis=0)
        first, second = full[:span], full[span : 2 * span]
        return (
            first[:, :HEAD_DIM],
            first[:, HEAD_DIM:],
            second[:, :HEAD_DIM],
            second[:, HEAD_DIM:],
            last,
        )

    for pair in range(HEADS // 2):
        both = [
            jnp.concatenate(sides, axis=1)
            for sides in zip(columns(2 * pair), columns(2 * pair + 1))
        ]
        for kind in range(2):
            start = kind * width + pair * LANES
            mem_ref[:, start : start + LANES] = both[kind]
        for kind in range(3):
            start = kind * width + pair * LANES
            qkv_ref[:, start : start + LANES] = both[2 + kind]
    total = got_ref[0, at:].astype(F32)
    for head in range(1, HEADS):
        total = total + got_ref[head, at:].astype(F32)
    ends_ref[...] = total[:tail]
    mod_ref[...] = total[tail:]


def unpack(got, span, tail):
    _, many, _ = got.shape
    shapes = [
        (span, 2 * HEADS * HEAD_DIM),
        (span, 3 * HEADS * HEAD_DIM),
        (many - tail - 2 * span - span // 2, LANES),
        (tail, LANES),
    ]
    return pl.pallas_call(
        functools.partial(unpack_kernel, tail),
        grid=(1,),
        in_specs=[whole(got.shape)],
        out_specs=[whole(shape) for shape in shapes],
        out_shape=[jax.ShapeDtypeStruct(shape, F32) for shape in shapes],
        compiler_params=pltpu.CompilerParams(vmem_limit_bytes=ROOM),
        name="unpack",
    )(got)


def gather_lanes(block, starts, span):
    out = []
    lane = lax.broadcasted_iota(jnp.int32, (block.shape[0], LANES), 1)
    for at in range(0, len(starts) * span, LANES):
        merged = None
        for to in range(0, LANES, min(span, LANES)):
            start = starts[(at + to) // span] + (at + to) % span
            base = start // LANES * LANES
            part = block[:, base : base + LANES]
            shift = (to - (start - base)) % LANES
            if shift:
                part = pltpu.roll(part, shift, 1)
            if merged is None:
                merged = part
            else:
                merged = jnp.where((lane >= to) & (lane < to + span), part, merged)
        out.append(merged)
    return jnp.concatenate(out, axis=1)


def starts_y(features, devices, quarter):
    span = features // devices
    return [(group * 4 + quarter) * span for group in range(devices // 4)]


def starts_x(features, devices, half, low):
    span = features // devices
    many = devices // 2
    return [
        (half * many + rest * 4 + y * 2 + low) * span
        for y in range(2)
        for rest in range(many // 4)
    ]


def mlp_kernel(
    steps,
    devices,
    normed_ref,
    dh_ref,
    up_ref,
    later_ref,
    c_ref,
    gain,
    out_hbm,
    hidden_ref,
    pre_ref,
    up_piece_ref,
    down_piece_ref,
    d_later_ref,
    low_ref,
    d_crossed_ref,
    sums_ref,
    total,
    out_w,
    sem,
):
    step = pl.program_id(0)
    fetch = pltpu.make_async_copy(out_hbm, out_w, sem)

    @pl.when(step == 0)
    def _():
        fetch.start()
        values = normed_ref[...].astype(F32)
        for quarter in range(4):
            starts = starts_y(values.shape[1], devices, quarter)
            span = values.shape[1] // devices
            up_piece_ref[quarter] = gather_lanes(values, starts, span).astype(BF)

    pre = mm(normed_ref[...], up_ref[...])
    square = pre * pre
    slope = (2.0 / 3.141592653589793) ** 0.5
    turn = jnp.tanh(slope * (pre + 0.044715 * (pre * square)))
    hidden = 0.5 * pre * (1.0 + turn)
    hidden_ref[...] = hidden.astype(BF)
    part = hidden.shape[1]
    span = part * steps // devices
    half = lax.div(step, steps // 2)
    for low in range(2):
        for y in range(2):
            starts = [(rest * 4 + y * 2 + low) * span for rest in range(part // (4 * span))]
            at = y * (part * steps // 8) + lax.rem(step, steps // 2) * (part // 4)
            at = pl.ds(pl.multiple_of(at, LANES), part // 4)
            down_piece_ref[2 * half + low, :, at] = gather_lanes(hidden, starts, span).astype(BF)
    change = 0.5 * (1.0 + turn) + 0.5 * pre * (1.0 - turn * turn) * (
        slope * (1.0 + 3.0 * 0.044715 * square)
    )
    d_pre = (dh_ref[...] * change).astype(BF)
    pre_ref[...] = d_pre
    added = mm_nt(d_pre, up_ref[...])

    @pl.when(step == 0)
    def _():
        total[...] = added

    @pl.when(step > 0)
    def _():
        total[...] += added

    @pl.when(step == steps - 1)
    def _():
        d_normed = total[...]
        unit, rstd = center_scale(later_ref[...])
        sums_ref[0:1] = jnp.sum(d_normed * unit, axis=0, keepdims=True)
        sums_ref[1:2] = jnp.sum(d_normed, axis=0, keepdims=True)
        d_later = c_ref[...].astype(F32) + norm_back(unit, rstd, d_normed * gain[...])
        d_later_ref[...] = d_later
        low = d_later.astype(BF)
        low_ref[...] = low
        fetch.wait()
        d_crossed_ref[...] = mm_nt(low, out_w[...]).astype(BF)


def mlp(devices, normed, d_hidden, up_weight, later, grad_out, gain, cross_out):
    rows, width = normed.shape
    hidden_width = up_weight.shape[1]
    part = min(1024, hidden_width)
    steps = hidden_width // part
    low = jax.ShapeDtypeStruct((rows, width), BF)
    return pl.pallas_call(
        functools.partial(mlp_kernel, steps, devices),
        grid=(steps,),
        in_specs=[
            whole((rows, width)),
            pl.BlockSpec((rows, part), lambda i: (0, i)),
            pl.BlockSpec((width, part), lambda i: (0, i)),
            whole((rows, width)),
            whole((rows, width)),
            whole((1, width)),
            ANYWHERE,
        ],
        out_specs=[
            pl.BlockSpec((rows, part), lambda i: (0, i)),
            pl.BlockSpec((rows, part), lambda i: (0, i)),
            whole((4, rows, width // 4)),
            whole((4, rows, hidden_width // 4)),
            whole((rows, width)),
            whole((rows, width)),
            whole((rows, width)),
            whole((2, width)),
        ],
        out_shape=[
            jax.ShapeDtypeStruct((rows, hidden_width), BF),
            jax.ShapeDtypeStruct((rows, hidden_width), BF),
            jax.ShapeDtypeStruct((4, rows, width // 4), BF),
            jax.ShapeDtypeStruct((4, rows, hidden_width // 4), BF),
            jax.ShapeDtypeStruct((rows, width), F32),
            low,
            low,
            jax.ShapeDtypeStruct((2, width), F32),
        ],
        scratch_shapes=[
            pltpu.VMEM((rows, width), F32),
            pltpu.VMEM((width, width), BF),
            pltpu.SemaphoreType.DMA,
        ],
        compiler_params=pltpu.CompilerParams(vmem_limit_bytes=ROOM),
        cost_estimate=pl.CostEstimate(
            flops=4 * rows * width * hidden_width,
            bytes_accessed=12 << 20,
            transcendentals=rows * hidden_width,
        ),
        name="mlp",
    )(normed, d_hidden, up_weight, later, grad_out, gain[None], cross_out)


def pieces_kernel(devices, *refs):
    out_ref = refs[-1]
    for k, ref in enumerate(refs[:-1]):
        values = ref[...].astype(F32)
        span = values.shape[1] // devices
        for half in range(2):
            for low in range(2):
                starts = starts_x(values.shape[1], devices, half, low)
                out_ref[2 * half + low, k] = gather_lanes(values, starts, span).astype(BF)


def pieces(devices, *arrays):
    rows, width = arrays[0].shape
    return pl.pallas_call(
        functools.partial(pieces_kernel, devices),
        grid=(1,),
        in_specs=[whole((rows, width))] * len(arrays),
        out_specs=whole((4, len(arrays), rows, width // 4)),
        out_shape=jax.ShapeDtypeStruct((4, len(arrays), rows, width // 4), BF),
        compiler_params=pltpu.CompilerParams(vmem_limit_bytes=ROOM),
        name="pieces",
    )(*arrays)


def product_kernel(half_ref, *refs):
    x_refs, y_refs, (keep_ref, send_ref, left, right) = refs[:4], refs[4:8], refs[8:]
    rows = x_refs[0].shape[1]

    @pl.when(pl.program_id(1) == 0)
    def _():
        for k, ref in enumerate(x_refs):
            left[k * rows : (k + 1) * rows] = ref[0]

    for k, ref in enumerate(y_refs):
        right[k * rows : (k + 1) * rows] = ref[0]
    wide = left.shape[1] // 2
    half = half_ref[0]
    for ref, which in ((keep_ref, half), (send_ref, 1 - half)):
        at = pl.ds(pl.multiple_of(which * wide, LANES), wide)
        ref[...] = mm_tn(left[:, at], right[...]).astype(BF).reshape(ref.shape)


def product(half, quads, left, right):
    entries, rows, wide = left[0].shape
    columns = right[0].shape[2]
    span = wide // (2 * quads)
    part = min(columns, 1024)
    shape = jax.ShapeDtypeStruct((quads, entries, span, columns), BF)
    spec = pl.BlockSpec((quads, 1, span, part), lambda e, i: (0, e, 0, i))
    return pl.pallas_call(
        product_kernel,
        grid=(entries, columns // part),
        in_specs=[IN_SMEM]
        + [pl.BlockSpec((1, rows, wide), lambda e, i: (e, 0, 0))] * 4
        + [pl.BlockSpec((1, rows, part), lambda e, i: (e, 0, i))] * 4,
        out_specs=[spec, spec],
        out_shape=[shape, shape],
        scratch_shapes=[pltpu.VMEM((4 * rows, wide), BF), pltpu.VMEM((4 * rows, part), BF)],
        compiler_params=pltpu.CompilerParams(vmem_limit_bytes=ROOM),
        cost_estimate=pl.CostEstimate(
            flops=8 * entries * rows * wide * columns, bytes_accessed=8 << 20, transcendentals=0
        ),
        name="product",
    )(half.reshape(1).astype(jnp.int32), *left, *right)


def xor_blk(values, bit, count):
    return lax.ppermute(values, "blk", [(i, i ^ bit) for i in range(count)])


def swap_batch(values):
    return lax.ppermute(values, "batch", [(0, 1), (1, 0)])


def after(values, *first):
    return lax.optimization_barrier((values, first))[0]


def take(values, index, axis):
    return lax.dynamic_index_in_dim(values, index, axis, keepdims=False)


def local(
    count_blk,
    triplane,
    patches,
    cotangent,
    camera_index,
    triplane_count,
    patch_count,
    camera_table,
    mod_weight,
    qkv_weight,
    self_out,
    gain_mid,
    bias_mid,
    cross_query,
    cross_memory,
    cross_out,
    gain_last,
    bias_last,
    up_weight,
    down_weight,
):
    items, own, width = triplane.shape
    own_patches = patches.shape[1]
    rows = items * own
    spare = count_blk // HEADS
    quads = count_blk // 4
    devices = 2 * count_blk
    row_groups = (
        None
        if spare == 1
        else [[part * HEADS + head for head in range(HEADS)] for part in range(spare)]
    )
    head_groups = [[part * HEADS + head for part in range(spare)] for head in range(HEADS)]
    batch_at = lax.axis_index("batch")
    blk_at = lax.axis_index("blk")
    head_at = lax.rem(blk_at, HEADS)
    place = batch_at * count_blk + blk_at

    def to_heads(values):
        return lax.all_to_all(values, "blk", 0, 0, axis_index_groups=row_groups, tiled=True)

    def swap_corner(values):
        return lax.ppermute(
            values,
            BOTH,
            [
                (b * count_blk + j, (1 - b) * count_blk + (j ^ 1))
                for b in range(2)
                for j in range(count_blk)
            ],
        )

    def quad_y(values):
        far = xor_blk(values, 2, count_blk)
        return [values, xor_blk(values, 1, count_blk), far, xor_blk(far, 1, count_blk)]

    def quad_x(values):
        far = swap_batch(values)
        return [values, xor_blk(values, 1, count_blk), far, xor_blk(far, 1, count_blk)]

    def exchange_y(cut):
        low = jnp.bitwise_and(blk_at, 3)
        got = [take(cut, low, 0)]
        for bit in (1, 2, 3):
            got.append(xor_blk(take(cut, jnp.bitwise_xor(low, bit), 0), bit, count_blk))
        return got

    def exchange_x(cut):
        low = jnp.bitwise_and(blk_at, 1)
        return [
            take(cut, 2 * batch_at + low, 0),
            xor_blk(take(cut, 2 * batch_at + 1 - low, 0), 1, count_blk),
            swap_batch(take(cut, 2 * (1 - batch_at) + low, 0)),
            swap_corner(take(cut, 2 * (1 - batch_at) + 1 - low, 0)),
        ]

    def half_x(values):
        given = swap_batch(take(values, 1 - batch_at, 0))
        return (take(values, batch_at, 0).astype(F32) + given.astype(F32)).astype(BF)

    def rest_sum(keep, given):
        many = quads
        bit = 4
        while many > 1:
            low = jnp.bitwise_and(lax.div(blk_at, bit), 1)
            shape = (many // 2, 2) + keep.shape[1:]
            keep, given = keep.reshape(shape), given.reshape(shape)

            def part(index):
                total = take(keep, index, 1).astype(F32) + take(given, index, 1).astype(F32)
                return total.astype(BF)

            keep, given = part(low), xor_blk(part(1 - low), bit, count_blk)
            many //= 2
            bit *= 2
        return (keep.astype(F32) + given.astype(F32))[0]

    views = camera_index.shape[1]
    table_rows = jnp.arange(camera_table.shape[0], dtype=jnp.int32)

    def pick_of(cams):
        return jnp.sum((cams[:, :, None] == table_rows[None, None, :]).astype(F32), axis=1)

    def code_of(pick):
        return (mm(pick.astype(BF), camera_table) / views).astype(BF)

    modulation = mm(code_of(pick_of(camera_index)), mod_weight)
    sent = project(triplane, modulation, qkv_weight)
    qkv = to_heads(sent)

    patches_all = lax.all_gather(patches, "blk", axis=1, tiled=True)
    bit_y = jnp.bitwise_and(lax.div(blk_at, 2), 1)
    many_patches = patches_all.shape[1]
    memory = (
        mm(patches_all.reshape(items * many_patches, width), cross_memory)
        .astype(BF)
        .reshape(items, many_patches, 2 * width)
    )
    grad_out = cotangent.reshape(rows, width)
    d_hidden = mm_nt(grad_out, down_weight)
    grad_quad = quad_x(lax.optimization_barrier((grad_out, sent))[0])

    qkv, d_hidden = lax.optimization_barrier((qkv, d_hidden))
    if spare == 1:
        kv, kv_first = qkv, 1
    else:
        kv = lax.all_gather(qkv[:, 1:], "blk", axis=0, axis_index_groups=head_groups, tiled=True)
        kv_first = 0
    attended_heads, self_lse = self_forward(triplane_count, qkv, kv, kv_first)
    attended_got = to_heads(attended_heads)
    kept = lax.optimization_barrier((triplane, attended_heads))[0]
    rows_all = lax.all_gather(kept, "blk", axis=1, axis_index_groups=row_groups, tiled=True)

    attended_got, memory = lax.optimization_barrier((attended_got, memory))
    attended_low, middle, normed_mid, cross_q = middle_part(
        attended_got, triplane.reshape(rows, width), self_out, gain_mid, bias_mid, cross_query
    )
    cross_q = cross_q.reshape(items, own, width)
    crossed, cross_lse, later, normed_last = cross_forward(
        patch_count, cross_q, memory, middle, cross_out, gain_last, bias_last
    )
    hidden, d_pre, last_pieces, hidden_pieces, d_later, d_later_low, d_crossed, sums_last = mlp(
        devices, normed_last, d_hidden, up_weight, later, grad_out, gain_last, cross_out
    )
    pre_far = xor_blk(d_pre, 2, count_blk)
    pre_near = xor_blk(d_pre, 1, count_blk)
    last_pieces = exchange_y(last_pieces)
    hidden_pieces = exchange_x(hidden_pieces)

    d_cross_q = cross_backward(
        patch_count, cross_q, memory, d_crossed.reshape(items, own, width), cross_lse
    )
    d_cross_low = d_cross_q.reshape(rows, width)
    d_middle, d_middle_low, back_heads, sums_mid = middle_back(
        own,
        d_cross_low,
        cross_query,
        middle,
        gain_mid,
        d_later,
        self_out,
        cross_q.reshape(rows, width),
        d_crossed,
    )
    pre_quad = [d_pre, pre_near, pre_far, xor_blk(pre_far, 1, count_blk)]
    back_heads = to_heads(back_heads)

    up_keep, up_send = product(
        batch_at, quads, [p[None] for p in last_pieces], [p[None] for p in pre_quad]
    )
    down_keep, down_send = product(
        bit_y, quads, [p[None] for p in hidden_pieces], [p[None] for p in grad_quad]
    )
    up_given = swap_batch(up_send)
    down_given = xor_blk(down_send, 2, count_blk)
    lefts, rights = after(
        (
            (crossed.reshape(rows, width), normed_mid, attended_low),
            (d_later_low, d_cross_low, d_middle_low),
        ),
        d_middle_low,
    )
    squares = exchange_x(pieces(devices, *lefts))
    rights = jnp.stack(rights)
    rights_far = swap_batch(rights)
    rights_near = xor_blk(rights, 1, count_blk)

    head = head_at.reshape(1).astype(jnp.int32)
    d_mem = memory_back(head, patch_count, back_heads, memory, own_patches, spare == 1)
    if spare == 1:
        d_heads = self_backward(triplane_count, qkv, kv, kv_first, back_heads, self_lse, d_mem)
    else:
        d_q, d_kv = self_backward(
            triplane_count, qkv, kv, kv_first, back_heads, self_lse, None
        )
        d_kv, d_mem = [
            lax.psum_scatter(
                values, "blk", scatter_dimension=0, axis_index_groups=head_groups, tiled=True
            ).astype(BF)
            for values in (d_kv, d_mem)
        ]
        d_heads = jnp.concatenate(
            [values.reshape(HEADS, -1, LANES) for values in (d_q, d_kv, d_mem)], axis=1
        )
    d_got = to_heads(d_heads)

    mod_rows = width // devices
    ends = jnp.concatenate([sums_mid, sums_last], axis=0)
    ends = jnp.transpose(ends.reshape(4, devices, -1), (1, 0, 2)).reshape(devices, 1, -1)
    packed = mod_rows % 32 == 0 and ends.shape[2] == LANES and spare == 1
    if packed:
        high = ends.astype(BF)
        low = (ends - high.astype(F32)).astype(BF)
        ends = jnp.concatenate([high, low, jnp.zeros((devices, 14, LANES), BF)], axis=1)
    part_patches = HEADS * own_patches
    first_patch = lax.div(blk_at, HEADS) * part_patches
    payload = head_back(
        head,
        d_heads,
        own,
        rows_all,
        lax.dynamic_slice_in_dim(patches_all, first_patch, part_patches, 1)
        if spare > 1
        else patches_all,
        qkv_weight,
        modulation,
        ends if packed else None,
    )
    later = after(later, payload)

    squares_quad = [rights, rights_near, rights_far, xor_blk(rights_far, 1, count_blk)]
    squares_keep, squares_send = product(bit_y, quads, squares, squares_quad)
    squares_given = xor_blk(squares_send, 2, count_blk)

    d_memory_rows = d_got[:, 3 * own :].reshape(HEADS, 2, own_patches, items, HEAD_DIM)
    d_memory_rows = jnp.transpose(d_memory_rows, (3, 2, 1, 0, 4)).reshape(-1, 2 * width)
    d_patches = mm_nt(d_memory_rows, cross_memory)

    def spread(values):
        span = values.shape[0] // devices
        return lax.all_to_all(
            values.reshape(devices, span, values.shape[1]), BOTH, 0, 0, tiled=True
        )

    if packed:
        own_part, terms = payload
        own_part = own_part.reshape((2, HEADS) + own_part.shape[1:])
        own_part = half_x(own_part)
        terms = jnp.broadcast_to(terms, (HEADS,) + terms.shape)
        got = to_heads(jnp.concatenate([own_part, terms], axis=1))
        g_cross_mem, g_qkv, d_modulation, ends = unpack(got, mod_rows, 16)
        ends = (ends[0] + ends[1]).reshape(4, -1)
        others = swap_batch(d_modulation)
        d_modulation = jnp.where(
            batch_at == 0,
            jnp.concatenate([d_modulation, others], axis=0),
            jnp.concatenate([others, d_modulation], axis=0),
        )
    else:
        qkv_product, memory_product, terms = payload
        g_qkv = by_heads(spread(qkv_product).reshape(2 * spare, HEADS, mod_rows, 3 * HEAD_DIM))
        terms = terms.reshape(1, -1, ends.shape[2])
        terms = jnp.broadcast_to(terms, (devices,) + terms.shape[1:])
        small = lax.all_to_all(jnp.concatenate([terms, ends], axis=1), BOTH, 0, 0, tiled=True)
        ends = jnp.sum(small[:, -1], axis=0).reshape(4, -1)
        d_modulation = jnp.sum(small[:, :-1].reshape(2, count_blk, -1), axis=1)
        memory_got = spread(memory_product).astype(F32)
        memory_got = memory_got.reshape(2 * spare, HEADS, mod_rows, 2, HEAD_DIM)
        memory_got = jnp.transpose(jnp.sum(memory_got, axis=0), (1, 2, 0, 3))
        g_cross_mem = memory_got.reshape(mod_rows, 2 * width)
    d_modulation = d_modulation.reshape(2 * items, 2 * width)
    own_cams = lax.optimization_barrier((camera_index, modulation))[0]
    others = swap_batch(own_cams)
    cams = jnp.where(
        batch_at == 0,
        jnp.concatenate([own_cams, others], axis=0),
        jnp.concatenate([others, own_cams], axis=0),
    )
    pick = pick_of(cams)
    code_low = code_of(pick)
    code_rows = lax.dynamic_slice_in_dim(code_low, place * mod_rows, mod_rows, 1).astype(F32)
    g_mod = jnp.sum(code_rows[:, :, None] * d_modulation[:, None, :], axis=0)
    d_code = mm_nt(d_modulation.astype(BF), mod_weight)
    cam_rows = camera_table.shape[0] // devices
    pick_rows = lax.dynamic_slice_in_dim(pick, place * cam_rows, cam_rows, 1)
    g_table = jnp.sum(pick_rows[:, :, None] * d_code[:, None, :], axis=0) / views

    d_triplane = first_back(
        d_got, qkv_weight, triplane, modulation, d_middle.reshape(items, own, width)
    )
    g_up = rest_sum(up_keep, up_given)[0]
    g_down = rest_sum(down_keep, down_given)[0]
    g_squares = rest_sum(squares_keep, squares_given)
    result = later + mm(hidden, down_weight)
    return (
        result.reshape(items, own, width),
        d_triplane,
        d_patches.reshape(items, own_patches, width),
        g_table,
        g_mod,
        g_qkv,
        g_squares[2],
        ends[0],
        ends[1],
        g_squares[1],
        g_cross_mem,
        g_squares[0],
        ends[2],
        ends[3],
        g_up,
        g_down,
    )


def solution(mesh):
    rows = P("batch", "blk", None)
    split = P(BOTH, None)
    line = P(BOTH)
    whole = P()
    return jax.shard_map(
        functools.partial(local, mesh.shape["blk"]),
        mesh=mesh,
        in_specs=(rows, rows, rows, P("batch", None), P("batch"), P("batch")) + (whole,) * 13,
        out_specs=(
            rows,
            rows,
            rows,
            split,
            split,
            split,
            split,
            line,
            line,
            split,
            split,
            split,
            line,
            line,
            split,
            split,
        ),
        check_vma=False,
    )
```
